32 devices in a mesh: rep: 4 (over y, x), fsdp: 8 (over z, core).
Axes of the slice: x: 2, y: 2, z: 4, core: 2. Of those that a mesh axis runs over, the one named last changes fastest.
Arguments:
- tokens_in: bfloat16 [8192, 768], P(('rep', 'fsdp')), may hold values from -6 to 6
- masked_flags: int32 [8192], P(('rep', 'fsdp')), may hold values 0 or 1
- mask_embedding: bfloat16 [768], replicated, may hold values from -6 to 6
- out_cotangent: bfloat16 [8192, 768], P(('rep', 'fsdp')), may hold values from -6 to 6
- w_qkv: float32 [2, 768, 2304], P(None, 'fsdp'), may hold values from -0.21875 to 0.21875
- m_qkv: float32 [2, 768, 2304], P(None, 'fsdp'), may hold values from -0.00011507027 to 0.00011507027
- v_qkv: float32 [2, 768, 2304], P(None, 'fsdp'), may hold values from 5.2964664e-11 to 2.1185866e-10
- w_out: float32 [2, 768, 768], P(None, 'fsdp'), may hold values from -0.4375 to 0.4375
- m_out: float32 [2, 768, 768], P(None, 'fsdp'), may hold values from -0.00011507027 to 0.00011507027
- v_out: float32 [2, 768, 768], P(None, 'fsdp'), may hold values from 5.2964664e-11 to 2.1185866e-10
- w_gu: float32 [2, 768, 6144], P(None, 'fsdp'), may hold values from -0.21875 to 0.21875
- m_gu: float32 [2, 768, 6144], P(None, 'fsdp'), may hold values from -0.00011507027 to 0.00011507027
- v_gu: float32 [2, 768, 6144], P(None, 'fsdp'), may hold values from 5.2964664e-11 to 2.1185866e-10
- w_down: float32 [2, 3072, 768], P(None, 'fsdp'), may hold values from -0.109375 to 0.109375
- m_down: float32 [2, 3072, 768], P(None, 'fsdp'), may hold values from -0.00011507027 to 0.00011507027
- v_down: float32 [2, 3072, 768], P(None, 'fsdp'), may hold values from 5.2964664e-11 to 2.1185866e-10
- norm_params: float32 [2, 4, 768], P(None, None, 'fsdp'), may hold values from -1 to 2
- m_norms: float32 [2, 4, 768], P(None, None, 'fsdp'), may hold values from -0.00046028107 to 0.00046028107
- v_norms: float32 [2, 4, 768], P(None, None, 'fsdp'), may hold values from 8.474346e-10 to 3.3897385e-09
Outputs:
- activations: bfloat16 [8192, 768], P(('rep', 'fsdp'))
- input_grad: float32 [8192, 768], P(('rep', 'fsdp'))
- grad_norm: float32 [], replicated
- new_w_qkv: float32 [2, 768, 2304], P(None, 'fsdp')
- new_m_qkv: float32 [2, 768, 2304], P(None, 'fsdp')
- new_v_qkv: float32 [2, 768, 2304], P(None, 'fsdp')
- new_w_out: float32 [2, 768, 768], P(None, 'fsdp')
- new_m_out: float32 [2, 768, 768], P(None, 'fsdp')
- new_v_out: float32 [2, 768, 768], P(None, 'fsdp')
- new_w_gu: float32 [2, 768, 6144], P(None, 'fsdp')
- new_m_gu: float32 [2, 768, 6144], P(None, 'fsdp')
- new_v_gu: float32 [2, 768, 6144], P(None, 'fsdp')
- new_w_down: float32 [2, 3072, 768], P(None, 'fsdp')
- new_m_down: float32 [2, 3072, 768], P(None, 'fsdp')
- new_v_down: float32 [2, 3072, 768], P(None, 'fsdp')
- new_norms: float32 [2, 4, 768], P(None, None, 'fsdp')
- new_m_norms: float32 [2, 4, 768], P(None, None, 'fsdp')
- new_v_norms: float32 [2, 4, 768], P(None, None, 'fsdp')
The draws below stay inside these ranges and needn't reach their ends.
All inputs are finite; a program needn't handle non-finite values. No bound on the sum of `masked_flags` on one device may be relied on, other than what follows from the above.
Results may differ from the reference program's by a relative error of at most 0.025.
Values may be sent and summed in bfloat16 or wider, within the bound.
No kernel may reach another device: no remote copies, remote signals or barrier semaphores. Data moves between devices by JAX's collectives and lax.ppermute only.
A program may use at most 256 MiB of HBM per device.

```python
import math
import jax
import jax.numpy as jnp
from jax import lax

D = 768
HEADS = 12
HEAD_DIM = 64
FF = 3072
LAYERS = 2
SEQ_LEN = 128
STEP = 10
SEQS = 64
TOKENS = 8192
NPARAM = 18880512


def draw_tokens_in(key, part):
    key = jax.random.fold_in(key, 11)
    column = jnp.arange(D).astype(jnp.float32) / max(D - 1, 1)
    profile = 0.5 + column
    base = jnp.clip(jax.random.normal(key, (TOKENS, D), jnp.float32), -4.0, 4.0)
    return (base * profile[None, :]).astype(jnp.bfloat16)


def draw_norm_params(key, part):
    key = jax.random.fold_in(key, 12)
    key_gain, key_shift = jax.random.split(key)
    column = jnp.arange(D).astype(jnp.float32) / max(D - 1, 1)
    profile = 0.5 + column
    noise = jnp.clip(0.1 * jax.random.normal(key_gain, (LAYERS, 4, D), jnp.float32), -0.25, 0.25)
    shifts = jnp.clip(0.3 * jax.random.normal(key_shift, (LAYERS, 4, D), jnp.float32), -0.9, 0.9)
    gains = profile[None, None, :] * (1.0 + noise)
    gain_rows = (jnp.arange(4) % 2 == 0)[None, :, None]
    return jnp.where(gain_rows, gains, shifts).astype(jnp.float32)


def with_ends(values, rng, smallest, high):
    index_at = [jax.random.randint(jax.random.fold_in(rng, axis), (), 0, length) for axis, length in enumerate(values.shape)]
    main_axis = values.shape.index(max(values.shape))
    next_to = index_at[:main_axis] + [(index_at[main_axis] + 1) % values.shape[main_axis]] + index_at[main_axis + 1:]
    return values.at[tuple(index_at)].set(smallest).at[tuple(next_to)].set(high)


def levels(key, extent, cuts, least, top_value):
    def one(axis_at, shards_of):
        heights = jax.random.uniform(jax.random.fold_in(jax.random.fold_in(key, 6), axis_at), (shards_of,), jnp.float32, least / len(cuts), top_value / len(cuts))
        return jnp.repeat(jnp.exp(heights), extent[axis_at] // shards_of).reshape((-1,) + (1,) * (len(extent) - axis_at - 1))

    level = one(*cuts[0])
    for cut in cuts[1:]:
        level = level * one(*cut)
    return level


def bell_draw(key, dims, width, bound, cuts=(), kind=jnp.bfloat16):
    level = levels(key, dims, cuts, -0.22, 0.18) if cuts else 1.0
    values = jax.random.normal(key, dims, jnp.float32) * width * level
    return jnp.minimum(jnp.maximum(values, -bound), bound).astype(kind)


def setup_inputs(seed: int = 0) -> dict:
    splits = jax.random.split(jax.random.key(seed), 20)
    return {
        "tokens_in": draw_tokens_in(jax.random.fold_in(splits[19], 71), 0),
        "masked_flags": with_ends((jax.random.randint(splits[1], (TOKENS,), 0, 100) < 15).astype(jnp.int32), jax.random.fold_in(splits[1], 1), 0, 1),
        "mask_embedding": bell_draw(splits[2], (D,), 1.0, 6.0),
        "out_cotangent": bell_draw(splits[3], (TOKENS, D), 1.0, 6.0, ((0, 32),)),
        "w_qkv": bell_draw(splits[4], (LAYERS, D, 3 * D), D ** -0.5, 0.21875, ((1, 8),), jnp.float32),
        "m_qkv": bell_draw(splits[5], (LAYERS, D, 3 * D), (0.11 * NPARAM ** -0.5), 0.00011507027, ((1, 8),), jnp.float32),
        "v_qkv": jnp.clip(jnp.exp(math.log(2.118586556187907e-10) - 1.3862944 * jax.random.uniform(splits[6], (LAYERS, D, 3 * D), jnp.float32) ** levels(splits[6], (LAYERS, D, 3 * D), ((1, 8),), -0.2, 0.2)), 5.296466390469767e-11, 2.118586556187907e-10),
        "w_out": bell_draw(splits[7], (LAYERS, D, D), (D // 4) ** -0.5, 0.4375, ((1, 8),), jnp.float32),
        "m_out": bell_draw(splits[8], (LAYERS, D, D), (0.11 * NPARAM ** -0.5), 0.00011507027, ((1, 8),), jnp.float32),
        "v_out": jnp.clip(jnp.exp(math.log(2.118586556187907e-10) - 1.3862944 * jax.random.uniform(splits[9], (LAYERS, D, D), jnp.float32) ** levels(splits[9], (LAYERS, D, D), ((1, 8),), -0.2, 0.2)), 5.296466390469767e-11, 2.118586556187907e-10),
        "w_gu": bell_draw(splits[10], (LAYERS, D, 2 * FF), D ** -0.5, 0.21875, ((1, 8),), jnp.float32),
        "m_gu": bell_draw(splits[11], (LAYERS, D, 2 * FF), (0.11 * NPARAM ** -0.5), 0.00011507027, ((1, 8),), jnp.float32),
        "v_gu": jnp.clip(jnp.exp(math.log(2.118586556187907e-10) - 1.3862944 * jax.random.uniform(splits[12], (LAYERS, D, 2 * FF), jnp.float32) ** levels(splits[12], (LAYERS, D, 2 * FF), ((1, 8),), -0.2, 0.2)), 5.296466390469767e-11, 2.118586556187907e-10),
        "w_down": bell_draw(splits[13], (LAYERS, FF, D), FF ** -0.5, 0.109375, ((1, 8),), jnp.float32),
        "m_down": bell_draw(splits[14], (LAYERS, FF, D), (0.11 * NPARAM ** -0.5), 0.00011507027, ((1, 8),), jnp.float32),
        "v_down": jnp.clip(jnp.exp(math.log(2.118586556187907e-10) - 1.3862944 * jax.random.uniform(splits[15], (LAYERS, FF, D), jnp.float32) ** levels(splits[15], (LAYERS, FF, D), ((1, 8),), -0.2, 0.2)), 5.296466390469767e-11, 2.118586556187907e-10),
        "norm_params": draw_norm_params(jax.random.fold_in(splits[19], 71), 0),
        "m_norms": bell_draw(splits[17], (LAYERS, 4, D), (0.44 * NPARAM ** -0.5), 0.00046028107, ((2, 8),), jnp.float32),
        "v_norms": jnp.clip(jnp.exp(math.log(3.389738489900651e-09) - 1.3862944 * jax.random.uniform(splits[18], (LAYERS, 4, D), jnp.float32) ** levels(splits[18], (LAYERS, 4, D), ((2, 8),), -0.2, 0.2)), 8.474346224751628e-10, 3.389738489900651e-09),
    }


beta_first = 0.9
beta_second = 0.999
adam_eps = 1e-08
clip_norm = 1.0
rate_matrix = 0.03
rate_norm = 0.5
decay_matrix = 0.01
norm_eps = 1e-05
highest_precision = lax.Precision.HIGHEST

@jax.custom_vjp
def low(v):
    return lax.optimization_barrier(v.astype(jnp.bfloat16)).astype(jnp.float32)

@jax.custom_vjp
def low_back(v):
    return v

def low_keep(v):
    return (low(v), None)

def low_pass(kept, grad):
    return (grad,)

def back_keep(v):
    return (v, None)

def back_low(kept, grad):
    return (low(grad),)
low.defvjp(low_keep, low_pass)
low_back.defvjp(back_keep, back_low)

def both_ways(value):
    return low(low_back(value))

def alibi_bias(length, head_count):
    slopes = 2.0 ** (-8.0 * (jnp.arange(head_count).astype(jnp.float32) + 1.0) / head_count)
    places = jnp.arange(length).astype(jnp.float32)
    distance = jnp.abs(places[:, None] - places[None, :])
    return -slopes[:, None, None] * distance[None, :, :]

def layer_norm(values_in, norm_gain, norm_shift):
    center = values_in - lax.optimization_barrier(jnp.mean(values_in, axis=-1, keepdims=True))
    spread = lax.optimization_barrier(jnp.mean(center * center, axis=-1, keepdims=True))
    return center * lax.rsqrt(spread + norm_eps) * norm_gain + norm_shift

def encoder_layer(hidden, weight_qkv, weight_out, weight_gu, weight_down, norm_set):
    weight_qkv = low(weight_qkv)
    weight_out = low(weight_out)
    weight_gu = low(weight_gu)
    weight_down = low(weight_down)
    norm_set = low(norm_set)
    seq_count = hidden.shape[0] // SEQ_LEN
    inputs_low = low(hidden)
    qkv_value = both_ways(jnp.dot(inputs_low, weight_qkv, precision=highest_precision))
    sections = qkv_value.reshape(seq_count, SEQ_LEN, 3, HEADS, HEAD_DIM)
    query_rows = sections[:, :, 0]
    key_rows = sections[:, :, 1]
    value_rows = sections[:, :, 2]
    raw_scores = jnp.einsum('sqhd,skhd->shqk', query_rows, key_rows, precision=highest_precision) * HEAD_DIM ** (-0.5) + alibi_bias(SEQ_LEN, HEADS)[None]
    scores = low_back(raw_scores)
    attention = jax.nn.softmax(scores, axis=-1)
    mixture = jnp.einsum('shqk,skhd->sqhd', low(attention), value_rows, precision=highest_precision)
    mixture = both_ways(mixture.reshape(hidden.shape[0], D))
    attended = low_back(jnp.dot(mixture, weight_out, precision=highest_precision))
    normed_one = layer_norm(hidden + attended, norm_set[0], norm_set[1])
    gate_up = low_back(jnp.dot(low(normed_one), weight_gu, precision=highest_precision))
    product = both_ways(jax.nn.gelu(gate_up[:, :FF], approximate=False) * gate_up[:, FF:])
    branch_out = low_back(jnp.dot(product, weight_down, precision=highest_precision))
    return layer_norm(normed_one + branch_out, norm_set[2], norm_set[3])

def forward_group(inputs_float, params, flags_group, embed_row):
    hidden = jnp.where(flags_group[:, None] == 1, embed_row[None, :], inputs_float)
    for layer_index in range(LAYERS):
        hidden = encoder_layer(hidden, params[0][layer_index], params[1][layer_index], params[2][layer_index], params[3][layer_index], params[4][layer_index])
    return hidden

def adam_step(weight, first_moment, second_moment, gradient, factor, step_rate, decay_rate):
    gradient = gradient * factor
    first_moment = beta_first * first_moment + (1.0 - beta_first) * gradient
    second_moment = beta_second * second_moment + (1.0 - beta_second) * gradient * gradient
    first_hat = first_moment / (1.0 - beta_first ** STEP)
    second_hat = second_moment / (1.0 - beta_second ** STEP)
    weight = weight - step_rate * (first_hat / (jnp.sqrt(second_hat) + adam_eps) + decay_rate * weight)
    return (weight, first_moment, second_moment)

def reference(tokens_in, masked_flags, mask_embedding, out_cotangent, w_qkv, m_qkv, v_qkv, w_out, m_out, v_out, w_gu, m_gu, v_gu, w_down, m_down, v_down, norm_params, m_norms, v_norms):
    per_group = math.gcd(SEQS, 4096 // SEQ_LEN)
    groups = SEQS // per_group
    group_rows = per_group * SEQ_LEN
    params = (w_qkv, w_out, w_gu, w_down, norm_params)
    embed_row = mask_embedding.astype(jnp.float32)
    inputs_all = (tokens_in.astype(jnp.float32).reshape(groups, group_rows, D), masked_flags.reshape(groups, group_rows), out_cotangent.astype(jnp.float32).reshape(groups, group_rows, D))

    def one_group(totals, pieces):
        inputs_group, flags_group, cotangent_group = pieces

        def forward_fn(inputs_value, param_value):
            return forward_group(inputs_value, param_value, flags_group, embed_row)
        outputs, pull_back = jax.vjp(forward_fn, inputs_group, params)
        input_part, param_part = pull_back(cotangent_group * flags_group[:, None].astype(jnp.float32))
        totals = jax.tree.map(lambda left_sum, right_sum: left_sum + right_sum, totals, param_part)
        return (totals, (outputs.astype(jnp.bfloat16), input_part))
    zero_grads = jax.tree.map(jnp.zeros_like, params)
    gradients, (act_groups, input_groups) = lax.scan(one_group, zero_grads, inputs_all)
    squares = jnp.float32(0.0)
    for piece_grad in gradients:
        squares = squares + jnp.sum(piece_grad * piece_grad)
    grad_norm = jnp.sqrt(squares)
    factor = clip_norm / jnp.maximum(grad_norm, clip_norm)
    new_qkv = adam_step(w_qkv, m_qkv, v_qkv, gradients[0], factor, rate_matrix, decay_matrix)
    new_out = adam_step(w_out, m_out, v_out, gradients[1], factor, rate_matrix, decay_matrix)
    new_gu = adam_step(w_gu, m_gu, v_gu, gradients[2], factor, rate_matrix, decay_matrix)
    new_down = adam_step(w_down, m_down, v_down, gradients[3], factor, rate_matrix, decay_matrix)
    new_norm = adam_step(norm_params, m_norms, v_norms, gradients[4], factor, rate_norm, 0.0)
    activations = act_groups.reshape(TOKENS, D)
    input_grad = input_groups.reshape(TOKENS, D)
    return (activations, input_grad, grad_norm, new_qkv[0], new_qkv[1], new_qkv[2], new_out[0], new_out[1], new_out[2], new_gu[0], new_gu[1], new_gu[2], new_down[0], new_down[1], new_down[2], new_norm[0], new_norm[1], new_norm[2])
```

```python
import jax
import jax.numpy as jnp
from jax import lax
from jax.experimental import pallas as pl
from jax.experimental.pallas import tpu as pltpu
from jax.sharding import PartitionSpec as P

D = 768
HEADS = 12
HEAD_DIM = 64
FF = 3072
SEQ_LEN = 128
STEP = 10


beta_first = 0.9
beta_second = 0.999
adam_eps = 1e-08
clip_norm = 1.0
rate_matrix = 0.03
rate_norm = 0.5
decay_matrix = 0.01
norm_eps = 1e-05


def alibi_bias(length, head_count):
    slopes = 2.0 ** (-8.0 * (jnp.arange(head_count).astype(jnp.float32) + 1.0) / head_count)
    places = jnp.arange(length).astype(jnp.float32)
    distance = jnp.abs(places[:, None] - places[None, :])
    return -slopes[:, None, None] * distance[None, :, :]


def layer_norm(values_in, norm_gain, norm_shift):
    center = values_in - jnp.mean(values_in, axis=-1, keepdims=True)
    spread = jnp.mean(center * center, axis=-1, keepdims=True)
    return center * lax.rsqrt(spread + norm_eps) * norm_gain + norm_shift


def gelu_gate(gate_part, up_part):
    return jax.nn.gelu(gate_part, approximate=False) * up_part


def outer_sum(left_rows, right_rows):
    return lax.dot_general(
        left_rows, right_rows, (((0,), (0,)), ((), ())), preferred_element_type=jnp.float32
    )


def back_product(gradient, weight):
    return lax.dot_general(
        gradient, weight, (((1,), (1,)), ((), ())), preferred_element_type=jnp.float32
    )


def split_heads(qkv_low):
    sections = qkv_low.reshape(-1, SEQ_LEN, 3, HEADS, HEAD_DIM)
    return (sections[:, :, 0], sections[:, :, 1], sections[:, :, 2])


def score_block(query_rows, key_rows):
    raw_scores = jnp.einsum(
        "sqhd,skhd->shqk", query_rows, key_rows, preferred_element_type=jnp.float32
    )
    return raw_scores * HEAD_DIM ** (-0.5) + alibi_bias(SEQ_LEN, HEADS)[None]


def forward_layer(hidden, weights):
    weight_qkv, weight_out, weight_gu, weight_down, norm_low = weights
    norm_set = norm_low.astype(jnp.float32)
    inputs_low = hidden.astype(jnp.bfloat16)
    qkv_low = jnp.dot(inputs_low, weight_qkv, preferred_element_type=jnp.float32).astype(
        jnp.bfloat16
    )
    query_rows, key_rows, value_rows = split_heads(qkv_low)
    scores = score_block(query_rows, key_rows)
    summit = jnp.max(scores, axis=-1, keepdims=True)
    log_total = summit + jnp.log(jnp.sum(jnp.exp(scores - summit), axis=-1, keepdims=True))
    attention = jnp.exp(scores - log_total)
    mixture = jnp.einsum(
        "shqk,skhd->sqhd",
        attention.astype(jnp.bfloat16),
        value_rows,
        preferred_element_type=jnp.float32,
    )
    mixture_low = mixture.reshape(hidden.shape[0], D).astype(jnp.bfloat16)
    residual_one = hidden + jnp.dot(mixture_low, weight_out, preferred_element_type=jnp.float32)
    normed_one = layer_norm(residual_one, norm_set[0], norm_set[1])
    normed_low = normed_one.astype(jnp.bfloat16)
    gate_up = jnp.dot(normed_low, weight_gu, preferred_element_type=jnp.float32)
    product_low = gelu_gate(gate_up[:, :FF], gate_up[:, FF:]).astype(jnp.bfloat16)
    residual_two = normed_one + jnp.dot(
        product_low, weight_down, preferred_element_type=jnp.float32
    )
    result = layer_norm(residual_two, norm_set[2], norm_set[3])
    kept_state = (
        inputs_low,
        qkv_low,
        log_total,
        mixture_low,
        residual_one,
        normed_low,
        gate_up,
        product_low,
        residual_two,
    )
    return (result, kept_state)


def backward_layer(grad_result, weights, kept_state):
    weight_qkv, weight_out, weight_gu, weight_down, norm_low = weights
    norm_set = norm_low.astype(jnp.float32)
    (
        inputs_low,
        qkv_low,
        log_total,
        mixture_low,
        residual_one,
        normed_low,
        gate_up,
        product_low,
        residual_two,
    ) = kept_state
    _, pull_two = jax.vjp(layer_norm, residual_two, norm_set[2], norm_set[3])
    grad_two, gain_two, shift_two = pull_two(grad_result)
    branch_low = grad_two.astype(jnp.bfloat16)
    grad_down = outer_sum(product_low, branch_low)
    product_grad = back_product(branch_low, weight_down).astype(jnp.bfloat16).astype(jnp.float32)
    _, pull_gate = jax.vjp(gelu_gate, gate_up[:, :FF], gate_up[:, FF:])
    grad_gate, grad_up = pull_gate(product_grad)
    gate_up_low = jnp.concatenate([grad_gate, grad_up], axis=1).astype(jnp.bfloat16)
    grad_gu = outer_sum(normed_low, gate_up_low)
    grad_normed = grad_two + back_product(gate_up_low, weight_gu)
    _, pull_one = jax.vjp(layer_norm, residual_one, norm_set[0], norm_set[1])
    grad_one, gain_one, shift_one = pull_one(grad_normed)
    attend_low = grad_one.astype(jnp.bfloat16)
    grad_out_weight = outer_sum(mixture_low, attend_low)
    mixture_grad = (
        back_product(attend_low, weight_out)
        .astype(jnp.bfloat16)
        .reshape(-1, SEQ_LEN, HEADS, HEAD_DIM)
    )
    query_rows, key_rows, value_rows = split_heads(qkv_low)
    attention = jnp.exp(score_block(query_rows, key_rows) - log_total)
    attention_grad = jnp.einsum(
        "sqhd,skhd->shqk", mixture_grad, value_rows, preferred_element_type=jnp.float32
    )
    value_grad = jnp.einsum(
        "shqk,sqhd->skhd",
        attention.astype(jnp.bfloat16),
        mixture_grad,
        preferred_element_type=jnp.float32,
    )
    score_grad = attention * (
        attention_grad - jnp.sum(attention * attention_grad, axis=-1, keepdims=True)
    )
    score_low = score_grad.astype(jnp.bfloat16)
    query_grad = jnp.einsum(
        "shqk,skhd->sqhd", score_low, key_rows, preferred_element_type=jnp.float32
    ) * HEAD_DIM ** (-0.5)
    key_grad = jnp.einsum(
        "shqk,sqhd->skhd", score_low, query_rows, preferred_element_type=jnp.float32
    ) * HEAD_DIM ** (-0.5)
    qkv_grad = (
        jnp.stack([query_grad, key_grad, value_grad], axis=2)
        .reshape(inputs_low.shape[0], 3 * D)
        .astype(jnp.bfloat16)
    )
    grad_qkv = outer_sum(inputs_low, qkv_grad)
    grad_input = grad_one + back_product(qkv_grad, weight_qkv)
    grad_norms = jnp.stack([gain_one, shift_one, gain_two, shift_two])
    return (grad_input, (grad_qkv, grad_out_weight, grad_gu, grad_down, grad_norms))


def adam_step(weight, first_moment, second_moment, gradient, factor, step_rate, decay_rate):
    gradient = gradient * factor
    first_moment = beta_first * first_moment + (1.0 - beta_first) * gradient
    second_moment = beta_second * second_moment + (1.0 - beta_second) * gradient * gradient
    first_hat = first_moment / (1.0 - beta_first**STEP)
    second_hat = second_moment / (1.0 - beta_second**STEP)
    weight = weight - step_rate * (
        first_hat / (jnp.sqrt(second_hat) + adam_eps) + decay_rate * weight
    )
    return (weight, first_moment, second_moment)


both_axes = ("rep", "fsdp")


def pairs_of(move):
    found = []
    for rep in range(4):
        for shard in range(8):
            target = move(rep // 2, rep % 2, shard // 2, shard % 2)
            if target is not None:
                to_y, to_x, to_z, to_c = target
                found.append((rep * 8 + shard, (to_y * 2 + to_x) * 8 + to_z * 2 + to_c))
    return found


FLIP_CORE = pairs_of(lambda y, x, z, c: (y, x, z, 1 - c))
FLIP_X = pairs_of(lambda y, x, z, c: (y, 1 - x, z, c))
FLIP_Y = pairs_of(lambda y, x, z, c: (1 - y, x, z, c))
FLIP_FIRST = pairs_of(lambda y, x, z, c: (y, 1 - x, z, c) if c == 0 else (1 - y, x, z, c))
FLIP_SECOND = pairs_of(lambda y, x, z, c: (1 - y, x, z, c) if c == 0 else (y, 1 - x, z, c))
Z_MATE = pairs_of(lambda y, x, z, c: (y, x, z ^ 1, c))
Z_CROSS = pairs_of(lambda y, x, z, c: (y, x, 3 - z, c))
Z_MIDDLE = pairs_of(lambda y, x, z, c: (y, x, 3 - z, c) if z in (1, 2) else None)
Z_OUTWARD = pairs_of(lambda y, x, z, c: (y, x, z ^ 1, c) if z in (1, 2) else None)
Z_INWARD = pairs_of(lambda y, x, z, c: (y, x, z ^ 1, c) if z in (0, 3) else None)


def send(values, pairs):
    return lax.ppermute(values, both_axes, pairs)


def place():
    rep = lax.axis_index("rep")
    shard = lax.axis_index("fsdp")
    y, x, z, c = rep // 2, rep % 2, shard // 2, shard % 2
    first = jnp.where(c == 0, x, y)
    second = jnp.where(c == 0, y, x)
    return (z, c, first, second)


def pick(values, index, axis):
    return lax.dynamic_index_in_dim(values, index, axis, keepdims=False)


def in_order(mine, other, bit):
    return lax.dynamic_slice_in_dim(jnp.stack([mine, other, mine]), bit, 2, 0)


def gather_chunk(own):
    z, c, first, second = place()
    quarter = pick(own, 2 * first + second, 0)
    mate = send(quarter, Z_MATE)
    pair = in_order(quarter, mate, z % 2)
    got_middle = send(pair, Z_MIDDLE)
    got_outward = send(got_middle, Z_OUTWARD)
    inner = (z == 1) | (z == 2)
    other = jnp.where(inner, got_middle, got_outward)
    three = jnp.concatenate([mate[None], other])
    six = jnp.stack([three, send(three, FLIP_SECOND)])
    far = send(six, FLIP_FIRST)
    return (own, six, far, send(own, FLIP_CORE), send(six, FLIP_CORE), send(far, FLIP_CORE))


def assemble(pieces, kind):
    count = pieces[0].shape[1]
    rows = pieces[0].shape[2]
    shapes = {
        "attend": ((8 * rows, 3 * D), (8 * rows, D)),
        "gate_up": ((8 * rows, 2 * FF),),
        "down": ((8 * 4 * rows, D),),
    }[kind]

    def kernel(*refs):
        in_refs, out_refs, sem = refs[:6], refs[6:-1], refs[-1]
        z, c, first, second = place()
        low = jnp.where(z < 2, 2, 0)
        others = (z ^ 1, low, low + 1)

        def copy(source, quarter, block, shard):
            row = pl.multiple_of(shard * rows, rows)
            if kind == "attend":

                @pl.when(quarter < 3)
                def _():
                    column = pl.multiple_of(quarter * D, D)
                    target = out_refs[0].at[pl.ds(row, rows), pl.ds(column, D)]
                    pltpu.make_async_copy(source, target, sem).start()

                @pl.when(quarter == 3)
                def _():
                    target = out_refs[1].at[pl.ds(row, rows), :]
                    pltpu.make_async_copy(source, target, sem).start()

            elif kind == "gate_up":
                column = pl.multiple_of((quarter + 4 * block) * D, D)
                target = out_refs[0].at[pl.ds(row, rows), pl.ds(column, D)]
                pltpu.make_async_copy(source, target, sem).start()
            else:
                row = pl.multiple_of((shard * 4 + quarter) * rows, rows)
                target = out_refs[0].at[pl.ds(row, rows), :]
                pltpu.make_async_copy(source, target, sem).start()

        for side in range(2):
            own, six, far = in_refs[3 * side : 3 * side + 3]
            core = c if side == 0 else 1 - c
            high, little = (first, second) if side == 0 else (second, first)
            for block in range(count):
                for quarter in range(4):
                    copy(own.at[quarter, block], jnp.int32(quarter), block, 2 * z + core)
                for turn in range(2):
                    unit = little if turn == 0 else 1 - little
                    for step in range(3):
                        shard = 2 * others[step] + core
                        copy(six.at[turn, step, block], 2 * high + unit, block, shard)
                        copy(far.at[turn, step, block], 2 * (1 - high) + unit, block, shard)
        for out_ref in out_refs:
            pltpu.make_async_copy(out_ref, out_ref, sem).wait()

    return pl.pallas_call(
        kernel,
        out_shape=tuple(jax.ShapeDtypeStruct(shape, jnp.bfloat16) for shape in shapes),
        in_specs=[pl.BlockSpec(memory_space=pl.ANY)] * 6,
        out_specs=tuple(pl.BlockSpec(memory_space=pltpu.VMEM) for _ in shapes),
        scratch_shapes=[pltpu.SemaphoreType.DMA],
        compiler_params=pltpu.CompilerParams(vmem_limit_bytes=24 * 2**20),
        name="assemble_" + kind,
    )(*pieces)


def add_low(left, right):
    return (left.astype(jnp.float32) + right.astype(jnp.float32)).astype(jnp.bfloat16)


def scatter_chunk(parts):
    z, c, first, second = place()
    count, rows = parts.shape[1], parts.shape[3]
    parts = parts.reshape(2, 2, count, 4, 2, rows, D)
    got = send(pick(parts, 1 - c, 4), FLIP_CORE)
    parts = add_low(pick(parts, c, 4), got)
    got = send(pick(parts, 1 - first, 0), FLIP_FIRST)
    parts = add_low(pick(parts, first, 0), got)
    parts = parts.reshape(2, count, 2, 2, rows, D)
    theirs = pick(parts, 1 - z // 2, 2)
    mine = pick(parts, z // 2, 2)
    theirs = add_low(theirs, send(theirs, Z_INWARD))
    mine = add_low(mine, send(theirs, Z_MIDDLE))
    got = send(pick(mine, 1 - z % 2, 2), Z_MATE)
    mine = add_low(pick(mine, z % 2, 2), got)
    got = send(pick(mine, 1 - second, 0), FLIP_SECOND)
    return add_low(pick(mine, second, 0), got)


def spread_chunk(quarter):
    z, c, first, second = place()
    row = in_order(quarter, send(quarter, FLIP_SECOND), second)
    whole = in_order(row, send(row, FLIP_FIRST), first)
    return whole.reshape((4,) + quarter.shape)


def sum_all(value):
    for pairs in (FLIP_CORE, FLIP_X, FLIP_Y, Z_MATE, Z_CROSS):
        value = value + send(value, pairs)
    return value


def by_neighbours():
    return lax.axis_size("rep") == 4 and lax.axis_size("fsdp") == 8


def gather_layer(w_qkv, w_out, w_gu, w_down):
    low = [weight.astype(jnp.bfloat16) for weight in (w_qkv, w_out, w_gu, w_down)]
    if not by_neighbours():
        return tuple(lax.all_gather(weight, "fsdp", axis=0, tiled=True) for weight in low)
    rows = w_qkv.shape[0]
    attend = jnp.stack([low[0][:, :D], low[0][:, D : 2 * D], low[0][:, 2 * D :], low[1]])
    gate_up = low[2].reshape(rows, 2, 4, D).transpose(2, 1, 0, 3)
    down = low[3].reshape(4, 1, rows, D)
    weight_qkv, weight_out = assemble(gather_chunk(attend[:, None]), "attend")
    (weight_gu,) = assemble(gather_chunk(gate_up), "gate_up")
    (weight_down,) = assemble(gather_chunk(down), "down")
    return (weight_qkv, weight_out, weight_gu, weight_down)


def reduce_layer(grad_qkv, grad_out, grad_gu, grad_down):
    if not by_neighbours():
        sums = []
        squares = jnp.float32(0.0)
        for grad in (grad_qkv, grad_out, grad_gu, grad_down):
            part = lax.psum_scatter(grad, "fsdp", scatter_dimension=0, tiled=True)
            part = lax.psum(part, "rep")
            squares = squares + jnp.sum(part * part) / lax.axis_size("rep")
            sums.append(part)
        return (tuple(sums), squares)
    rows = grad_qkv.shape[0] // 8
    grad_qkv, grad_out, grad_gu, grad_down = (
        grad.astype(jnp.bfloat16) for grad in (grad_qkv, grad_out, grad_gu, grad_down)
    )
    attend = jnp.stack(
        [grad_qkv[:, :D], grad_qkv[:, D : 2 * D], grad_qkv[:, 2 * D :], grad_out]
    ).reshape(4, 1, 8, rows, D)
    gate_up = grad_gu.reshape(8, rows, 2, 4, D).transpose(3, 2, 0, 1, 4)
    down = grad_down.reshape(8, 4, rows, D).transpose(1, 0, 2, 3)[:, None]
    squares = jnp.float32(0.0)
    sums = []
    for chunk in (down, gate_up, attend):
        quarter = scatter_chunk(chunk)
        wide = quarter.astype(jnp.float32)
        squares = squares + jnp.sum(wide * wide)
        sums.append(spread_chunk(quarter))
    down, gate_up, attend = sums
    grad_qkv = jnp.concatenate([attend[0, 0], attend[1, 0], attend[2, 0]], axis=1)
    grad_gu = gate_up.transpose(2, 1, 0, 3).reshape(rows, 2 * FF)
    return ((grad_qkv, attend[3, 0], grad_gu, down.reshape(4 * rows, D)), squares)


def body(
    tokens_in,
    masked_flags,
    mask_embedding,
    out_cotangent,
    w_qkv,
    m_qkv,
    v_qkv,
    w_out,
    m_out,
    v_out,
    w_gu,
    m_gu,
    v_gu,
    w_down,
    m_down,
    v_down,
    norm_params,
    m_norms,
    v_norms,
):
    layer_count = w_qkv.shape[0]
    masked = masked_flags[:, None] == 1
    hidden = jnp.where(
        masked, mask_embedding.astype(jnp.float32)[None, :], tokens_in.astype(jnp.float32)
    )
    norm_low = lax.all_gather(norm_params.astype(jnp.bfloat16), "fsdp", axis=2, tiled=True)
    kept_list = []
    weight_list = []
    for layer in range(layer_count):
        weights = gather_layer(w_qkv[layer], w_out[layer], w_gu[layer], w_down[layer])
        weights = weights + (norm_low[layer],)
        hidden, kept_state = forward_layer(hidden, weights)
        kept_list.append(kept_state)
        weight_list.append(weights)
    activations = hidden.astype(jnp.bfloat16)
    grad_hidden = out_cotangent.astype(jnp.float32) * masked_flags[:, None].astype(jnp.float32)
    grad_list = [None] * layer_count
    norm_list = [None] * layer_count
    squares = jnp.float32(0.0)
    for layer in reversed(range(layer_count)):
        grad_hidden, local_grads = backward_layer(
            grad_hidden, weight_list[layer], kept_list[layer]
        )
        grad_list[layer], part = reduce_layer(*local_grads[:4])
        squares = squares + part
        norm_list[layer] = local_grads[4]
    grad_norms = lax.psum(jnp.stack(norm_list), both_axes)
    total = sum_all(squares) if by_neighbours() else lax.psum(squares, both_axes)
    grad_norm = jnp.sqrt(total + jnp.sum(grad_norms * grad_norms))
    factor = clip_norm / jnp.maximum(grad_norm, clip_norm)
    width = norm_params.shape[2]
    grad_norms = lax.dynamic_slice_in_dim(grad_norms, lax.axis_index("fsdp") * width, width, 2)
    states = (
        (w_qkv, m_qkv, v_qkv),
        (w_out, m_out, v_out),
        (w_gu, m_gu, v_gu),
        (w_down, m_down, v_down),
    )
    updated = []
    for kind, state in enumerate(states):
        gradient = jnp.stack([grads[kind] for grads in grad_list]).astype(jnp.float32)
        updated += adam_step(*state, gradient, factor, rate_matrix, decay_matrix)
    updated += adam_step(norm_params, m_norms, v_norms, grad_norms, factor, rate_norm, 0.0)
    input_grad = jnp.where(masked, 0.0, grad_hidden)
    return (activations, input_grad, grad_norm, *updated)


def solution(mesh):
    return jax.shard_map(
        body,
        mesh=mesh,
        in_specs=(
            P(("rep", "fsdp"), None),
            P(("rep", "fsdp")),
            P(),
            P(("rep", "fsdp"), None),
            P(None, "fsdp", None),
            P(None, "fsdp", None),
            P(None, "fsdp", None),
            P(None, "fsdp", None),
            P(None, "fsdp", None),
            P(None, "fsdp", None),
            P(None, "fsdp", None),
            P(None, "fsdp", None),
            P(None, "fsdp", None),
            P(None, "fsdp", None),
            P(None, "fsdp", None),
            P(None, "fsdp", None),
            P(None, None, "fsdp"),
            P(None, None, "fsdp"),
            P(None, None, "fsdp"),
        ),
        out_specs=(
            P(("rep", "fsdp"), None),
            P(("rep", "fsdp"), None),
            P(),
            P(None, "fsdp", None),
            P(None, "fsdp", None),
            P(None, "fsdp", None),
            P(None, "fsdp", None),
            P(None, "fsdp", None),
            P(None, "fsdp", None),
            P(None, "fsdp", None),
            P(None, "fsdp", None),
            P(None, "fsdp", None),
            P(None, "fsdp", None),
            P(None, "fsdp", None),
            P(None, "fsdp", None),
            P(None, None, "fsdp"),
            P(None, None, "fsdp"),
            P(None, None, "fsdp"),
        ),
        check_vma=False,
    )
```

```python
import jax
import jax.numpy as jnp
from jax import lax
from jax.experimental import pallas as pl
from jax.experimental.pallas import tpu as pltpu
from jax.sharding import PartitionSpec as P

D = 768
HEADS = 12
HEAD_DIM = 64
FF = 3072
SEQ_LEN = 128
STEP = 10


beta_first = 0.9
beta_second = 0.999
adam_eps = 1e-08
clip_norm = 1.0
rate_matrix = 0.03
rate_norm = 0.5
decay_matrix = 0.01
norm_eps = 1e-05


def alibi_bias(length, head_count):
    slopes = 2.0 ** (-8.0 * (jnp.arange(head_count).astype(jnp.float32) + 1.0) / head_count)
    places = jnp.arange(length).astype(jnp.float32)
    distance = jnp.abs(places[:, None] - places[None, :])
    return -slopes[:, None, None] * distance[None, :, :]


def layer_norm(values_in, norm_gain, norm_shift):
    center = values_in - jnp.mean(values_in, axis=-1, keepdims=True)
    spread = jnp.mean(center * center, axis=-1, keepdims=True)
    return center * lax.rsqrt(spread + norm_eps) * norm_gain + norm_shift


def gelu_gate(gate_part, up_part):
    return jax.nn.gelu(gate_part, approximate=False) * up_part


def outer_sum(left_rows, right_rows):
    return lax.dot_general(
        left_rows, right_rows, (((0,), (0,)), ((), ())), preferred_element_type=jnp.float32
    )


def back_product(gradient, weight):
    return lax.dot_general(
        gradient, weight, (((1,), (1,)), ((), ())), preferred_element_type=jnp.float32
    )


def split_heads(qkv_low):
    sections = qkv_low.reshape(-1, SEQ_LEN, 3, HEADS, HEAD_DIM)
    return (sections[:, :, 0], sections[:, :, 1], sections[:, :, 2])


def score_block(query_rows, key_rows):
    raw_scores = jnp.einsum(
        "sqhd,skhd->shqk", query_rows, key_rows, preferred_element_type=jnp.float32
    )
    return raw_scores * HEAD_DIM ** (-0.5) + alibi_bias(SEQ_LEN, HEADS)[None]


def forward_layer(hidden, weights):
    weight_qkv, weight_out, weight_gu, weight_down, norm_low = weights
    norm_set = norm_low.astype(jnp.float32)
    inputs_low = hidden.astype(jnp.bfloat16)
    qkv_low = jnp.dot(inputs_low, weight_qkv, preferred_element_type=jnp.float32).astype(
        jnp.bfloat16
    )
    query_rows, key_rows, value_rows = split_heads(qkv_low)
    scores = score_block(query_rows, key_rows)
    summit = jnp.max(scores, axis=-1, keepdims=True)
    log_total = summit + jnp.log(jnp.sum(jnp.exp(scores - summit), axis=-1, keepdims=True))
    attention = jnp.exp(scores - log_total)
    mixture = jnp.einsum(
        "shqk,skhd->sqhd",
        attention.astype(jnp.bfloat16),
        value_rows,
        preferred_element_type=jnp.float32,
    )
    mixture_low = mixture.reshape(hidden.shape[0], D).astype(jnp.bfloat16)
    residual_one = hidden + jnp.dot(mixture_low, weight_out, preferred_element_type=jnp.float32)
    normed_one = layer_norm(residual_one, norm_set[0], norm_set[1])
    normed_low = normed_one.astype(jnp.bfloat16)
    gate_up = jnp.dot(normed_low, weight_gu, preferred_element_type=jnp.float32)
    product_low = gelu_gate(gate_up[:, :FF], gate_up[:, FF:]).astype(jnp.bfloat16)
    residual_two = normed_one + jnp.dot(
        product_low, weight_down, preferred_element_type=jnp.float32
    )
    result = layer_norm(residual_two, norm_set[2], norm_set[3])
    kept_state = (
        inputs_low,
        qkv_low,
        log_total,
        mixture_low,
        residual_one,
        normed_low,
        gate_up,
        product_low,
        residual_two,
    )
    return (result, kept_state)


def backward_layer(grad_result, weights, kept_state):
    weight_qkv, weight_out, weight_gu, weight_down, norm_low = weights
    norm_set = norm_low.astype(jnp.float32)
    (
        inputs_low,
        qkv_low,
        log_total,
        mixture_low,
        residual_one,
        normed_low,
        gate_up,
        product_low,
        residual_two,
    ) = kept_state
    _, pull_two = jax.vjp(layer_norm, residual_two, norm_set[2], norm_set[3])
    grad_two, gain_two, shift_two = pull_two(grad_result)
    branch_low = grad_two.astype(jnp.bfloat16)
    product_grad = back_product(branch_low, weight_down).astype(jnp.bfloat16).astype(jnp.float32)
    _, pull_gate = jax.vjp(gelu_gate, gate_up[:, :FF], gate_up[:, FF:])
    grad_gate, grad_up = pull_gate(product_grad)
    gate_up_low = jnp.concatenate([grad_gate, grad_up], axis=1).astype(jnp.bfloat16)
    grad_normed = grad_two + back_product(gate_up_low, weight_gu)
    _, pull_one = jax.vjp(layer_norm, residual_one, norm_set[0], norm_set[1])
    grad_one, gain_one, shift_one = pull_one(grad_normed)
    attend_low = grad_one.astype(jnp.bfloat16)
    mixture_grad = (
        back_product(attend_low, weight_out)
        .astype(jnp.bfloat16)
        .reshape(-1, SEQ_LEN, HEADS, HEAD_DIM)
    )
    query_rows, key_rows, value_rows = split_heads(qkv_low)
    attention = jnp.exp(score_block(query_rows, key_rows) - log_total)
    attention_grad = jnp.einsum(
        "sqhd,skhd->shqk", mixture_grad, value_rows, preferred_element_type=jnp.float32
    )
    value_grad = jnp.einsum(
        "shqk,sqhd->skhd",
        attention.astype(jnp.bfloat16),
        mixture_grad,
        preferred_element_type=jnp.float32,
    )
    score_grad = attention * (
        attention_grad - jnp.sum(attention * attention_grad, axis=-1, keepdims=True)
    )
    score_low = score_grad.astype(jnp.bfloat16)
    query_grad = jnp.einsum(
        "shqk,skhd->sqhd", score_low, key_rows, preferred_element_type=jnp.float32
    ) * HEAD_DIM ** (-0.5)
    key_grad = jnp.einsum(
        "shqk,sqhd->skhd", score_low, query_rows, preferred_element_type=jnp.float32
    ) * HEAD_DIM ** (-0.5)
    qkv_grad = (
        jnp.stack([query_grad, key_grad, value_grad], axis=2)
        .reshape(inputs_low.shape[0], 3 * D)
        .astype(jnp.bfloat16)
    )
    grad_input = grad_one + back_product(qkv_grad, weight_qkv)
    grad_norms = jnp.stack([gain_one, shift_one, gain_two, shift_two])
    factors = (
        (inputs_low, qkv_grad),
        (mixture_low, attend_low),
        (normed_low, gate_up_low),
        (product_low, branch_low),
    )
    return (grad_input, factors, grad_norms)


def adam_step(weight, first_moment, second_moment, gradient, factor, step_rate, decay_rate):
    gradient = gradient * factor
    first_moment = beta_first * first_moment + (1.0 - beta_first) * gradient
    second_moment = beta_second * second_moment + (1.0 - beta_second) * gradient * gradient
    first_hat = first_moment / (1.0 - beta_first**STEP)
    second_hat = second_moment / (1.0 - beta_second**STEP)
    weight = weight - step_rate * (
        first_hat / (jnp.sqrt(second_hat) + adam_eps) + decay_rate * weight
    )
    return (weight, first_moment, second_moment)


both_axes = ("rep", "fsdp")
HALF = D // 2


def pairs_of(move):
    found = []
    for rep in range(4):
        for shard in range(8):
            to_y, to_x, to_z, to_c = move(rep // 2, rep % 2, shard // 2, shard % 2)
            found.append((rep * 8 + shard, (to_y * 2 + to_x) * 8 + to_z * 2 + to_c))
    return found


FLIP_CORE = pairs_of(lambda y, x, z, c: (y, x, z, 1 - c))
FLIP_X = pairs_of(lambda y, x, z, c: (y, 1 - x, z, c))
FLIP_Y = pairs_of(lambda y, x, z, c: (1 - y, x, z, c))
FLIP_FIRST = pairs_of(lambda y, x, z, c: (y, 1 - x, z, c) if c == 0 else (1 - y, x, z, c))
FLIP_SECOND = pairs_of(lambda y, x, z, c: (1 - y, x, z, c) if c == 0 else (y, 1 - x, z, c))
Z_ONE = pairs_of(lambda y, x, z, c: (y, x, z ^ 1, c))
Z_TWO = pairs_of(lambda y, x, z, c: (y, x, z ^ 2, c))
Z_THREE = pairs_of(lambda y, x, z, c: (y, x, z ^ 3, c))


def send(values, pairs):
    return lax.ppermute(values, both_axes, pairs)


def place():
    rep = lax.axis_index("rep")
    shard = lax.axis_index("fsdp")
    y, x, z, c = rep // 2, rep % 2, shard // 2, shard % 2
    first = jnp.where(c == 0, x, y)
    second = jnp.where(c == 0, y, x)
    return (z, c, first, second)


def place_array():
    return jnp.stack(place()).astype(jnp.int32)


def by_neighbours():
    return lax.axis_size("rep") == 4 and lax.axis_size("fsdp") == 8


def whole(array):
    zeros = (0,) * array.ndim
    return pl.BlockSpec(array.shape, lambda *_: zeros)


def kernel_cost(flops, bytes_accessed):
    return pl.CostEstimate(flops=flops, bytes_accessed=bytes_accessed, transcendentals=0)


def gather_chunk(own):
    z, c, first, second = place()
    quarter = lax.dynamic_index_in_dim(own, 2 * first + second, 0, keepdims=False)
    near = jnp.stack([send(quarter, Z_ONE), send(quarter, Z_TWO), send(quarter, Z_THREE)])
    across = send(near, FLIP_SECOND)
    far = send(near, FLIP_FIRST)
    corner = send(across, FLIP_FIRST)
    pieces = (own, near, across, far, corner)
    return pieces + tuple(send(piece, FLIP_CORE) for piece in pieces)


def assemble(pieces, kind):
    count = pieces[0].shape[1]
    rows = pieces[0].shape[2]
    shapes = {
        "attend": ((8 * rows, 3 * D), (8 * rows, D)),
        "gate_up": ((8 * rows, 2 * FF),),
        "down": ((8 * 4 * rows, D),),
    }[kind]

    def kernel(*refs):
        in_refs, out_refs, sem = refs[:10], refs[10:-1], refs[-1]
        z, c, first, second = place()

        def copy(source, quarter, block, shard):
            row = pl.multiple_of(shard * rows, rows)
            if kind == "attend":

                @pl.when(quarter < 3)
                def _():
                    column = pl.multiple_of(quarter * D, D)
                    target = out_refs[0].at[pl.ds(row, rows), pl.ds(column, D)]
                    pltpu.make_async_copy(source, target, sem).start()

                @pl.when(quarter == 3)
                def _():
                    target = out_refs[1].at[pl.ds(row, rows), :]
                    pltpu.make_async_copy(source, target, sem).start()

            elif kind == "gate_up":
                column = pl.multiple_of((quarter + 4 * block) * D, D)
                target = out_refs[0].at[pl.ds(row, rows), pl.ds(column, D)]
                pltpu.make_async_copy(source, target, sem).start()
            else:
                row = pl.multiple_of((shard * 4 + quarter) * rows, rows)
                target = out_refs[0].at[pl.ds(row, rows), :]
                pltpu.make_async_copy(source, target, sem).start()

        for side in range(2):
            own, near, across, far, corner = in_refs[5 * side : 5 * side + 5]
            core = c if side == 0 else 1 - c
            high, low = (first, second) if side == 0 else (second, first)
            for block in range(count):
                for quarter in range(4):
                    copy(own.at[quarter, block], jnp.int32(quarter), block, 2 * z + core)
                for step in range(3):
                    shard = 2 * (z ^ (step + 1)) + core
                    copy(near.at[step, block], 2 * high + low, block, shard)
                    copy(across.at[step, block], 2 * high + 1 - low, block, shard)
                    copy(far.at[step, block], 2 * (1 - high) + low, block, shard)
                    copy(corner.at[step, block], 2 * (1 - high) + 1 - low, block, shard)
        for out_ref in out_refs:
            pltpu.make_async_copy(out_ref, out_ref, sem).wait()

    return pl.pallas_call(
        kernel,
        out_shape=tuple(jax.ShapeDtypeStruct(shape, jnp.bfloat16) for shape in shapes),
        in_specs=[pl.BlockSpec(memory_space=pl.ANY)] * 10,
        out_specs=tuple(pl.BlockSpec(memory_space=pltpu.VMEM) for _ in shapes),
        scratch_shapes=[pltpu.SemaphoreType.DMA],
        compiler_params=pltpu.CompilerParams(vmem_limit_bytes=24 * 2**20),
        cost_estimate=kernel_cost(0, 2 * 2 * 8 * 4 * count * rows * D),
        name="assemble_" + kind,
    )(*pieces)


def gather_norms(norm_params):
    width = norm_params.shape[2]
    own = norm_params.astype(jnp.bfloat16).reshape(8, width)
    mine = jnp.stack([own, send(own, Z_ONE), send(own, Z_TWO), send(own, Z_THREE)])
    parts = jnp.stack([mine, send(mine, FLIP_CORE)]).astype(jnp.float32)

    def kernel(place_ref, parts_ref, out_ref):
        z, c = place_ref[0], place_ref[1]
        for shard in range(8):
            values = parts_ref[(shard % 2) ^ c, (shard // 2) ^ z]
            out_ref[:, shard * width : (shard + 1) * width] = values

    return pl.pallas_call(
        kernel,
        out_shape=jax.ShapeDtypeStruct((8, 8 * width), jnp.float32),
        in_specs=[
            pl.BlockSpec(memory_space=pltpu.SMEM),
            pl.BlockSpec(memory_space=pltpu.VMEM),
        ],
        out_specs=pl.BlockSpec(memory_space=pltpu.VMEM),
        name="norm_columns",
    )(place_array(), parts)


def chip_product(left, right, left_other, right_other):
    dims = (((0,), (0,)), ((), ()))
    return lax.dot_general(
        left, right, dims, preferred_element_type=jnp.float32
    ) + lax.dot_general(left_other, right_other, dims, preferred_element_type=jnp.float32)


def turn(step, where):
    first, second = where[2], where[3]
    return 2 * (first ^ (1 - step // 2)) + (second ^ (1 - step % 2))


def store_rows(out_ref, product, z, rows):
    for chip in range(4):
        piece = product[chip * 2 * rows : (chip + 1) * 2 * rows]
        out_ref[0, chip ^ z, 0] = piece.reshape(2, rows, HALF).astype(jnp.bfloat16)


def grad_attend(inputs, inputs_other, qkv, qkv_other, mixed, mixed_other, out, out_other):
    tokens = inputs.shape[0]
    rows = D // 8

    def kernel(where, a, a2, g, g2, o, o2, b, b2, sent, kept):
        step = pl.program_id(0)
        quarter = turn(step, where)

        def put(product):
            @pl.when(step < 2)
            def _():
                store_rows(sent, product, where[0], rows)

            @pl.when(step >= 2)
            def _():
                store_rows(kept, product, where[0], rows)

        @pl.when(quarter < 3)
        def _():
            put(chip_product(a[...], g[...], a2[...], g2[...]))

        @pl.when(quarter == 3)
        def _():
            put(chip_product(o[...], b[...], o2[...], b2[...]))

    def own_column(step, where):
        return (0, 2 * jnp.minimum(turn(step, where), 2) + where[1])

    def other_column(step, where):
        return (0, jnp.minimum(turn(step, where), 2))

    shape = (2, 4, 1, 2, rows, HALF)
    block = (1, 4, 1, 2, rows, HALF)
    return pl.pallas_call(
        kernel,
        out_shape=(jax.ShapeDtypeStruct(shape, jnp.bfloat16),) * 2,
        grid_spec=pltpu.PrefetchScalarGridSpec(
            num_scalar_prefetch=1,
            grid=(4,),
            in_specs=[
                whole(inputs),
                whole(inputs_other),
                pl.BlockSpec((tokens, HALF), own_column),
                pl.BlockSpec((tokens, HALF), other_column),
                whole(mixed),
                whole(mixed_other),
                pl.BlockSpec((tokens, HALF), lambda step, where: (0, where[1])),
                whole(out_other),
            ],
            out_specs=[
                pl.BlockSpec(block, lambda step, where: (jnp.minimum(step, 1), 0, 0, 0, 0, 0)),
                pl.BlockSpec(
                    block, lambda step, where: (jnp.maximum(step, 2) - 2, 0, 0, 0, 0, 0)
                ),
            ],
        ),
        compiler_params=pltpu.CompilerParams(vmem_limit_bytes=32 * 2**20),
        cost_estimate=kernel_cost(2 * 2 * tokens * 2 * D * D, 2 * D * 2 * D + 12 * tokens * D),
        name="grad_attend",
    )(place_array(), inputs, inputs_other, qkv, qkv_other, mixed, mixed_other, out, out_other)


def grad_gate_up(inputs, inputs_other, grads, grads_other):
    tokens = inputs.shape[0]
    rows = D // 8

    def kernel(where, a, a2, g, g2, sent, kept):
        step = pl.program_id(0)
        product = chip_product(a[...], g[...], a2[...], g2[...])

        @pl.when(step < 4)
        def _():
            store_rows(sent, product, where[0], rows)

        @pl.when(step >= 4)
        def _():
            store_rows(kept, product, where[0], rows)

    def column(step, where):
        return (step % 2) * 4 + turn(step // 2, where)

    shape = (2, 4, 2, 2, rows, HALF)
    block = (1, 4, 1, 2, rows, HALF)

    def sent_at(step, where):
        held = jnp.minimum(step, 3)
        return (held // 2, 0, held % 2, 0, 0, 0)

    def kept_at(step, where):
        held = jnp.maximum(step, 4) - 4
        return (held // 2, 0, held % 2, 0, 0, 0)

    return pl.pallas_call(
        kernel,
        out_shape=(jax.ShapeDtypeStruct(shape, jnp.bfloat16),) * 2,
        grid_spec=pltpu.PrefetchScalarGridSpec(
            num_scalar_prefetch=1,
            grid=(8,),
            in_specs=[
                whole(inputs),
                whole(inputs_other),
                pl.BlockSpec(
                    (tokens, HALF), lambda step, where: (0, 2 * column(step, where) + where[1])
                ),
                pl.BlockSpec((tokens, HALF), lambda step, where: (0, column(step, where))),
            ],
            out_specs=[pl.BlockSpec(block, sent_at), pl.BlockSpec(block, kept_at)],
        ),
        compiler_params=pltpu.CompilerParams(vmem_limit_bytes=32 * 2**20),
        cost_estimate=kernel_cost(2 * 2 * tokens * D * FF, 2 * D * FF + 8 * tokens * FF),
        name="grad_gate_up",
    )(place_array(), inputs, inputs_other, grads, grads_other)


def grad_down(inputs, inputs_other, grads, grads_other):
    tokens = inputs.shape[0]
    rows = FF // 32

    def kernel(where, a, a2, g, g2, sent, kept):
        product = chip_product(a[...], g[...], a2[...], g2[...])
        product = product.astype(jnp.bfloat16).reshape(2, 4, rows, HALF)
        for quarter in range(4):
            away = (quarter // 2) ^ where[2]
            spot = 1 - ((quarter % 2) ^ where[3])

            @pl.when(away == 1)
            def _():
                sent[spot, 0, 0] = product[:, quarter]

            @pl.when(away == 0)
            def _():
                kept[spot, 0, 0] = product[:, quarter]

    def chip_columns(step, where):
        return (0, step ^ where[0])

    shape = (2, 4, 1, 2, rows, HALF)
    spec = pl.BlockSpec((2, 1, 1, 2, rows, HALF), lambda step, where: (0, step, 0, 0, 0, 0))
    return pl.pallas_call(
        kernel,
        out_shape=(jax.ShapeDtypeStruct(shape, jnp.bfloat16),) * 2,
        grid_spec=pltpu.PrefetchScalarGridSpec(
            num_scalar_prefetch=1,
            grid=(4,),
            in_specs=[
                pl.BlockSpec((tokens, FF // 4), chip_columns),
                pl.BlockSpec((tokens, FF // 4), chip_columns),
                pl.BlockSpec((tokens, HALF), lambda step, where: (0, where[1])),
                whole(grads_other),
            ],
            out_specs=[spec, spec],
        ),
        compiler_params=pltpu.CompilerParams(vmem_limit_bytes=32 * 2**20),
        cost_estimate=kernel_cost(2 * 2 * tokens * FF * HALF, 2 * FF * HALF + 8 * tokens * FF),
        name="grad_down",
    )(place_array(), inputs, inputs_other, grads, grads_other)


def add_halves(kept, got):
    def kernel(kept_ref, got_ref, sent_ref, left_ref):
        for place_at, out_ref in ((0, sent_ref), (1, left_ref)):
            total = kept_ref[place_at].astype(jnp.float32) + got_ref[place_at].astype(jnp.float32)
            out_ref[...] = total.astype(jnp.bfloat16)

    rest = kept.shape[3:]
    count = kept.shape[2]
    spec_in = pl.BlockSpec((2, 1, count) + rest, lambda step: (0, step, 0, 0, 0, 0))
    spec_out = pl.BlockSpec((1, count) + rest, lambda step: (step, 0, 0, 0, 0))
    return pl.pallas_call(
        kernel,
        grid=(4,),
        out_shape=(jax.ShapeDtypeStruct(kept.shape[1:], jnp.bfloat16),) * 2,
        in_specs=[spec_in] * 2,
        out_specs=[spec_out] * 2,
        compiler_params=pltpu.CompilerParams(vmem_limit_bytes=32 * 2**20),
        cost_estimate=kernel_cost(kept.size, 6 * kept.size),
        name="add_halves",
    )(kept, got)


def add_chips(left, got):
    def kernel(left_ref, got_ref, *out_refs):
        for chip, out_ref in enumerate(out_refs):
            total = left_ref[chip].astype(jnp.float32) + got_ref[chip].astype(jnp.float32)
            out_ref[...] = total.astype(jnp.bfloat16)

    return pl.pallas_call(
        kernel,
        out_shape=(jax.ShapeDtypeStruct(left.shape[1:], jnp.bfloat16),) * 4,
        in_specs=[pl.BlockSpec(memory_space=pltpu.VMEM)] * 2,
        out_specs=[pl.BlockSpec(memory_space=pltpu.VMEM)] * 4,
        compiler_params=pltpu.CompilerParams(vmem_limit_bytes=32 * 2**20),
        cost_estimate=kernel_cost(left.size, 6 * left.size),
        name="add_chips",
    )(left, got)


def add_last(parts):
    count, _, rows, width = parts[0].shape

    def kernel(where, *refs):
        part_refs, (mine, theirs, squares) = refs[:4], refs[4:]
        total = jnp.zeros((8, width), jnp.float32)
        for block in range(count):
            for core in range(2):
                value = part_refs[0][block, core].astype(jnp.float32)
                for part_ref in part_refs[1:]:
                    value = value + part_ref[block, core].astype(jnp.float32)
                low = value.astype(jnp.bfloat16)
                value = low.astype(jnp.float32)
                total = total + jnp.sum((value * value).reshape(rows // 8, 8, width), axis=0)

                @pl.when(where[1] == core)
                def _():
                    mine[block] = low

                @pl.when(where[1] != core)
                def _():
                    theirs[block] = low

        squares[...] = total

    shape = jax.ShapeDtypeStruct((count, rows, width), jnp.bfloat16)
    vmem = pl.BlockSpec(memory_space=pltpu.VMEM)
    return pl.pallas_call(
        kernel,
        out_shape=(shape, shape, jax.ShapeDtypeStruct((8, width), jnp.float32)),
        in_specs=[pl.BlockSpec(memory_space=pltpu.SMEM)] + [vmem] * 4,
        out_specs=[vmem] * 3,
        compiler_params=pltpu.CompilerParams(vmem_limit_bytes=32 * 2**20),
        cost_estimate=kernel_cost(4 * parts[0].size, 10 * parts[0].size),
        name="add_last",
    )(place_array(), *parts)


def reduce_chunk(sent, kept):
    away, left = add_halves(kept, send(sent, FLIP_FIRST))
    parts = add_chips(left, send(away, FLIP_SECOND))
    parts = (
        parts[0],
        send(parts[1], Z_ONE),
        send(parts[2], Z_TWO),
        send(parts[3], Z_THREE),
    )
    mine, theirs, squares = add_last(parts)
    pair = jnp.stack([mine, send(theirs, FLIP_CORE)])
    across = send(pair, FLIP_SECOND)
    far = send(pair, FLIP_FIRST)
    return ((pair, across, far, send(across, FLIP_FIRST)), squares)


def other_half(grads, c):
    tokens, width = grads.shape
    blocks = grads.reshape(tokens, width // D, 2, HALF)
    chosen = jnp.where(c == 0, blocks[:, :, 1], blocks[:, :, 0])
    return chosen.reshape(tokens, width // 2)


def reduce_layer(factors):
    (inputs, qkv), (mixed, out), (normed, gate_up), (product, branch) = factors
    c = place()[1]
    rest = tuple(send(other_half(grads, c), FLIP_CORE) for grads in (qkv, out, gate_up, branch))
    qkv_other, out_other, gate_up_other, branch_other = rest
    down = grad_down(product, send(product, FLIP_CORE), branch, branch_other)
    wide = grad_gate_up(normed, send(normed, FLIP_CORE), gate_up, gate_up_other)
    attend = grad_attend(
        inputs,
        send(inputs, FLIP_CORE),
        qkv,
        qkv_other,
        mixed,
        send(mixed, FLIP_CORE),
        out,
        out_other,
    )
    down, squares_down = reduce_chunk(*down)
    wide, squares_wide = reduce_chunk(*wide)
    attend, squares_attend = reduce_chunk(*attend)
    return (attend, wide, down, squares_down + squares_wide + squares_attend)


def adam_blocks(weight, first_moment, second_moment, layers, factor, kind):
    layer_count, rows_all, width = weight.shape
    rows = layers[0][0].shape[2]
    blocks = (rows_all // rows) * (width // D)
    by_rows = rows_all // rows

    def kernel(where, factor_ref, w, m, v, *refs):
        piece_refs, outs = refs[: 4 * layer_count], refs[4 * layer_count :]
        layer = pl.program_id(0)
        block = pl.program_id(1)
        c, first, second = where[1], where[2], where[3]
        if kind == "gate_up":
            quarter, index = block % 4, block // 4
        elif kind == "out":
            quarter, index = 3, 0
        else:
            quarter, index = block, 0
        for half in range(2):
            other = c ^ half
            swapped = other == 1
            high, low = quarter // 2, quarter % 2
            flip_first = first ^ jnp.where(swapped, low, high)
            flip_second = second ^ jnp.where(swapped, high, low)
            number = 2 * flip_first + flip_second
            columns = slice(half * HALF, (half + 1) * HALF)

            def pick_piece(at):
                values = [piece_refs[4 * at + turn][other, index] for turn in range(4)]
                low_pair = jnp.where(number % 2 == 0, values[0], values[1])
                high_pair = jnp.where(number % 2 == 0, values[2], values[3])
                return jnp.where(number // 2 == 0, low_pair, high_pair).astype(jnp.float32)

            gradient = pick_piece(0)
            for at in range(1, layer_count):
                gradient = jnp.where(layer == at, pick_piece(at), gradient)
            results = adam_step(
                w[0, :, columns],
                m[0, :, columns],
                v[0, :, columns],
                gradient,
                factor_ref[0],
                rate_matrix,
                decay_matrix,
            )
            for out, result in zip(outs, results):
                out[0, :, columns] = result

    def at(layer, block, where):
        return (layer, block, 0) if by_rows > 1 else (layer, 0, block)

    state = pl.BlockSpec((1, rows, D), at)
    pieces = [piece for layer in layers for piece in layer]
    return pl.pallas_call(
        kernel,
        out_shape=(jax.ShapeDtypeStruct(weight.shape, jnp.float32),) * 3,
        grid_spec=pltpu.PrefetchScalarGridSpec(
            num_scalar_prefetch=1,
            grid=(layer_count, blocks),
            in_specs=[pl.BlockSpec(memory_space=pltpu.SMEM)]
            + [state] * 3
            + [whole(piece) for piece in pieces],
            out_specs=[state] * 3,
        ),
        compiler_params=pltpu.CompilerParams(vmem_limit_bytes=32 * 2**20),
        cost_estimate=kernel_cost(20 * weight.size, 24 * weight.size),
        name="adam_" + kind,
    )(place_array(), factor.reshape(1), weight, first_moment, second_moment, *pieces)


def sum_all(value):
    for pairs in (FLIP_CORE, FLIP_X, FLIP_Y, Z_ONE, Z_TWO):
        value = value + send(value, pairs)
    return value


def gather_layer(w_qkv, w_out, w_gu, w_down):
    low = [weight.astype(jnp.bfloat16) for weight in (w_qkv, w_out, w_gu, w_down)]
    if not by_neighbours():
        return tuple(lax.all_gather(weight, "fsdp", axis=0, tiled=True) for weight in low)
    rows = w_qkv.shape[0]
    attend = jnp.stack([low[0][:, :D], low[0][:, D : 2 * D], low[0][:, 2 * D :], low[1]])
    gate_up = low[2].reshape(rows, 2, 4, D).transpose(2, 1, 0, 3)
    down = low[3].reshape(4, 1, rows, D)
    weight_qkv, weight_out = assemble(gather_chunk(attend[:, None]), "attend")
    (weight_gu,) = assemble(gather_chunk(gate_up), "gate_up")
    (weight_down,) = assemble(gather_chunk(down), "down")
    return (weight_qkv, weight_out, weight_gu, weight_down)


def update(states, norm_state, factors, norm_list):
    layer_count = len(factors)
    norm_grads = jnp.concatenate(norm_list)
    width = norm_state[0].shape[2]
    if by_neighbours():
        reduced = [None] * layer_count
        squares = jnp.zeros((8, HALF), jnp.float32)
        for layer in reversed(range(layer_count)):
            *reduced[layer], part = reduce_layer(factors[layer])
            squares = squares + part
        rows = norm_grads.shape[0]
        packed = jnp.concatenate([norm_grads, jnp.pad(squares, ((0, 0), (0, D - HALF)))])
        packed = sum_all(packed)
        norm_grads = packed[:rows]
        total = jnp.sum(packed[rows:])
    else:
        total = jnp.float32(0.0)
        reduced = []
        for layer in range(layer_count):
            sums = []
            for left, right in factors[layer]:
                part = outer_sum(left, right)
                part = lax.psum_scatter(part, "fsdp", scatter_dimension=0, tiled=True)
                part = lax.psum(part, "rep")
                total = total + jnp.sum(part * part)
                sums.append(part)
            reduced.append(sums)
        total = lax.psum(total, "fsdp")
        norm_grads = lax.psum(norm_grads, both_axes)
    grad_norm = jnp.sqrt(total + jnp.sum(norm_grads * norm_grads))
    factor = clip_norm / jnp.maximum(grad_norm, clip_norm)
    updated = []
    for kind, state in enumerate(states):
        if by_neighbours():
            chunk, name = ((0, "qkv"), (0, "out"), (1, "gate_up"), (2, "down"))[kind]
            layers = [pieces[chunk] for pieces in reduced]
            updated += adam_blocks(*state, layers, factor, name)
        else:
            gradient = jnp.stack([sums[kind] for sums in reduced])
            updated += adam_step(*state, gradient, factor, rate_matrix, decay_matrix)
    norm_grads = norm_grads.reshape(layer_count, -1, D)
    norm_grads = lax.dynamic_slice_in_dim(norm_grads, lax.axis_index("fsdp") * width, width, 2)
    updated += adam_step(*norm_state, norm_grads, factor, rate_norm, 0.0)
    return (grad_norm, updated)


def body(
    tokens_in,
    masked_flags,
    mask_embedding,
    out_cotangent,
    w_qkv,
    m_qkv,
    v_qkv,
    w_out,
    m_out,
    v_out,
    w_gu,
    m_gu,
    v_gu,
    w_down,
    m_down,
    v_down,
    norm_params,
    m_norms,
    v_norms,
):
    layer_count = w_qkv.shape[0]
    masked = masked_flags[:, None] == 1
    hidden = jnp.where(
        masked, mask_embedding.astype(jnp.float32)[None, :], tokens_in.astype(jnp.float32)
    )
    if by_neighbours():
        norm_all = gather_norms(norm_params).reshape(layer_count, 4, D)
    else:
        norm_all = lax.all_gather(norm_params.astype(jnp.bfloat16), "fsdp", axis=2, tiled=True)
    kept_list = []
    weight_list = []
    for layer in range(layer_count):
        weights = gather_layer(w_qkv[layer], w_out[layer], w_gu[layer], w_down[layer])
        weights = weights + (norm_all[layer],)
        hidden, kept_state = forward_layer(hidden, weights)
        kept_list.append(kept_state)
        weight_list.append(weights)
    activations = hidden.astype(jnp.bfloat16)
    grad_hidden = out_cotangent.astype(jnp.float32) * masked_flags[:, None].astype(jnp.float32)
    factor_list = [None] * layer_count
    norm_list = [None] * layer_count
    for layer in reversed(range(layer_count)):
        grad_hidden, factor_list[layer], norm_list[layer] = backward_layer(
            grad_hidden, weight_list[layer], kept_list[layer]
        )
    states = (
        (w_qkv, m_qkv, v_qkv),
        (w_out, m_out, v_out),
        (w_gu, m_gu, v_gu),
        (w_down, m_down, v_down),
    )
    norm_state = (norm_params, m_norms, v_norms)
    grad_norm, updated = update(states, norm_state, factor_list, norm_list)
    input_grad = jnp.where(masked, 0.0, grad_hidden)
    return (activations, input_grad, grad_norm, *updated)


def solution(mesh):
    return jax.shard_map(
        body,
        mesh=mesh,
        in_specs=(
            P(("rep", "fsdp"), None),
            P(("rep", "fsdp")),
            P(),
            P(("rep", "fsdp"), None),
            P(None, "fsdp", None),
            P(None, "fsdp", None),
            P(None, "fsdp", None),
            P(None, "fsdp", None),
            P(None, "fsdp", None),
            P(None, "fsdp", None),
            P(None, "fsdp", None),
            P(None, "fsdp", None),
            P(None, "fsdp", None),
            P(None, "fsdp", None),
            P(None, "fsdp", None),
            P(None, "fsdp", None),
            P(None, None, "fsdp"),
            P(None, None, "fsdp"),
            P(None, None, "fsdp"),
        ),
        out_specs=(
            P(("rep", "fsdp"), None),
            P(("rep", "fsdp"), None),
            P(),
            P(None, "fsdp", None),
            P(None, "fsdp", None),
            P(None, "fsdp", None),
            P(None, "fsdp", None),
            P(None, "fsdp", None),
            P(None, "fsdp", None),
            P(None, "fsdp", None),
            P(None, "fsdp", None),
            P(None, "fsdp", None),
            P(None, "fsdp", None),
            P(None, "fsdp", None),
            P(None, "fsdp", None),
            P(None, None, "fsdp"),
            P(None, None, "fsdp"),
            P(None, None, "fsdp"),
        ),
        check_vma=False,
    )
```

```python
import jax
import jax.numpy as jnp
from jax import lax
from jax.experimental import pallas as pl
from jax.experimental.pallas import tpu as pltpu
from jax.sharding import PartitionSpec as P

D = 768
HEADS = 12
HEAD_DIM = 64
FF = 3072
SEQ_LEN = 128
STEP = 10
HALF = D // 2
PAIR = 2 * HEAD_DIM


beta_first = 0.9
beta_second = 0.999
adam_eps = 1e-08
clip_norm = 1.0
rate_matrix = 0.03
rate_norm = 0.5
decay_matrix = 0.01
norm_eps = 1e-05
low_type = jnp.bfloat16
wide_type = jnp.float32
both_axes = ("rep", "fsdp")


def pairs_of(move):
    found = []
    for rep in range(4):
        for shard in range(8):
            to_y, to_x, to_z, to_c = move(rep // 2, rep % 2, shard // 2, shard % 2)
            found.append((rep * 8 + shard, (to_y * 2 + to_x) * 8 + to_z * 2 + to_c))
    return found


FLIP_CORE = pairs_of(lambda y, x, z, c: (y, x, z, 1 - c))
FLIP_X = pairs_of(lambda y, x, z, c: (y, 1 - x, z, c))
FLIP_Y = pairs_of(lambda y, x, z, c: (1 - y, x, z, c))
FLIP_FIRST = pairs_of(lambda y, x, z, c: (y, 1 - x, z, c) if c == 0 else (1 - y, x, z, c))
FLIP_SECOND = pairs_of(lambda y, x, z, c: (1 - y, x, z, c) if c == 0 else (y, 1 - x, z, c))
Z_ONE = pairs_of(lambda y, x, z, c: (y, x, z ^ 1, c))
Z_TWO = pairs_of(lambda y, x, z, c: (y, x, z ^ 2, c))
Z_THREE = pairs_of(lambda y, x, z, c: (y, x, z ^ 3, c))


def send(values, pairs):
    return lax.ppermute(values, both_axes, pairs)


def place():
    rep = lax.axis_index("rep")
    shard = lax.axis_index("fsdp")
    y, x, z, c = rep // 2, rep % 2, shard // 2, shard % 2
    first = jnp.where(c == 0, x, y)
    second = jnp.where(c == 0, y, x)
    return (z, c, first, second)


def by_neighbours():
    return lax.axis_size("rep") == 4 and lax.axis_size("fsdp") == 8


def run(
    kernel, name, where, args, in_specs, outs, out_specs, grid=(1,), scratch=(), after=(), reuse=None
):
    first_out = 1 + len(args) + len(after)

    def body_of(*refs):
        kernel(*refs[: 1 + len(args)], *refs[first_out:])

    return pl.pallas_call(
        body_of,
        out_shape=[jax.ShapeDtypeStruct(shape, dtype) for shape, dtype in outs],
        grid_spec=pltpu.PrefetchScalarGridSpec(
            num_scalar_prefetch=1,
            grid=grid,
            in_specs=list(in_specs) + [pl.BlockSpec(memory_space=pl.ANY)] * len(after),
            out_specs=list(out_specs),
            scratch_shapes=list(scratch),
        ),
        input_output_aliases={1 + at: out for at, out in (reuse or {}).items()},
        compiler_params=pltpu.CompilerParams(vmem_limit_bytes=40 * 2**20),
        cost_estimate=pl.CostEstimate(flops=1000, bytes_accessed=1000, transcendentals=0),
        name=name,
    )(where, *args, *after)


class Chain:
    def __init__(self, where):
        self.where = where
        self.last = ()

    def __call__(self, call, *args):
        results = call(*args, self.where, self.last)
        self.last = (min(results, key=lambda array: array.size),)
        return results

    def wait(self, *arrays):
        self.last += arrays


def full(shape):
    zeros = (0,) * len(shape)
    return pl.BlockSpec(shape, lambda *_: zeros)


def fulls(arrays):
    return [full(array.shape) for array in arrays]


def dot(left, right):
    return jnp.dot(left, right, preferred_element_type=wide_type)


def dot_right(left, right):
    return lax.dot_general(
        left, right, (((1,), (1,)), ((), ())), preferred_element_type=wide_type
    )


def dot_left(left, right):
    return lax.dot_general(
        left, right, (((0,), (0,)), ((), ())), preferred_element_type=wide_type
    )


def spread_of(values):
    center = values - jnp.mean(values, axis=-1, keepdims=True)
    variance = jnp.mean(center * center, axis=-1, keepdims=True)
    scale = lax.rsqrt(variance + norm_eps)
    return (center * scale, scale)


def norm_back(grad, values, gain):
    unit, scale = spread_of(values)
    inner = grad * gain
    mean_inner = jnp.mean(inner, axis=-1, keepdims=True)
    mean_product = jnp.mean(inner * unit, axis=-1, keepdims=True)
    grad_values = scale * (inner - mean_inner - unit * mean_product)
    return (
        grad_values,
        jnp.sum(grad * unit, axis=0, keepdims=True),
        jnp.sum(grad, axis=0, keepdims=True),
    )


def put_theirs(out_ref, at, block, core):
    @pl.when(core == 0)
    def _():
        out_ref[at] = block[:, HALF:]

    @pl.when(core != 0)
    def _():
        out_ref[at] = block[:, :HALF]


def head_tools():
    lane = lax.broadcasted_iota(jnp.int32, (1, PAIR), 1)
    masks = ((lane < HEAD_DIM).astype(low_type), (lane >= HEAD_DIM).astype(low_type))
    rows = lax.broadcasted_iota(jnp.int32, (SEQ_LEN, SEQ_LEN), 0)
    columns = lax.broadcasted_iota(jnp.int32, (SEQ_LEN, SEQ_LEN), 1)
    distance = jnp.abs(rows - columns).astype(wide_type)
    return (masks, distance, columns)


def head_slope(head):
    return 2.0 ** (-8.0 * (head + 1.0) / HEADS)


def attend_forward(hidden, weight_qkv, weight_out, norms, layer, where, after=()):
    tokens = hidden.shape[0]

    def kernel(where, h, wq, wo, n, trio, qkv, log_total, residual, normed):
        low = h[...].astype(low_type)
        trio[0] = low
        for part in range(3):
            columns = slice(part * D, (part + 1) * D)
            qkv[:, columns] = dot(low, wq[:, columns]).astype(low_type)
        masks, distance, lanes = head_tools()
        for sequence in range(tokens // SEQ_LEN):
            rows = slice(sequence * SEQ_LEN, (sequence + 1) * SEQ_LEN)
            logs = jnp.zeros((SEQ_LEN, SEQ_LEN), wide_type)
            for pair in range(HEADS // 2):
                query, key, value = (
                    qkv[rows, part * D + pair * PAIR : part * D + (pair + 1) * PAIR]
                    for part in range(3)
                )
                mixture = jnp.zeros((SEQ_LEN, PAIR), wide_type)
                for side in range(2):
                    head = 2 * pair + side
                    scores = dot_right(query * masks[side], key) * HEAD_DIM ** (-0.5)
                    scores = scores - head_slope(head) * distance
                    summit = jnp.max(scores, axis=-1, keepdims=True)
                    powers = jnp.exp(scores - summit)
                    total = jnp.sum(powers, axis=-1, keepdims=True)
                    logs = jnp.where(lanes == head, summit + jnp.log(total), logs)
                    attention = (powers * (1.0 / total)).astype(low_type)
                    mixture = mixture + dot(attention, value * masks[side])
                trio[1, rows, pair * PAIR : (pair + 1) * PAIR] = mixture.astype(low_type)
            log_total[rows, :] = logs
        total = h[...] + dot(trio[1], wo[...])
        residual[...] = total
        unit, _ = spread_of(total)
        result = unit * n[4 * layer : 4 * layer + 1] + n[4 * layer + 1 : 4 * layer + 2]
        normed[...] = result
        trio[2] = result.astype(low_type)

    args = (hidden, weight_qkv, weight_out, norms)
    outs = [
        ((3, tokens, D), low_type),
        ((tokens, 3 * D), low_type),
        ((tokens, SEQ_LEN), wide_type),
        ((tokens, D), wide_type),
        ((tokens, D), wide_type),
    ]
    specs = [full(shape) for shape, _ in outs]
    return run(kernel, "attend_forward", where, args, fulls(args), outs, specs, after=after)


def gate_forward(trio, weight_gu, where, after=()):
    tokens = trio.shape[1]

    def kernel(where, a, wg, wu, product, slopes):
        gate = dot(a[0], wg[...])
        up = dot(a[0], wu[...])
        bell = 0.5 * (1.0 + lax.erf(gate * 0.5**0.5))
        curve = gate * bell
        product[...] = (curve * up).astype(low_type)
        density = jnp.exp(-0.5 * gate * gate) * 0.3989422804014327
        slopes[0] = (up * (bell + gate * density)).astype(low_type)
        slopes[1] = curve.astype(low_type)

    return run(
        kernel,
        "gate_forward",
        where,
        (trio, weight_gu, weight_gu),
        [
            pl.BlockSpec((1, tokens, D), lambda step, where: (2, 0, 0)),
            pl.BlockSpec((D, D), lambda step, where: (0, step)),
            pl.BlockSpec((D, D), lambda step, where: (0, step + FF // D)),
        ],
        [((tokens, FF), low_type), ((2, tokens, FF), low_type)],
        [
            pl.BlockSpec((tokens, D), lambda step, where: (0, step)),
            pl.BlockSpec((2, tokens, D), lambda step, where: (0, 0, step)),
        ],
        grid=(FF // D,),
        after=after,
    )


def down_forward(product, weight_down, normed, norms, layer, where, after=()):
    tokens = normed.shape[0]

    def kernel(where, x, w, h, n, residual, result):
        step = pl.program_id(0)

        @pl.when(step == 0)
        def _():
            residual[...] = h[...]

        residual[...] += dot(x[...], w[...])

        @pl.when(step == FF // D - 1)
        def _():
            unit, _ = spread_of(residual[...])
            result[...] = unit * n[4 * layer + 2 : 4 * layer + 3] + n[4 * layer + 3 : 4 * layer + 4]

    return run(
        kernel,
        "down_forward",
        where,
        (product, weight_down, normed, norms),
        [
            pl.BlockSpec((tokens, D), lambda step, where: (0, step)),
            pl.BlockSpec((D, D), lambda step, where: (step, 0)),
            full(normed.shape),
            full(norms.shape),
        ],
        [((tokens, D), wide_type)] * 2,
        [full((tokens, D))] * 2,
        grid=(FF // D,),
        after=after,
    )


def feed_backward(grad, residual_two, residual_one, slopes, weights, norms, layer, where, after=()):
    _, weight_out, weight_gu, weight_down = weights
    tokens = grad.shape[0]
    last = FF // D - 1

    def kernel(where, g, r2, r1, s, wd, wg, wu, wo, n, *refs):
        gates, theirs, branch, grad_one, attend, mixed, grad_norms, total = refs
        step = pl.program_id(0)
        core = where[1]

        def norm_row(at):
            return n[4 * layer + at : 4 * layer + at + 1]

        @pl.when(step == 0)
        def _():
            grad_two, gain, shift = norm_back(g[...], r2[...], norm_row(2))
            total[...] = grad_two
            low = grad_two.astype(low_type)
            branch[...] = low
            put_theirs(theirs, (slice(None), slice(8 * HALF, 9 * HALF)), low, core)
            grad_norms[2:3] = gain
            grad_norms[3:4] = shift

        grad_product = dot_right(branch[...], wd[...]).astype(low_type).astype(wide_type)
        for side, weight in ((0, wg), (1, wu)):
            low = (grad_product * s[side].astype(wide_type)).astype(low_type)
            gates[side] = low
            column = pl.multiple_of((4 * side + step) * HALF, HALF)
            put_theirs(theirs, (slice(None), pl.ds(column, HALF)), low, core)
            total[...] += dot_right(low, weight[...])

        @pl.when(step == last)
        def _():
            one, gain, shift = norm_back(total[...], r1[...], norm_row(0))
            grad_one[...] = one
            low = one.astype(low_type)
            attend[...] = low
            put_theirs(theirs, (slice(None), slice(9 * HALF, 10 * HALF)), low, core)
            mixed[...] = dot_right(low, wo[...]).astype(low_type)
            grad_norms[0:1] = gain
            grad_norms[1:2] = shift

    def columns(step, where):
        return (0, 0, step)

    outs = [
        ((2, tokens, FF), low_type),
        ((tokens, 10 * HALF), low_type),
        ((tokens, D), low_type),
        ((tokens, D), wide_type),
        ((tokens, D), low_type),
        ((tokens, D), low_type),
        ((4, D), wide_type),
    ]
    return run(
        kernel,
        "feed_backward",
        where,
        (
            grad,
            residual_two,
            residual_one,
            slopes,
            weight_down,
            weight_gu,
            weight_gu,
            weight_out,
            norms,
        ),
        [
            full(grad.shape),
            full(grad.shape),
            full(grad.shape),
            pl.BlockSpec((2, tokens, D), columns),
            pl.BlockSpec((D, D), lambda step, where: (step, 0)),
            pl.BlockSpec((D, D), lambda step, where: (0, step)),
            pl.BlockSpec((D, D), lambda step, where: (0, step + FF // D)),
            full(weight_out.shape),
            full(norms.shape),
        ],
        outs,
        [
            pl.BlockSpec((2, tokens, D), columns),
        ]
        + [full(shape) for shape, _ in outs[1:]],
        grid=(FF // D,),
        scratch=[pltpu.VMEM((tokens, D), wide_type)],
        after=after,
    )


def attend_backward(grad_mixed, qkv, log_total, grad_one, weight_qkv, where, after=()):
    tokens = grad_mixed.shape[0]

    def kernel(where, g, x, logs, one, wq, grads, theirs, result):
        masks, distance, lanes = head_tools()
        for sequence in range(tokens // SEQ_LEN):
            rows = slice(sequence * SEQ_LEN, (sequence + 1) * SEQ_LEN)
            all_logs = logs[rows, :]
            for pair in range(HEADS // 2):
                columns = [
                    slice(part * D + pair * PAIR, part * D + (pair + 1) * PAIR)
                    for part in range(3)
                ]
                query, key, value = (x[rows, column] for column in columns)
                grad = g[rows, columns[0]]
                sums = [jnp.zeros((SEQ_LEN, PAIR), wide_type) for _ in range(3)]
                for side in range(2):
                    head = 2 * pair + side
                    mask = masks[side]
                    scores = dot_right(query * mask, key) * HEAD_DIM ** (-0.5)
                    scores = scores - head_slope(head) * distance
                    attention = jnp.exp(scores - all_logs[:, head : head + 1])
                    grad_side = grad * mask
                    grad_attention = dot_right(grad_side, value)
                    sums[2] += dot_left(attention.astype(low_type), grad_side)
                    weighted = attention * grad_attention
                    inner = jnp.sum(weighted, axis=-1, keepdims=True)
                    grad_scores = (weighted - attention * inner).astype(low_type)
                    sums[0] += dot(grad_scores, key * mask)
                    sums[1] += dot_left(grad_scores, query * mask)
                for column, total, scale in zip(
                    columns, sums, (HEAD_DIM ** (-0.5), HEAD_DIM ** (-0.5), 1.0)
                ):
                    grads[rows, column] = (total * scale).astype(low_type)
        total = one[...]
        for part in range(3):
            block = grads[:, part * D : (part + 1) * D]
            total = total + dot_right(block, wq[:, part * D : (part + 1) * D])
            at = (slice(None), slice(part * HALF, (part + 1) * HALF))
            put_theirs(theirs, at, block, where[1])
        result[...] = total

    args = (grad_mixed, qkv, log_total, grad_one, weight_qkv)
    outs = [
        ((tokens, 3 * D), low_type),
        ((tokens, 3 * HALF), low_type),
        ((tokens, D), wide_type),
    ]
    specs = [full(shape) for shape, _ in outs]
    return run(kernel, "attend_backward", where, args, fulls(args), outs, specs, after=after)


KINDS = ("attend", "gate_up", "down")
BLOCKS = {"attend": 1, "gate_up": 2, "down": 1}


NORM_ROWS = 16


def own_chunks(chunks, weights, norm_params, where, after=()):
    rows = weights[0].shape[1]
    more = 0 if norm_params is None else NORM_ROWS
    counts = [BLOCKS[kind] for kind, _ in chunks]
    names = {"attend": (0, 1), "gate_up": (2,), "down": (3,)}
    used = [(at, layer) for kind, layer in chunks for at in names[kind]]

    def kernel(where, *refs):
        matrix = dict(zip(used, refs))
        owns, quarters = refs[len(args) : -1], refs[-1]
        start = 0
        if more:
            quarters[:, rows:] = jnp.zeros((sum(counts), more, D), low_type)
            count, width = norm_params.shape
            quarters[0, rows : rows + count, :width] = refs[len(used)][...].astype(low_type)
        for (kind, layer), own, count in zip(chunks, owns, counts):
            if kind == "attend":
                for part in range(3):
                    values = matrix[0, layer][0, :, part * D : (part + 1) * D]
                    own[part, 0] = values.astype(low_type)
                own[3, 0] = matrix[1, layer][0].astype(low_type)
            elif kind == "gate_up":
                for block in range(8):
                    values = matrix[2, layer][0, :, block * D : (block + 1) * D]
                    own[block % 4, block // 4] = values.astype(low_type)
            else:
                for block in range(4):
                    values = matrix[3, layer][0, block * rows : (block + 1) * rows, :]
                    own[block, 0] = values.astype(low_type)
            quarters[start : start + count, :rows] = own[2 * where[2] + where[3]]
            start += count

    def at_layer(layer):
        return lambda step, where: (layer, 0, 0)

    args = [weights[at] for at, _ in used]
    specs = [
        pl.BlockSpec((1,) + weights[at].shape[1:], at_layer(layer)) for at, layer in used
    ]
    if more:
        args.append(norm_params)
        specs.append(full(norm_params.shape))
    outs = [((4, count, rows, D), low_type) for count in counts]
    outs.append(((sum(counts), rows + more, D), low_type))
    out_specs = [full(shape) for shape, _ in outs]
    return run(kernel, "own_chunks", where, args, specs, outs, out_specs, after=after)


def stack_chips(arrived, rows, where, after=()):
    count = arrived[0].shape[0]
    more = arrived[0].shape[1] - rows

    def kernel(where, *refs):
        out, rest = refs[3:]
        for spot in range(3):
            out[spot] = refs[spot][:, :rows]
            if more:
                rest[spot] = refs[spot][0, rows:, :SEQ_LEN]

    shape = (3, count, rows, D)
    rest = (3, max(more, NORM_ROWS), SEQ_LEN)
    outs = [(shape, low_type), (rest, low_type)]
    specs = [full(shape), full(rest)]
    return run(kernel, "stack_chips", where, arrived, fulls(arrived), outs, specs, after=after)


def stack_two(one, two, where, after=()):
    def kernel(where, one, two, out, token, sem):
        copies = [
            pltpu.make_async_copy(one, out.at[0], sem.at[0]),
            pltpu.make_async_copy(two, out.at[1], sem.at[1]),
        ]
        for copy in copies:
            copy.start()
        for copy in copies:
            copy.wait()

    shape = (2,) + one.shape
    return run(
        kernel,
        "stack_two",
        where,
        (one, two),
        [pl.BlockSpec(memory_space=pl.ANY)] * 2,
        [(shape, low_type), ((8, 128), low_type)],
        [full(shape), full((8, 128))],
        scratch=[pltpu.SemaphoreType.DMA((2,))],
        after=after,
    )


def pack(owns, six, far, where, after=()):
    counts = [own.shape[1] for own in owns]
    total, rows = sum(counts), owns[0].shape[2]
    number = len(owns) + 4

    def kernel(where, *refs):
        in_refs, (six_ref, far_ref, out, token, sem) = refs[: len(owns)], refs[len(owns) :]
        moves = []
        begin = 0
        for ref, count in zip(in_refs, counts):
            moves.append((ref, out.at[pl.ds(0, 4), pl.ds(begin, count)]))
            begin += count
        for index in range(4):
            ref = (six_ref, far_ref)[index // 2]
            moves.append((ref.at[index % 2], out.at[pl.ds(4 + 3 * index, 3)]))
        copies = [
            pltpu.make_async_copy(*move, sem.at[index]) for index, move in enumerate(moves)
        ]
        for copy in copies:
            copy.start()
        for copy in copies:
            copy.wait()

    shape = (16, total, rows, D)
    return run(
        kernel,
        "pack",
        where,
        (*owns, six, far),
        [pl.BlockSpec(memory_space=pl.ANY)] * (len(owns) + 2),
        [(shape, low_type), ((8, 128), low_type)],
        [full(shape), full((8, 128))],
        scratch=[pltpu.SemaphoreType.DMA((number,))],
        after=after,
    )


def assemble(pieces, kind, begin, where, after=()):
    count = pieces[0].shape[1]
    rows = pieces[0].shape[2]
    shapes = {
        "attend": ((8 * rows, 3 * D), (8 * rows, D)),
        "gate_up": ((8 * rows, 2 * FF),),
        "down": ((8 * 4 * rows, D),),
    }[kind]

    def kernel(where, *refs):
        own_ref, six_ref, far_ref, packed = refs[:4]
        out_refs, sem = refs[4:-1], refs[-1]
        mine = (own_ref, six_ref.at[0], six_ref.at[1], far_ref.at[0], far_ref.at[1])
        others = (packed, *(packed.at[pl.ds(at, 3)] for at in (4, 7, 10, 13)))
        z, c, first, second = (where[at] for at in range(4))

        def copy(source, quarter, block, shard):
            row = pl.multiple_of(shard * rows, rows)
            if kind == "attend":

                @pl.when(quarter < 3)
                def _():
                    column = pl.multiple_of(quarter * D, D)
                    target = out_refs[0].at[pl.ds(row, rows), pl.ds(column, D)]
                    pltpu.make_async_copy(source, target, sem).start()

                @pl.when(quarter == 3)
                def _():
                    target = out_refs[1].at[pl.ds(row, rows), :]
                    pltpu.make_async_copy(source, target, sem).start()

            elif kind == "gate_up":
                column = pl.multiple_of((quarter + 4 * block) * D, D)
                target = out_refs[0].at[pl.ds(row, rows), pl.ds(column, D)]
                pltpu.make_async_copy(source, target, sem).start()
            else:
                row = pl.multiple_of((shard * 4 + quarter) * rows, rows)
                target = out_refs[0].at[pl.ds(row, rows), :]
                pltpu.make_async_copy(source, target, sem).start()

        for side in range(2):
            own, near, across, far, corner = mine if side == 0 else others
            own_begin = 0 if side == 0 else begin
            core = c if side == 0 else 1 - c
            high, low = (first, second) if side == 0 else (second, first)
            for block in range(count):
                for quarter in range(4):
                    copy(
                        own.at[quarter, own_begin + block], jnp.int32(quarter), block, 2 * z + core
                    )
                for step in range(3):
                    shard = 2 * (z ^ (step + 1)) + core
                    copy(near.at[step, begin + block], 2 * high + low, block, shard)
                    copy(across.at[step, begin + block], 2 * high + 1 - low, block, shard)
                    copy(far.at[step, begin + block], 2 * (1 - high) + low, block, shard)
                    copy(corner.at[step, begin + block], 2 * (1 - high) + 1 - low, block, shard)
        for out_ref in out_refs:
            pltpu.make_async_copy(out_ref, out_ref, sem).wait()

    return run(
        kernel,
        "assemble_" + kind,
        where,
        pieces,
        [pl.BlockSpec(memory_space=pl.ANY)] * 4,
        [(shape, low_type) for shape in shapes],
        [pl.BlockSpec(memory_space=pltpu.VMEM) for _ in shapes],
        scratch=[pltpu.SemaphoreType.DMA],
        after=after,
    )


def norm_columns(near, other, norm_params, where, after=()):
    count, width = norm_params.shape

    def kernel(where, own_ref, near_ref, other_ref, out_ref):
        for shard in range(8):
            side = (shard % 2) ^ where[1]
            chip = (shard // 2) ^ where[0]
            here = near_ref[jnp.maximum(chip, 1) - 1, :count, :width].astype(wide_type)
            here = jnp.where(chip == 0, own_ref[...].astype(low_type).astype(wide_type), here)
            there = other_ref[chip, :count, :width].astype(wide_type)
            out_ref[:, shard * width : (shard + 1) * width] = jnp.where(side == 0, here, there)

    args = (norm_params, near, other)
    outs = [((count, 8 * width), wide_type)]
    specs = [full(outs[0][0])]
    return run(kernel, "norm_columns", where, args, fulls(args), outs, specs, after=after)


def turn(step, where):
    first, second = where[2], where[3]
    return 2 * (first ^ (1 - step // 2)) + (second ^ (1 - step % 2))


def fill_left(left, values, values_other):
    tokens = values.shape[0]
    left[:, :tokens] = values.T
    left[:, tokens:] = values_other.T


def chip_dot(left, right, right_other):
    tokens = right.shape[0]
    return dot(left[:, :tokens], right) + dot(left[:, tokens:], right_other)


def store_rows(out_ref, product, z, rows):
    for chip in range(4):
        piece = product[chip * 2 * rows : (chip + 1) * 2 * rows]
        out_ref[0, chip ^ z, 0] = piece.reshape(2, rows, HALF).astype(low_type)


def trio_part(tokens, part):
    return pl.BlockSpec((1, tokens, D), lambda step, where: (part, 0, 0))


def grad_attend(trio, trio_other, qkv, qkv_other, out, feed_other, filled, where, after=()):
    tokens = out.shape[0]
    rows = D // 8

    def kernel(where, a, a2, o, o2, g, g2, b, b2, _, __, sent, kept, left_a, left_o):
        step = pl.program_id(0)
        quarter = turn(step, where)

        @pl.when(step == 0)
        def _():
            fill_left(left_a, a[0], a2[0])
            fill_left(left_o, o[0], o2[0])

        def put(product):
            @pl.when(step < 2)
            def _():
                store_rows(sent, product, where[0], rows)

            @pl.when(step >= 2)
            def _():
                store_rows(kept, product, where[0], rows)

        @pl.when(quarter < 3)
        def _():
            put(chip_dot(left_a, g[...], g2[...]))

        @pl.when(quarter == 3)
        def _():
            put(chip_dot(left_o, b[...], b2[...]))

    def own_column(step, where):
        return (0, 2 * jnp.minimum(turn(step, where), 2) + where[1])

    def other_column(step, where):
        return (0, jnp.minimum(turn(step, where), 2))

    shape = (2, 4, 2, 2, rows, HALF)
    block = (1, 4, 1, 2, rows, HALF)
    return run(
        kernel,
        "grad_attend",
        where,
        (trio, trio_other, trio, trio_other, qkv, qkv_other, out, feed_other, *filled),
        [
            trio_part(tokens, 0),
            trio_part(tokens, 0),
            trio_part(tokens, 1),
            trio_part(tokens, 1),
            pl.BlockSpec((tokens, HALF), own_column),
            pl.BlockSpec((tokens, HALF), other_column),
            pl.BlockSpec((tokens, HALF), lambda step, where: (0, where[1])),
            pl.BlockSpec((tokens, HALF), lambda step, where: (0, 9)),
        ]
        + [pl.BlockSpec(memory_space=pl.ANY)] * 2,
        [(shape, low_type)] * 2,
        [
            pl.BlockSpec(block, lambda step, where: (jnp.minimum(step, 1), 0, 1, 0, 0, 0)),
            pl.BlockSpec(block, lambda step, where: (jnp.maximum(step, 2) - 2, 0, 1, 0, 0, 0)),
        ],
        grid=(4,),
        scratch=[pltpu.VMEM((D, 2 * tokens), low_type)] * 2,
        after=after,
        reuse={8: 0, 9: 1},
    )


def grad_gate_up(trio, trio_other, grads, feed_other, where, after=()):
    tokens = trio.shape[1]
    rows = D // 8

    def kernel(where, a, a2, g, g2, sent, kept, left):
        step = pl.program_id(0)

        @pl.when(step == 0)
        def _():
            fill_left(left, a[0], a2[0])

        product = chip_dot(left, g[0], g2[...])

        @pl.when(step < 4)
        def _():
            store_rows(sent, product, where[0], rows)

        @pl.when(step >= 4)
        def _():
            store_rows(kept, product, where[0], rows)

    def own_column(step, where):
        return (step % 2, 0, 2 * turn(step // 2, where) + where[1])

    def other_column(step, where):
        return (0, 4 * (step % 2) + turn(step // 2, where))

    def sent_at(step, where):
        held = jnp.minimum(step, 3)
        return (held // 2, 0, held % 2, 0, 0, 0)

    def kept_at(step, where):
        held = jnp.maximum(step, 4) - 4
        return (held // 2, 0, held % 2, 0, 0, 0)

    shape = (2, 4, 2, 2, rows, HALF)
    block = (1, 4, 1, 2, rows, HALF)
    return run(
        kernel,
        "grad_gate_up",
        where,
        (trio, trio_other, grads, feed_other),
        [
            trio_part(tokens, 2),
            trio_part(tokens, 2),
            pl.BlockSpec((1, tokens, HALF), own_column),
            pl.BlockSpec((tokens, HALF), other_column),
        ],
        [(shape, low_type)] * 2,
        [pl.BlockSpec(block, sent_at), pl.BlockSpec(block, kept_at)],
        grid=(8,),
        scratch=[pltpu.VMEM((D, 2 * tokens), low_type)],
        after=after,
    )


def grad_down(inputs, inputs_other, grads, feed_other, where, after=()):
    tokens = inputs.shape[0]
    rows = FF // 32

    def kernel(where, a, a2, g, g2, sent, kept, left):
        fill_left(left, a[...], a2[...])
        product = chip_dot(left, g[...], g2[...])
        product = product.astype(low_type).reshape(2, 4, rows, HALF)
        for quarter in range(4):
            away = (quarter // 2) ^ where[2]
            spot = 1 - ((quarter % 2) ^ where[3])

            @pl.when(away == 1)
            def _():
                sent[spot, 0, 0] = product[:, quarter]

            @pl.when(away == 0)
            def _():
                kept[spot, 0, 0] = product[:, quarter]

    def chip_columns(step, where):
        return (0, step ^ where[0])

    shape = (2, 4, 2, 2, rows, HALF)
    spec = pl.BlockSpec((2, 1, 1, 2, rows, HALF), lambda step, where: (0, step, 0, 0, 0, 0))
    return run(
        kernel,
        "grad_down",
        where,
        (inputs, inputs_other, grads, feed_other),
        [
            pl.BlockSpec((tokens, FF // 4), chip_columns),
            pl.BlockSpec((tokens, FF // 4), chip_columns),
            pl.BlockSpec((tokens, HALF), lambda step, where: (0, where[1])),
            pl.BlockSpec((tokens, HALF), lambda step, where: (0, 8)),
        ],
        [(shape, low_type)] * 2,
        [spec, spec],
        grid=(4,),
        scratch=[pltpu.VMEM((FF // 4, 2 * tokens), low_type)],
        after=after,
    )


def add_halves(kept, got, where, after=()):
    def kernel(where, kept_ref, got_ref, sent_ref, left_ref):
        for spot, out_ref in ((0, sent_ref), (1, left_ref)):
            total = kept_ref[spot].astype(wide_type) + got_ref[spot].astype(wide_type)
            out_ref[...] = total.astype(low_type)

    rest = kept.shape[2:]
    spec_in = pl.BlockSpec((2, 1) + rest, lambda step, where: (0, step, 0, 0, 0, 0))
    spec_out = pl.BlockSpec((1,) + rest, lambda step, where: (step, 0, 0, 0, 0))
    outs = [(kept.shape[1:], low_type)] * 2
    return run(
        kernel,
        "add_halves",
        where,
        (kept, got),
        [spec_in] * 2,
        outs,
        [spec_out] * 2,
        grid=(4,),
        after=after,
    )


def add_chips(sums, where, after=()):
    args = [array for both in sums for array in both]
    counts = [left.shape[1] for left, _ in sums]
    rest = sums[0][0].shape[2:]

    def kernel(where, *refs):
        in_refs, out_refs = refs[: len(args)], refs[len(args) :]
        start = 0
        for index, count in enumerate(counts):
            left_ref, got_ref = in_refs[2 * index : 2 * index + 2]
            for chip, out_ref in enumerate(out_refs):
                total = left_ref[chip].astype(wide_type) + got_ref[chip].astype(wide_type)
                out_ref[start : start + count] = total.astype(low_type)
            start += count

    outs = [((sum(counts),) + rest, low_type)] * 4
    specs = [full(shape) for shape, _ in outs]
    return run(kernel, "add_chips", where, args, fulls(args), outs, specs, after=after)


def add_last(parts, where, after=()):
    count, _, rows, width = parts[0].shape

    def kernel(where, *refs):
        part_refs, (total, squares) = refs[:4], refs[4:]
        added = jnp.zeros((8, width), wide_type)
        for block in range(count):
            for core in range(2):
                value = part_refs[0][block, core].astype(wide_type)
                for part_ref in part_refs[1:]:
                    value = value + part_ref[block, core].astype(wide_type)
                low = value.astype(low_type)
                total[block, core] = low
                value = low.astype(wide_type)
                added = added + jnp.sum((value * value).reshape(rows // 8, 8, width), axis=0)
        squares[...] = added

    outs = [(parts[0].shape, low_type), ((8, width), wide_type)]
    specs = [full(shape) for shape, _ in outs]
    return run(kernel, "add_last", where, parts, fulls(parts), outs, specs, after=after)


def pack_replicas(row, far, where, after=()):
    def kernel(where, row, far, out, token, sem):
        copies = [
            pltpu.make_async_copy(row, out.at[pl.ds(0, 2)], sem.at[0]),
            pltpu.make_async_copy(far, out.at[pl.ds(2, 2)], sem.at[1]),
        ]
        for copy in copies:
            copy.start()
        for copy in copies:
            copy.wait()

    shape = (4,) + row.shape[1:]
    return run(
        kernel,
        "pack_replicas",
        where,
        (row, far),
        [pl.BlockSpec(memory_space=pl.ANY)] * 2,
        [(shape, low_type), ((8, 128), low_type)],
        [full(shape), full((8, 128))],
        scratch=[pltpu.SemaphoreType.DMA((2,))],
        after=after,
    )


def adam_step(weight, first_moment, second_moment, gradient, factor, step_rate, decay_rate):
    gradient = gradient * factor
    first_moment = beta_first * first_moment + (1.0 - beta_first) * gradient
    second_moment = beta_second * second_moment + (1.0 - beta_second) * gradient * gradient
    first_hat = first_moment / (1.0 - beta_first**STEP)
    second_hat = second_moment / (1.0 - beta_second**STEP)
    weight = weight - step_rate * (
        first_hat / (jnp.sqrt(second_hat) + adam_eps) + decay_rate * weight
    )
    return (weight, first_moment, second_moment)


def adam_blocks(weight, first_moment, second_moment, layers, factor, kind, where):
    layer_count, rows_all, width = weight.shape
    rows = layers[0][0][0].shape[-2]
    blocks = (rows_all // rows) * (width // D)
    by_rows = rows_all // rows
    pieces = [piece for layer, _ in layers for piece in layer]

    def kernel(where, factor_ref, w, m, v, *refs):
        piece_refs, outs = refs[: len(pieces)], refs[len(pieces) :]
        layer = pl.program_id(0)
        block = pl.program_id(1)
        c, first, second = where[1], where[2], where[3]
        if kind == "gate_up":
            quarter, index = block % 4, block // 4
        elif kind == "out":
            quarter, index = 3, 0
        else:
            quarter, index = block, 0
        high, low = quarter // 2, quarter % 2
        for at in range(layer_count):
            own, swapped = piece_refs[2 * at : 2 * at + 2]
            start = layers[at][1]

            @pl.when(layer == at)
            def _():
                mine = own[2 * (first ^ high) + (second ^ low), start + index, c]
                theirs = swapped[2 * (second ^ high) + (first ^ low), start + index, c]
                mine, theirs = mine.astype(wide_type), theirs.astype(wide_type)
                for half in range(2):
                    columns = slice(half * HALF, (half + 1) * HALF)
                    results = adam_step(
                        w[0, :, columns],
                        m[0, :, columns],
                        v[0, :, columns],
                        jnp.where(c == half, mine, theirs),
                        factor_ref[0],
                        rate_matrix,
                        decay_matrix,
                    )
                    for out, result in zip(outs, results):
                        out[0, :, columns] = result

    def at(layer, block, where):
        return (layer, block, 0) if by_rows > 1 else (layer, 0, block)

    state = pl.BlockSpec((1, rows, D), at)
    return run(
        kernel,
        "adam_" + kind,
        where,
        (factor.reshape(1), weight, first_moment, second_moment, *pieces),
        [pl.BlockSpec(memory_space=pltpu.SMEM)] + [state] * 3 + fulls(pieces),
        [(weight.shape, wide_type)] * 3,
        [state] * 3,
        grid=(layer_count, blocks),
    )


def sum_all(value):
    for pairs in (FLIP_CORE, FLIP_X, FLIP_Y, Z_ONE, Z_TWO):
        value = value + send(value, pairs)
    return value


def keep_attend(results):
    names = ("trio", "qkv", "logs", "residual_one", "normed")
    return dict(zip(names, results))


def forward(hidden, weight_list, norms, where):
    kept_list = []
    for layer, weights in enumerate(weight_list):
        kept = keep_attend(attend_forward(hidden, *weights[:2], norms, layer, where))
        kept["product"], kept["slopes"] = gate_forward(kept["trio"], weights[2], where)
        kept["residual_two"], hidden = down_forward(
            kept["product"], weights[3], kept["normed"], norms, layer, where
        )
        kept_list.append(kept)
    return (hidden, kept_list)


def forward_neighbours(hidden, states, norm_params, chain):
    layer_count = states[0].shape[0]
    norm_params = norm_params.reshape(8, -1)
    rows = states[0].shape[1]
    kept_list = [None] * layer_count
    weight_list = [()] * layer_count
    groups = [(("attend", 0),)]
    for layer in range(layer_count):
        groups.append((("gate_up", layer),))
        if layer < layer_count - 1:
            groups.append((("down", layer), ("attend", layer + 1)))
    groups.append((("down", layer_count - 1),))
    owns, started, near, across, six, far, other, weights = ({} for _ in range(8))
    norms = []

    def start(at):
        more = norm_params if at == 0 else None
        *owns[at], quarters = chain(own_chunks, groups[at], states, more)
        started[at] = [send(quarters, move) for move in (Z_ONE, Z_TWO, Z_THREE)]

    def spread(at):
        near[at], rest = chain(stack_chips, started[at], rows)
        across[at] = send(near[at], FLIP_SECOND)
        if at == 0:
            count, width = norm_params.shape
            own = jnp.pad(
                norm_params.astype(low_type), ((0, NORM_ROWS - count), (0, SEQ_LEN - width))
            )
            other_rest = send(jnp.concatenate([own[None], rest]), FLIP_CORE)
            norms.extend((rest, other_rest))

    def spread_on(at):
        six[at], _ = chain(stack_two, near[at], across[at])
        far[at] = send(six[at], FLIP_FIRST)

    def swap(at):
        whole, _ = chain(pack, owns[at], six[at], far[at])
        other[at] = send(whole, FLIP_CORE)

    def lay_out(at):
        begin = 0
        if at == 0:
            norms[:] = chain(norm_columns, *norms, norm_params)
        for (kind, layer), own in zip(groups[at], owns[at]):
            weights[kind, layer] = chain(assemble, (own, six[at], far[at], other[at]), kind, begin)
            weight_list[layer] += tuple(weights[kind, layer])
            begin += BLOCKS[kind]

    def compute(at, hidden):
        for kind, layer in groups[at]:
            args = weights[kind, layer]
            if kind == "attend":
                results = chain(attend_forward, hidden, *args, norms[0], layer)
                kept_list[layer] = keep_attend(results)
                continue
            kept = kept_list[layer]
            if kind == "gate_up":
                kept["product"], kept["slopes"] = chain(gate_forward, kept["trio"], *args)
            else:
                kept["residual_two"], hidden = chain(
                    down_forward, kept["product"], *args, kept["normed"], norms[0], layer
                )
        return hidden

    last = len(groups) - 1
    start(0)
    spread(0)
    start(1)
    spread_on(0)
    for at in range(len(groups)):
        if at < last:
            spread(at + 1)
        if at + 2 <= last:
            start(at + 2)
        swap(at)
        lay_out(at)
        if at < last:
            spread_on(at + 1)
        hidden = compute(at, hidden)
    return (hidden, weight_list, kept_list, norms[0])


def gather_weights(states):
    return [
        tuple(
            lax.all_gather(weight[layer].astype(low_type), "fsdp", axis=0, tiled=True)
            for weight in states
        )
        for layer in range(states[0].shape[0])
    ]


def backward(grad, weights, kept, norms, layer, where):
    gates, _, branch, grad_one, attend, grad_mixed, grad_norms = feed_backward(
        grad, kept["residual_two"], kept["residual_one"], kept["slopes"], weights, norms, layer, where
    )
    grad_qkv, _, grad = attend_backward(
        grad_mixed, kept["qkv"], kept["logs"], grad_one, weights[0], where
    )
    gate_up = jnp.concatenate([gates[0], gates[1]], axis=1)
    factors = (
        (kept["trio"][0], grad_qkv),
        (kept["trio"][1], attend),
        (kept["trio"][2], gate_up),
        (kept["product"], branch),
    )
    return (grad, factors, grad_norms)


def backward_neighbours(grad, weight_list, kept_list, norms, chain):
    layer_count = len(weight_list)
    norm_list = [None] * layer_count
    pieces = [[None] * 4 for _ in range(layer_count)]
    squares = []
    sums = [{} for _ in range(layer_count)]

    def feed(layer, grad):
        kept = kept_list[layer]
        gates, theirs, branch, grad_one, attend, grad_mixed, norm_list[layer] = chain(
            feed_backward,
            grad,
            kept["residual_two"],
            kept["residual_one"],
            kept["slopes"],
            weight_list[layer],
            norms,
            layer,
        )
        return dict(
            gates=gates,
            feed_other=send(theirs, FLIP_CORE),
            branch=branch,
            grad_one=grad_one,
            attend=attend,
            grad_mixed=grad_mixed,
        )

    def attention(layer, made):
        kept = kept_list[layer]
        made["qkv"], theirs, grad = chain(
            attend_backward,
            made["grad_mixed"],
            kept["qkv"],
            kept["logs"],
            made["grad_one"],
            weight_list[layer][0],
        )
        made["qkv_other"] = send(theirs, FLIP_CORE)
        return grad

    def product_wide(layer, made):
        kept = kept_list[layer]
        sent, held = chain(
            grad_gate_up, kept["trio"], kept["trio_other"], made["gates"], made["feed_other"]
        )
        sums[layer]["wide"] = (held, send(sent, FLIP_FIRST))

    def product_rest(layer, made):
        kept = kept_list[layer]
        other = made["feed_other"]
        filled = chain(grad_down, kept["product"], kept["product_other"], made["branch"], other)
        qkv, qkv_other = made["qkv"], made["qkv_other"]
        trio, trio_other = kept["trio"], kept["trio_other"]
        sent, held = chain(
            grad_attend, trio, trio_other, qkv, qkv_other, made["attend"], other, filled
        )
        sums[layer]["rest"] = (held, send(sent, FLIP_FIRST))

    def halves(layer, name):
        away, left = chain(add_halves, *sums[layer][name])
        sums[layer][name] = (left, send(away, FLIP_SECOND))

    def chips(layer, names):
        own, *parts = chain(add_chips, [sums[layer][name] for name in names])
        moves = (Z_ONE, Z_TWO, Z_THREE)
        return [own] + [send(part, move) for part, move in zip(parts, moves)]

    def share(parts):
        total, part = chain(add_last, parts)
        squares.append(part)
        return (total, send(total, FLIP_SECOND))

    def share_on(found):
        row, _ = chain(stack_two, *found)
        return (row, send(row, FLIP_FIRST))

    def swap(layer, names, found):
        mine, _ = chain(pack_replicas, *found)
        found = (mine, send(mine, FLIP_CORE))
        order = {"wide": (("gate_up", (2,)),), "rest": (("down", (3,)), ("attend", (0, 1)))}
        start = 0
        for name in names:
            for kind, indices in order[name]:
                for index in indices:
                    pieces[layer][index] = (found, start)
                start += BLOCKS[kind]

    for kept in kept_list:
        for name in ("trio", "product"):
            kept[name + "_other"] = send(kept[name], FLIP_CORE)
    made = feed(layer_count - 1, grad)
    for kept in kept_list:
        chain.wait(kept["trio_other"], kept["product_other"])
    for layer in reversed(range(layer_count)):
        product_wide(layer, made)
        if layer < layer_count - 1:
            halves(layer + 1, "rest")
        grad = attention(layer, made)
        if layer > 0:
            product_rest(layer, made)
            made = feed(layer - 1, grad)
            halves(layer, "wide")
    both = ("wide", "rest")
    earlier = layer_count - 1
    parts = chips(earlier, both)
    product_rest(0, made)
    halves(0, "wide")
    found = share(parts)
    halves(0, "rest")
    parts = chips(0, ("wide",))
    found = share_on(found)
    swap(earlier, both, found)
    found = share(parts)
    parts = chips(0, ("rest",))
    found = share_on(found)
    swap(0, ("wide",), found)
    found = share(parts)
    found = share_on(found)
    swap(0, ("rest",), found)
    return (grad, norm_list, pieces, sum(squares))


def body(
    tokens_in,
    masked_flags,
    mask_embedding,
    out_cotangent,
    w_qkv,
    m_qkv,
    v_qkv,
    w_out,
    m_out,
    v_out,
    w_gu,
    m_gu,
    v_gu,
    w_down,
    m_down,
    v_down,
    norm_params,
    m_norms,
    v_norms,
):
    layer_count = w_qkv.shape[0]
    masked = masked_flags[:, None] == 1
    where = jnp.stack(place()).astype(jnp.int32)
    hidden = jnp.where(masked, mask_embedding.astype(wide_type)[None, :], tokens_in.astype(wide_type))
    grad = out_cotangent.astype(wide_type) * masked_flags[:, None].astype(wide_type)
    chain = Chain(where)
    matrices = (w_qkv, w_out, w_gu, w_down)
    if by_neighbours():
        hidden, weight_list, kept, norms = forward_neighbours(hidden, matrices, norm_params, chain)
    else:
        norms = lax.all_gather(norm_params.astype(low_type), "fsdp", axis=2, tiled=True)
        norms = norms.astype(wide_type).reshape(-1, D)
        weight_list = gather_weights(matrices)
        hidden, kept = forward(hidden, weight_list, norms, where)
    activations = hidden.astype(low_type)
    states = (
        (w_qkv, m_qkv, v_qkv),
        (w_out, m_out, v_out),
        (w_gu, m_gu, v_gu),
        (w_down, m_down, v_down),
    )
    if by_neighbours():
        grad, norm_list, pieces, squares = backward_neighbours(
            grad, weight_list, kept, norms, chain
        )
        norm_grads = jnp.concatenate(norm_list)
        rows = norm_grads.shape[0]
        packed = jnp.concatenate([norm_grads, jnp.pad(squares, ((0, 0), (0, D - HALF)))])
        packed = sum_all(packed)
        norm_grads = packed[:rows]
        total = jnp.sum(packed[rows:])
    else:
        norm_list = [None] * layer_count
        sums = [None] * layer_count
        total = wide_type(0.0)
        for layer in reversed(range(layer_count)):
            grad, factors, norm_list[layer] = backward(
                grad, weight_list[layer], kept[layer], norms, layer, where
            )
            sums[layer] = []
            for left, right in factors:
                part = dot_left(left, right)
                part = lax.psum_scatter(part, "fsdp", scatter_dimension=0, tiled=True)
                part = lax.psum(part, "rep")
                total = total + jnp.sum(part * part)
                sums[layer].append(part)
        total = lax.psum(total, "fsdp")
        norm_grads = lax.psum(jnp.concatenate(norm_list), both_axes)
    grad_norm = jnp.sqrt(total + jnp.sum(norm_grads * norm_grads))
    factor = clip_norm / jnp.maximum(grad_norm, clip_norm)
    updated = []
    for kind, state in enumerate(states):
        if by_neighbours():
            name = ("qkv", "out", "gate_up", "down")[kind]
            layers = [layer[kind] for layer in pieces]
            updated += adam_blocks(*state, layers, factor, name, where)
        else:
            gradient = jnp.stack([layer[kind] for layer in sums])
            updated += adam_step(*state, gradient, factor, rate_matrix, decay_matrix)
    width = norm_params.shape[2]
    norm_grads = norm_grads.reshape(layer_count, -1, D)
    norm_grads = lax.dynamic_slice_in_dim(norm_grads, lax.axis_index("fsdp") * width, width, 2)
    updated += adam_step(norm_params, m_norms, v_norms, norm_grads, factor, rate_norm, 0.0)
    input_grad = jnp.where(masked, 0.0, grad)
    return (activations, input_grad, grad_norm, *updated)


def solution(mesh):
    return jax.shard_map(
        body,
        mesh=mesh,
        in_specs=(
            P(("rep", "fsdp"), None),
            P(("rep", "fsdp")),
            P(),
            P(("rep", "fsdp"), None),
            P(None, "fsdp", None),
            P(None, "fsdp", None),
            P(None, "fsdp", None),
            P(None, "fsdp", None),
            P(None, "fsdp", None),
            P(None, "fsdp", None),
            P(None, "fsdp", None),
            P(None, "fsdp", None),
            P(None, "fsdp", None),
            P(None, "fsdp", None),
            P(None, "fsdp", None),
            P(None, "fsdp", None),
            P(None, None, "fsdp"),
            P(None, None, "fsdp"),
            P(None, None, "fsdp"),
        ),
        out_specs=(
            P(("rep", "fsdp"), None),
            P(("rep", "fsdp"), None),
            P(),
            P(None, "fsdp", None),
            P(None, "fsdp", None),
            P(None, "fsdp", None),
            P(None, "fsdp", None),
            P(None, "fsdp", None),
            P(None, "fsdp", None),
            P(None, "fsdp", None),
            P(None, "fsdp", None),
            P(None, "fsdp", None),
            P(None, "fsdp", None),
            P(None, "fsdp", None),
            P(None, "fsdp", None),
            P(None, None, "fsdp"),
            P(None, None, "fsdp"),
            P(None, None, "fsdp"),
        ),
        check_vma=False,
    )
```

```python
import jax
import jax.numpy as jnp
from jax import lax
from jax.experimental import pallas as pl
from jax.experimental.pallas import tpu as pltpu
from jax.sharding import PartitionSpec as P

D = 768
HEADS = 12
HEAD_DIM = 64
FF = 3072
SEQ_LEN = 128
STEP = 10
HALF = D // 2
PAIR = 2 * HEAD_DIM


beta_first = 0.9
beta_second = 0.999
adam_eps = 1e-08
clip_norm = 1.0
rate_matrix = 0.03
rate_norm = 0.5
decay_matrix = 0.01
norm_eps = 1e-05
low_type = jnp.bfloat16
wide_type = jnp.float32
both_axes = ("rep", "fsdp")


def pairs_of(move):
    found = []
    for rep in range(4):
        for shard in range(8):
            to_y, to_x, to_z, to_c = move(rep // 2, rep % 2, shard // 2, shard % 2)
            found.append((rep * 8 + shard, (to_y * 2 + to_x) * 8 + to_z * 2 + to_c))
    return found


FLIP_CORE = pairs_of(lambda y, x, z, c: (y, x, z, 1 - c))
FLIP_X = pairs_of(lambda y, x, z, c: (y, 1 - x, z, c))
FLIP_Y = pairs_of(lambda y, x, z, c: (1 - y, x, z, c))
FLIP_XY = pairs_of(lambda y, x, z, c: (1 - y, 1 - x, z, c))
FLIP_FIRST = pairs_of(lambda y, x, z, c: (y, 1 - x, z, c) if c == 0 else (1 - y, x, z, c))
FLIP_SECOND = pairs_of(lambda y, x, z, c: (1 - y, x, z, c) if c == 0 else (y, 1 - x, z, c))
Z_ONE = pairs_of(lambda y, x, z, c: (y, x, z ^ 1, c))
Z_TWO = pairs_of(lambda y, x, z, c: (y, x, z ^ 2, c))
Z_THREE = pairs_of(lambda y, x, z, c: (y, x, z ^ 3, c))


def send(values, pairs):
    return lax.ppermute(values, both_axes, pairs)


def place():
    rep = lax.axis_index("rep")
    shard = lax.axis_index("fsdp")
    y, x, z, c = rep // 2, rep % 2, shard // 2, shard % 2
    first = jnp.where(c == 0, x, y)
    second = jnp.where(c == 0, y, x)
    return (z, c, first, second)


def by_neighbours():
    return lax.axis_size("rep") == 4 and lax.axis_size("fsdp") == 8


KERNEL_TIMES = {
    "own_chunks": 1,
    "stack_chips": 1.5,
    "stack_two": 2,
    "relay": 1,
    "pack": 2.5,
    "norm_columns": 1,
    "assemble_attend": 3,
    "assemble_gate_up": 6,
    "assemble_down": 5,
    "attend_forward": 7.5,
    "gate_forward": 7,
    "down_forward": 4,
    "feed_backward": 13,
    "attend_backward": 8,
    "grad_gate_up": 9,
    "grad_down": 5,
    "grad_attend": 6,
    "add_halves": 4,
    "add_chips": 2.5,
    "add_last": 2,
    "pack_replicas": 2,
    "adam_all": 30,
}
TIME_SCALE = 10.0
VMEM_MIB = {"adam_all": 58}


def run(
    kernel, name, where, args, in_specs, outs, out_specs, grid=(1,), scratch=(), after=(), reuse=None
):
    first_out = 1 + len(args) + len(after)

    def body_of(*refs):
        kernel(*refs[: 1 + len(args)], *refs[first_out:])

    return pl.pallas_call(
        body_of,
        out_shape=[jax.ShapeDtypeStruct(shape, dtype) for shape, dtype in outs],
        grid_spec=pltpu.PrefetchScalarGridSpec(
            num_scalar_prefetch=1,
            grid=grid,
            in_specs=list(in_specs) + [pl.BlockSpec(memory_space=pl.ANY)] * len(after),
            out_specs=list(out_specs),
            scratch_shapes=list(scratch),
        ),
        input_output_aliases={1 + at: out for at, out in (reuse or {}).items()},
        compiler_params=pltpu.CompilerParams(vmem_limit_bytes=VMEM_MIB.get(name, 40) * 2**20),
        cost_estimate=pl.CostEstimate(
            flops=int(KERNEL_TIMES[name] * TIME_SCALE * 1e9), bytes_accessed=1000, transcendentals=0
        ),
        name=name,
    )(where, *args, *after)


class Chain:
    def __init__(self, where):
        self.where = where
        self.last = ()

    def __call__(self, call, *args):
        results = call(*args, self.where, self.last)
        self.last = (min(results, key=lambda array: array.size),)
        return results

    def wait(self, *arrays):
        self.last += arrays


def full(shape):
    zeros = (0,) * len(shape)
    return pl.BlockSpec(shape, lambda *_: zeros)


def fulls(arrays):
    return [full(array.shape) for array in arrays]


def dot(left, right):
    return jnp.dot(left, right, preferred_element_type=wide_type)


def dot_right(left, right):
    return lax.dot_general(
        left, right, (((1,), (1,)), ((), ())), preferred_element_type=wide_type
    )


def dot_left(left, right):
    return lax.dot_general(
        left, right, (((0,), (0,)), ((), ())), preferred_element_type=wide_type
    )


def spread_of(values):
    center = values - jnp.mean(values, axis=-1, keepdims=True)
    variance = jnp.mean(center * center, axis=-1, keepdims=True)
    scale = lax.rsqrt(variance + norm_eps)
    return (center * scale, scale)


def norm_back(grad, values, gain):
    unit, scale = spread_of(values)
    inner = grad * gain
    mean_inner = jnp.mean(inner, axis=-1, keepdims=True)
    mean_product = jnp.mean(inner * unit, axis=-1, keepdims=True)
    grad_values = scale * (inner - mean_inner - unit * mean_product)
    return (
        grad_values,
        jnp.sum(grad * unit, axis=0, keepdims=True),
        jnp.sum(grad, axis=0, keepdims=True),
    )


def put_theirs(out_ref, at, block, core):
    @pl.when(core == 0)
    def _():
        out_ref[at] = block[:, HALF:]

    @pl.when(core != 0)
    def _():
        out_ref[at] = block[:, :HALF]


def head_tools():
    lane = lax.broadcasted_iota(jnp.int32, (1, PAIR), 1)
    masks = ((lane < HEAD_DIM).astype(low_type), (lane >= HEAD_DIM).astype(low_type))
    rows = lax.broadcasted_iota(jnp.int32, (SEQ_LEN, SEQ_LEN), 0)
    columns = lax.broadcasted_iota(jnp.int32, (SEQ_LEN, SEQ_LEN), 1)
    distance = jnp.abs(rows - columns).astype(wide_type)
    return (masks, distance, columns)


def head_slope(head):
    return 2.0 ** (-8.0 * (head + 1.0) / HEADS)


def attend_forward(hidden, weight_qkv, weight_out, norms, layer, where, after=()):
    tokens = hidden.shape[0]

    def kernel(where, h, wq, wo, n, trio, qkv, log_total, residual, normed):
        low = h[...].astype(low_type)
        trio[0] = low
        for part in range(3):
            columns = slice(part * D, (part + 1) * D)
            qkv[:, columns] = dot(low, wq[:, columns]).astype(low_type)
        masks, distance, lanes = head_tools()
        for sequence in range(tokens // SEQ_LEN):
            rows = slice(sequence * SEQ_LEN, (sequence + 1) * SEQ_LEN)
            logs = jnp.zeros((SEQ_LEN, SEQ_LEN), wide_type)
            for pair in range(HEADS // 2):
                query, key, value = (
                    qkv[rows, part * D + pair * PAIR : part * D + (pair + 1) * PAIR]
                    for part in range(3)
                )
                mixture = jnp.zeros((SEQ_LEN, PAIR), wide_type)
                for side in range(2):
                    head = 2 * pair + side
                    scores = dot_right(query * masks[side], key) * HEAD_DIM ** (-0.5)
                    scores = scores - head_slope(head) * distance
                    summit = jnp.max(scores, axis=-1, keepdims=True)
                    powers = jnp.exp(scores - summit)
                    total = jnp.sum(powers, axis=-1, keepdims=True)
                    logs = jnp.where(lanes == head, summit + jnp.log(total), logs)
                    attention = (powers * (1.0 / total)).astype(low_type)
                    mixture = mixture + dot(attention, value * masks[side])
                trio[1, rows, pair * PAIR : (pair + 1) * PAIR] = mixture.astype(low_type)
            log_total[rows, :] = logs
        total = h[...] + dot(trio[1], wo[...])
        residual[...] = total
        unit, _ = spread_of(total)
        result = unit * n[4 * layer : 4 * layer + 1] + n[4 * layer + 1 : 4 * layer + 2]
        normed[...] = result
        trio[2] = result.astype(low_type)

    args = (hidden, weight_qkv, weight_out, norms)
    outs = [
        ((3, tokens, D), low_type),
        ((tokens, 3 * D), low_type),
        ((tokens, SEQ_LEN), wide_type),
        ((tokens, D), wide_type),
        ((tokens, D), wide_type),
    ]
    specs = [full(shape) for shape, _ in outs]
    return run(kernel, "attend_forward", where, args, fulls(args), outs, specs, after=after)


def gate_forward(trio, weight_gu, where, after=()):
    tokens = trio.shape[1]

    def kernel(where, a, wg, wu, product, slopes):
        gate = dot(a[0], wg[...])
        up = dot(a[0], wu[...])
        bell = 0.5 * (1.0 + lax.erf(gate * 0.5**0.5))
        curve = gate * bell
        product[...] = (curve * up).astype(low_type)
        density = jnp.exp(-0.5 * gate * gate) * 0.3989422804014327
        slopes[0] = (up * (bell + gate * density)).astype(low_type)
        slopes[1] = curve.astype(low_type)

    return run(
        kernel,
        "gate_forward",
        where,
        (trio, weight_gu, weight_gu),
        [
            pl.BlockSpec((1, tokens, D), lambda step, where: (2, 0, 0)),
            pl.BlockSpec((D, D), lambda step, where: (0, step)),
            pl.BlockSpec((D, D), lambda step, where: (0, step + FF // D)),
        ],
        [((tokens, FF), low_type), ((2, tokens, FF), low_type)],
        [
            pl.BlockSpec((tokens, D), lambda step, where: (0, step)),
            pl.BlockSpec((2, tokens, D), lambda step, where: (0, 0, step)),
        ],
        grid=(FF // D,),
        after=after,
    )


def down_forward(product, weight_down, normed, norms, layer, where, after=()):
    tokens = normed.shape[0]

    def kernel(where, x, w, h, n, residual, result):
        step = pl.program_id(0)

        @pl.when(step == 0)
        def _():
            residual[...] = h[...]

        residual[...] += dot(x[...], w[...])

        @pl.when(step == FF // D - 1)
        def _():
            unit, _ = spread_of(residual[...])
            result[...] = unit * n[4 * layer + 2 : 4 * layer + 3] + n[4 * layer + 3 : 4 * layer + 4]

    return run(
        kernel,
        "down_forward",
        where,
        (product, weight_down, normed, norms),
        [
            pl.BlockSpec((tokens, D), lambda step, where: (0, step)),
            pl.BlockSpec((D, D), lambda step, where: (step, 0)),
            full(normed.shape),
            full(norms.shape),
        ],
        [((tokens, D), wide_type)] * 2,
        [full((tokens, D))] * 2,
        grid=(FF // D,),
        after=after,
    )


def feed_backward(grad, residual_two, residual_one, slopes, weights, norms, layer, where, after=()):
    _, weight_out, weight_gu, weight_down = weights
    tokens = grad.shape[0]
    last = FF // D - 1

    def kernel(where, g, r2, r1, s, wd, wg, wu, wo, n, *refs):
        gates, theirs, branch, grad_one, attend, mixed, grad_norms, total = refs
        step = pl.program_id(0)
        core = where[1]

        def norm_row(at):
            return n[4 * layer + at : 4 * layer + at + 1]

        @pl.when(step == 0)
        def _():
            grad_two, gain, shift = norm_back(g[...], r2[...], norm_row(2))
            total[...] = grad_two
            low = grad_two.astype(low_type)
            branch[...] = low
            put_theirs(theirs, (slice(None), slice(8 * HALF, 9 * HALF)), low, core)
            grad_norms[2:3] = gain
            grad_norms[3:4] = shift

        grad_product = dot_right(branch[...], wd[...]).astype(low_type).astype(wide_type)
        for side, weight in ((0, wg), (1, wu)):
            low = (grad_product * s[side].astype(wide_type)).astype(low_type)
            gates[side] = low
            column = pl.multiple_of((4 * side + step) * HALF, HALF)
            put_theirs(theirs, (slice(None), pl.ds(column, HALF)), low, core)
            total[...] += dot_right(low, weight[...])

        @pl.when(step == last)
        def _():
            one, gain, shift = norm_back(total[...], r1[...], norm_row(0))
            grad_one[...] = one
            low = one.astype(low_type)
            attend[...] = low
            put_theirs(theirs, (slice(None), slice(9 * HALF, 10 * HALF)), low, core)
            mixed[...] = dot_right(low, wo[...]).astype(low_type)
            grad_norms[0:1] = gain
            grad_norms[1:2] = shift

    def columns(step, where):
        return (0, 0, step)

    outs = [
        ((2, tokens, FF), low_type),
        ((tokens, 10 * HALF), low_type),
        ((tokens, D), low_type),
        ((tokens, D), wide_type),
        ((tokens, D), low_type),
        ((tokens, D), low_type),
        ((4, D), wide_type),
    ]
    return run(
        kernel,
        "feed_backward",
        where,
        (
            grad,
            residual_two,
            residual_one,
            slopes,
            weight_down,
            weight_gu,
            weight_gu,
            weight_out,
            norms,
        ),
        [
            full(grad.shape),
            full(grad.shape),
            full(grad.shape),
            pl.BlockSpec((2, tokens, D), columns),
            pl.BlockSpec((D, D), lambda step, where: (step, 0)),
            pl.BlockSpec((D, D), lambda step, where: (0, step)),
            pl.BlockSpec((D, D), lambda step, where: (0, step + FF // D)),
            full(weight_out.shape),
            full(norms.shape),
        ],
        outs,
        [
            pl.BlockSpec((2, tokens, D), columns),
        ]
        + [full(shape) for shape, _ in outs[1:]],
        grid=(FF // D,),
        scratch=[pltpu.VMEM((tokens, D), wide_type)],
        after=after,
    )


def attend_backward(grad_mixed, qkv, log_total, grad_one, weight_qkv, where, after=()):
    tokens = grad_mixed.shape[0]

    def kernel(where, g, x, logs, one, wq, grads, theirs, result):
        masks, distance, lanes = head_tools()
        for sequence in range(tokens // SEQ_LEN):
            rows = slice(sequence * SEQ_LEN, (sequence + 1) * SEQ_LEN)
            all_logs = logs[rows, :]
            for pair in range(HEADS // 2):
                columns = [
                    slice(part * D + pair * PAIR, part * D + (pair + 1) * PAIR)
                    for part in range(3)
                ]
                query, key, value = (x[rows, column] for column in columns)
                grad = g[rows, columns[0]]
                sums = [jnp.zeros((SEQ_LEN, PAIR), wide_type) for _ in range(3)]
                for side in range(2):
                    head = 2 * pair + side
                    mask = masks[side]
                    scores = dot_right(query * mask, key) * HEAD_DIM ** (-0.5)
                    scores = scores - head_slope(head) * distance
                    attention = jnp.exp(scores - all_logs[:, head : head + 1])
                    grad_side = grad * mask
                    grad_attention = dot_right(grad_side, value)
                    sums[2] += dot_left(attention.astype(low_type), grad_side)
                    weighted = attention * grad_attention
                    inner = jnp.sum(weighted, axis=-1, keepdims=True)
                    grad_scores = (weighted - attention * inner).astype(low_type)
                    sums[0] += dot(grad_scores, key * mask)
                    sums[1] += dot_left(grad_scores, query * mask)
                for column, total, scale in zip(
                    columns, sums, (HEAD_DIM ** (-0.5), HEAD_DIM ** (-0.5), 1.0)
                ):
                    grads[rows, column] = (total * scale).astype(low_type)
        total = one[...]
        for part in range(3):
            block = grads[:, part * D : (part + 1) * D]
            total = total + dot_right(block, wq[:, part * D : (part + 1) * D])
            at = (slice(None), slice(part * HALF, (part + 1) * HALF))
            put_theirs(theirs, at, block, where[1])
        result[...] = total

    args = (grad_mixed, qkv, log_total, grad_one, weight_qkv)
    outs = [
        ((tokens, 3 * D), low_type),
        ((tokens, 3 * HALF), low_type),
        ((tokens, D), wide_type),
    ]
    specs = [full(shape) for shape, _ in outs]
    return run(kernel, "attend_backward", where, args, fulls(args), outs, specs, after=after)


KINDS = ("attend", "gate_up", "down")
BLOCKS = {"attend": 1, "gate_up": 2, "down": 1}


NORM_ROWS = 16


def own_chunks(chunks, weights, norm_params, where, after=()):
    rows = weights[0].shape[1]
    more = 0 if norm_params is None else NORM_ROWS
    counts = [BLOCKS[kind] for kind, _ in chunks]
    names = {"attend": (0, 1), "gate_up": (2,), "down": (3,)}
    used = [(at, layer) for kind, layer in chunks for at in names[kind]]

    def kernel(where, *refs):
        matrix = dict(zip(used, refs))
        owns, quarters = refs[len(args) : -1], refs[-1]
        start = 0
        if more:
            quarters[:, rows:] = jnp.zeros((sum(counts), more, D), low_type)
            count, width = norm_params.shape
            quarters[0, rows : rows + count, :width] = refs[len(used)][...].astype(low_type)
        for (kind, layer), own, count in zip(chunks, owns, counts):
            if kind == "attend":
                for part in range(3):
                    values = matrix[0, layer][0, :, part * D : (part + 1) * D]
                    own[part, 0] = values.astype(low_type)
                own[3, 0] = matrix[1, layer][0].astype(low_type)
            elif kind == "gate_up":
                for block in range(8):
                    values = matrix[2, layer][0, :, block * D : (block + 1) * D]
                    own[block % 4, block // 4] = values.astype(low_type)
            else:
                for block in range(4):
                    values = matrix[3, layer][0, block * rows : (block + 1) * rows, :]
                    own[block, 0] = values.astype(low_type)
            quarters[start : start + count, :rows] = own[2 * where[2] + where[3]]
            start += count

    def at_layer(layer):
        return lambda step, where: (layer, 0, 0)

    args = [weights[at] for at, _ in used]
    specs = [
        pl.BlockSpec((1,) + weights[at].shape[1:], at_layer(layer)) for at, layer in used
    ]
    if more:
        args.append(norm_params)
        specs.append(full(norm_params.shape))
    outs = [((4, count, rows, D), low_type) for count in counts]
    outs.append(((sum(counts), rows + more, D), low_type))
    out_specs = [full(shape) for shape, _ in outs]
    return run(kernel, "own_chunks", where, args, specs, outs, out_specs, after=after)


def stack_chips(arrived, rows, where, after=()):
    count = arrived[0].shape[0]
    more = arrived[0].shape[1] - rows

    def kernel(where, *refs):
        out, rest = refs[3:]
        for spot in range(3):
            out[spot] = refs[spot][:, :rows]
            if more:
                rest[spot] = refs[spot][0, rows:, :SEQ_LEN]

    shape = (3, count, rows, D)
    rest = (3, max(more, NORM_ROWS), SEQ_LEN)
    outs = [(shape, low_type), (rest, low_type)]
    specs = [full(shape), full(rest)]
    return run(kernel, "stack_chips", where, arrived, fulls(arrived), outs, specs, after=after)


def relay(values, where, after=()):
    def kernel(where, x, out, token, sem):
        copy = pltpu.make_async_copy(x, out, sem)
        copy.start()
        copy.wait()

    return run(
        kernel,
        "relay",
        where,
        (values,),
        [pl.BlockSpec(memory_space=pl.ANY)],
        [(values.shape, low_type), ((8, 128), low_type)],
        [full(values.shape), full((8, 128))],
        scratch=[pltpu.SemaphoreType.DMA],
        after=after,
    )


def stack_two(one, two, where, after=()):
    def kernel(where, one, two, out, token, sem):
        copies = [
            pltpu.make_async_copy(one, out.at[0], sem.at[0]),
            pltpu.make_async_copy(two, out.at[1], sem.at[1]),
        ]
        for copy in copies:
            copy.start()
        for copy in copies:
            copy.wait()

    shape = (2,) + one.shape
    return run(
        kernel,
        "stack_two",
        where,
        (one, two),
        [pl.BlockSpec(memory_space=pl.ANY)] * 2,
        [(shape, low_type), ((8, 128), low_type)],
        [full(shape), full((8, 128))],
        scratch=[pltpu.SemaphoreType.DMA((2,))],
        after=after,
    )


def pack(owns, six, far, where, after=()):
    counts = [own.shape[1] for own in owns]
    total, rows = sum(counts), owns[0].shape[2]
    number = len(owns) + 4

    def kernel(where, *refs):
        in_refs, (six_ref, far_ref, out, token, sem) = refs[: len(owns)], refs[len(owns) :]
        moves = []
        begin = 0
        for ref, count in zip(in_refs, counts):
            moves.append((ref, out.at[pl.ds(0, 4), pl.ds(begin, count)]))
            begin += count
        for index in range(4):
            ref = (six_ref, far_ref)[index // 2]
            moves.append((ref.at[index % 2], out.at[pl.ds(4 + 3 * index, 3)]))
        copies = [
            pltpu.make_async_copy(*move, sem.at[index]) for index, move in enumerate(moves)
        ]
        for copy in copies:
            copy.start()
        for copy in copies:
            copy.wait()

    shape = (16, total, rows, D)
    return run(
        kernel,
        "pack",
        where,
        (*owns, six, far),
        [pl.BlockSpec(memory_space=pl.ANY)] * (len(owns) + 2),
        [(shape, low_type), ((8, 128), low_type)],
        [full(shape), full((8, 128))],
        scratch=[pltpu.SemaphoreType.DMA((number,))],
        after=after,
    )


def assemble(pieces, kind, begin, where, after=()):
    count = pieces[0].shape[1]
    rows = pieces[0].shape[2]
    shapes = {
        "attend": ((8 * rows, 3 * D), (8 * rows, D)),
        "gate_up": ((8 * rows, 2 * FF),),
        "down": ((8 * 4 * rows, D),),
    }[kind]

    def kernel(where, *refs):
        own_ref, six_ref, far_ref, packed = refs[:4]
        out_refs, sem = refs[4:-1], refs[-1]
        mine = (own_ref, six_ref.at[0], six_ref.at[1], far_ref.at[0], far_ref.at[1])
        others = (packed, *(packed.at[pl.ds(at, 3)] for at in (4, 7, 10, 13)))
        z, c, first, second = (where[at] for at in range(4))

        def copy(source, quarter, block, shard):
            row = pl.multiple_of(shard * rows, rows)
            if kind == "attend":

                @pl.when(quarter < 3)
                def _():
                    column = pl.multiple_of(quarter * D, D)
                    target = out_refs[0].at[pl.ds(row, rows), pl.ds(column, D)]
                    pltpu.make_async_copy(source, target, sem).start()

                @pl.when(quarter == 3)
                def _():
                    target = out_refs[1].at[pl.ds(row, rows), :]
                    pltpu.make_async_copy(source, target, sem).start()

            elif kind == "gate_up":
                column = pl.multiple_of((quarter + 4 * block) * D, D)
                target = out_refs[0].at[pl.ds(row, rows), pl.ds(column, D)]
                pltpu.make_async_copy(source, target, sem).start()
            else:
                row = pl.multiple_of((shard * 4 + quarter) * rows, rows)
                target = out_refs[0].at[pl.ds(row, rows), :]
                pltpu.make_async_copy(source, target, sem).start()

        for side in range(2):
            own, near, across, far, corner = mine if side == 0 else others
            own_begin = 0 if side == 0 else begin
            core = c if side == 0 else 1 - c
            high, low = (first, second) if side == 0 else (second, first)
            for block in range(count):
                for quarter in range(4):
                    copy(
                        own.at[quarter, own_begin + block], jnp.int32(quarter), block, 2 * z + core
                    )
                for step in range(3):
                    shard = 2 * (z ^ (step + 1)) + core
                    copy(near.at[step, begin + block], 2 * high + low, block, shard)
                    copy(across.at[step, begin + block], 2 * high + 1 - low, block, shard)
                    copy(far.at[step, begin + block], 2 * (1 - high) + low, block, shard)
                    copy(corner.at[step, begin + block], 2 * (1 - high) + 1 - low, block, shard)
        for out_ref in out_refs:
            pltpu.make_async_copy(out_ref, out_ref, sem).wait()

    return run(
        kernel,
        "assemble_" + kind,
        where,
        pieces,
        [pl.BlockSpec(memory_space=pl.ANY)] * 4,
        [(shape, low_type) for shape in shapes],
        [pl.BlockSpec(memory_space=pltpu.VMEM) for _ in shapes],
        scratch=[pltpu.SemaphoreType.DMA],
        after=after,
    )


def norm_columns(near, other, norm_params, where, after=()):
    count, width = norm_params.shape

    def kernel(where, own_ref, near_ref, other_ref, out_ref):
        for shard in range(8):
            side = (shard % 2) ^ where[1]
            chip = (shard // 2) ^ where[0]
            here = near_ref[jnp.maximum(chip, 1) - 1, :count, :width].astype(wide_type)
            here = jnp.where(chip == 0, own_ref[...].astype(low_type).astype(wide_type), here)
            there = other_ref[chip, :count, :width].astype(wide_type)
            out_ref[:, shard * width : (shard + 1) * width] = jnp.where(side == 0, here, there)

    args = (norm_params, near, other)
    outs = [((count, 8 * width), wide_type)]
    specs = [full(outs[0][0])]
    return run(kernel, "norm_columns", where, args, fulls(args), outs, specs, after=after)


def turn(step, where):
    first, second = where[2], where[3]
    return 2 * (first ^ (1 - step // 2)) + (second ^ (1 - step % 2))


def fill_left(left, values, values_other):
    tokens = values.shape[0]
    left[:, :tokens] = values.T
    left[:, tokens:] = values_other.T


def chip_dot(left, right, right_other):
    tokens = right.shape[0]
    return dot(left[:, :tokens], right) + dot(left[:, tokens:], right_other)


def store_rows(out_ref, product, z, rows):
    for chip in range(4):
        piece = product[chip * 2 * rows : (chip + 1) * 2 * rows]
        out_ref[0, chip ^ z, 0] = piece.reshape(2, rows, HALF).astype(low_type)


def trio_part(tokens, part):
    return pl.BlockSpec((1, tokens, D), lambda step, where: (part, 0, 0))


def grad_attend(trio, trio_other, qkv, qkv_other, out, feed_other, filled, where, after=()):
    tokens = out.shape[0]
    rows = D // 8

    def kernel(where, a, a2, o, o2, g, g2, b, b2, _, __, sent, kept, left_a, left_o):
        step = pl.program_id(0)
        quarter = turn(step, where)

        @pl.when(step == 0)
        def _():
            fill_left(left_a, a[0], a2[0])
            fill_left(left_o, o[0], o2[0])

        def put(product):
            @pl.when(step < 2)
            def _():
                store_rows(sent, product, where[0], rows)

            @pl.when(step >= 2)
            def _():
                store_rows(kept, product, where[0], rows)

        @pl.when(quarter < 3)
        def _():
            put(chip_dot(left_a, g[...], g2[...]))

        @pl.when(quarter == 3)
        def _():
            put(chip_dot(left_o, b[...], b2[...]))

    def own_column(step, where):
        return (0, 2 * jnp.minimum(turn(step, where), 2) + where[1])

    def other_column(step, where):
        return (0, jnp.minimum(turn(step, where), 2))

    shape = (2, 4, 2, 2, rows, HALF)
    block = (1, 4, 1, 2, rows, HALF)
    return run(
        kernel,
        "grad_attend",
        where,
        (trio, trio_other, trio, trio_other, qkv, qkv_other, out, feed_other, *filled),
        [
            trio_part(tokens, 0),
            trio_part(tokens, 0),
            trio_part(tokens, 1),
            trio_part(tokens, 1),
            pl.BlockSpec((tokens, HALF), own_column),
            pl.BlockSpec((tokens, HALF), other_column),
            pl.BlockSpec((tokens, HALF), lambda step, where: (0, where[1])),
            pl.BlockSpec((tokens, HALF), lambda step, where: (0, 9)),
        ]
        + [pl.BlockSpec(memory_space=pl.ANY)] * 2,
        [(shape, low_type)] * 2,
        [
            pl.BlockSpec(block, lambda step, where: (jnp.minimum(step, 1), 0, 1, 0, 0, 0)),
            pl.BlockSpec(block, lambda step, where: (jnp.maximum(step, 2) - 2, 0, 1, 0, 0, 0)),
        ],
        grid=(4,),
        scratch=[pltpu.VMEM((D, 2 * tokens), low_type)] * 2,
        after=after,
        reuse={8: 0, 9: 1},
    )


def grad_gate_up(trio, trio_other, grads, feed_other, where, after=()):
    tokens = trio.shape[1]
    rows = D // 8

    def kernel(where, a, a2, g, g2, sent, kept, left):
        step = pl.program_id(0)

        @pl.when(step == 0)
        def _():
            fill_left(left, a[0], a2[0])

        product = chip_dot(left, g[0], g2[...])

        @pl.when(step < 4)
        def _():
            store_rows(sent, product, where[0], rows)

        @pl.when(step >= 4)
        def _():
            store_rows(kept, product, where[0], rows)

    def own_column(step, where):
        return (step % 2, 0, 2 * turn(step // 2, where) + where[1])

    def other_column(step, where):
        return (0, 4 * (step % 2) + turn(step // 2, where))

    def sent_at(step, where):
        held = jnp.minimum(step, 3)
        return (held // 2, 0, held % 2, 0, 0, 0)

    def kept_at(step, where):
        held = jnp.maximum(step, 4) - 4
        return (held // 2, 0, held % 2, 0, 0, 0)

    shape = (2, 4, 2, 2, rows, HALF)
    block = (1, 4, 1, 2, rows, HALF)
    return run(
        kernel,
        "grad_gate_up",
        where,
        (trio, trio_other, grads, feed_other),
        [
            trio_part(tokens, 2),
            trio_part(tokens, 2),
            pl.BlockSpec((1, tokens, HALF), own_column),
            pl.BlockSpec((tokens, HALF), other_column),
        ],
        [(shape, low_type)] * 2,
        [pl.BlockSpec(block, sent_at), pl.BlockSpec(block, kept_at)],
        grid=(8,),
        scratch=[pltpu.VMEM((D, 2 * tokens), low_type)],
        after=after,
    )


def grad_down(inputs, inputs_other, grads, feed_other, where, after=()):
    tokens = inputs.shape[0]
    rows = FF // 32

    def kernel(where, a, a2, g, g2, sent, kept, left):
        fill_left(left, a[...], a2[...])
        product = chip_dot(left, g[...], g2[...])
        product = product.astype(low_type).reshape(2, 4, rows, HALF)
        for quarter in range(4):
            away = (quarter // 2) ^ where[2]
            spot = 1 - ((quarter % 2) ^ where[3])

            @pl.when(away == 1)
            def _():
                sent[spot, 0, 0] = product[:, quarter]

            @pl.when(away == 0)
            def _():
                kept[spot, 0, 0] = product[:, quarter]

    def chip_columns(step, where):
        return (0, step ^ where[0])

    shape = (2, 4, 2, 2, rows, HALF)
    spec = pl.BlockSpec((2, 1, 1, 2, rows, HALF), lambda step, where: (0, step, 0, 0, 0, 0))
    return run(
        kernel,
        "grad_down",
        where,
        (inputs, inputs_other, grads, feed_other),
        [
            pl.BlockSpec((tokens, FF // 4), chip_columns),
            pl.BlockSpec((tokens, FF // 4), chip_columns),
            pl.BlockSpec((tokens, HALF), lambda step, where: (0, where[1])),
            pl.BlockSpec((tokens, HALF), lambda step, where: (0, 8)),
        ],
        [(shape, low_type)] * 2,
        [spec, spec],
        grid=(4,),
        scratch=[pltpu.VMEM((FF // 4, 2 * tokens), low_type)],
        after=after,
    )


def add_halves(kept, got, where, after=()):
    def kernel(where, kept_ref, got_ref, sent_ref, left_ref):
        for spot, out_ref in ((0, sent_ref), (1, left_ref)):
            total = kept_ref[spot].astype(wide_type) + got_ref[spot].astype(wide_type)
            out_ref[...] = total.astype(low_type)

    rest = kept.shape[2:]
    spec_in = pl.BlockSpec((2, 1) + rest, lambda step, where: (0, step, 0, 0, 0, 0))
    spec_out = pl.BlockSpec((1,) + rest, lambda step, where: (step, 0, 0, 0, 0))
    outs = [(kept.shape[1:], low_type)] * 2
    return run(
        kernel,
        "add_halves",
        where,
        (kept, got),
        [spec_in] * 2,
        outs,
        [spec_out] * 2,
        grid=(4,),
        after=after,
    )


def add_chips(sums, where, after=()):
    args = [array for both in sums for array in both]
    counts = [left.shape[1] for left, _ in sums]
    rest = sums[0][0].shape[2:]

    def kernel(where, *refs):
        in_refs, out_refs = refs[: len(args)], refs[len(args) :]
        start = 0
        for index, count in enumerate(counts):
            left_ref, got_ref = in_refs[2 * index : 2 * index + 2]
            for chip, out_ref in enumerate(out_refs):
                total = left_ref[chip].astype(wide_type) + got_ref[chip].astype(wide_type)
                out_ref[start : start + count] = total.astype(low_type)
            start += count

    outs = [((sum(counts),) + rest, low_type)] * 4
    specs = [full(shape) for shape, _ in outs]
    return run(kernel, "add_chips", where, args, fulls(args), outs, specs, after=after)


def add_last(parts, where, after=()):
    count, _, rows, width = parts[0].shape

    def kernel(where, *refs):
        part_refs, (total, squares) = refs[:4], refs[4:]
        added = jnp.zeros((8, width), wide_type)
        for block in range(count):
            for core in range(2):
                value = part_refs[0][block, core].astype(wide_type)
                for part_ref in part_refs[1:]:
                    value = value + part_ref[block, core].astype(wide_type)
                low = value.astype(low_type)
                total[block, core] = low
                value = low.astype(wide_type)
                added = added + jnp.sum((value * value).reshape(rows // 8, 8, width), axis=0)
        squares[...] = added

    outs = [(parts[0].shape, low_type), ((8, width), wide_type)]
    specs = [full(shape) for shape, _ in outs]
    return run(kernel, "add_last", where, parts, fulls(parts), outs, specs, after=after)


def pack_replicas(row, far, where, after=()):
    def kernel(where, row, far, out, token, sem):
        copies = [
            pltpu.make_async_copy(row, out.at[pl.ds(0, 2)], sem.at[0]),
            pltpu.make_async_copy(far, out.at[pl.ds(2, 2)], sem.at[1]),
        ]
        for copy in copies:
            copy.start()
        for copy in copies:
            copy.wait()

    shape = (4,) + row.shape[1:]
    return run(
        kernel,
        "pack_replicas",
        where,
        (row, far),
        [pl.BlockSpec(memory_space=pl.ANY)] * 2,
        [(shape, low_type), ((8, 128), low_type)],
        [full(shape), full((8, 128))],
        scratch=[pltpu.SemaphoreType.DMA((2,))],
        after=after,
    )


def adam_step(weight, first_moment, second_moment, gradient, factor, step_rate, decay_rate):
    gradient = gradient * factor
    first_moment = beta_first * first_moment + (1.0 - beta_first) * gradient
    second_moment = beta_second * second_moment + (1.0 - beta_second) * gradient * gradient
    first_hat = first_moment * (1.0 / (1.0 - beta_first**STEP))
    second_hat = second_moment * (1.0 / (1.0 - beta_second**STEP))
    weight = weight - step_rate * (
        first_hat / (jnp.sqrt(second_hat) + adam_eps) + decay_rate * weight
    )
    return (weight, first_moment, second_moment)


def adam_all(states, pieces, factor, where):
    layer_count = len(pieces)
    rows = states[0][0].shape[1]
    sizes = [state[0].shape[1] * state[0].shape[2] // (rows * D) for state in states]
    spans = []
    begin = 0
    for kind, size in enumerate(sizes):
        spans.append((kind, begin, size))
        begin += size

    def quarter_of(kind, block):
        return ((block, 0), (3, 0), (block % 4, block // 4), (block, 0))[kind]

    def kernel(where, factor_ref, *refs):
        step = pl.program_id(0)
        in_refs, piece_refs = refs[: 3 * len(states)], refs[3 * len(states) : -3 * len(states)]
        out_refs = refs[-3 * len(states) :]
        for kind, start, size in spans:

            @pl.when((step >= start) & (step < start + size))
            def _():
                w, m, v = in_refs[3 * kind : 3 * kind + 3]
                outs = out_refs[3 * kind : 3 * kind + 3]
                for layer in range(layer_count):
                    first = 2 * (kind * layer_count + layer)
                    mine, theirs = (ref[0, 0, 0] for ref in piece_refs[first : first + 2])
                    mine, theirs = mine.astype(wide_type), theirs.astype(wide_type)
                    for half in range(2):
                        columns = slice(half * HALF, (half + 1) * HALF)
                        results = adam_step(
                            w[layer, :, columns],
                            m[layer, :, columns],
                            v[layer, :, columns],
                            jnp.where(where[1] == half, mine, theirs),
                            factor_ref[0],
                            rate_matrix,
                            decay_matrix,
                        )
                        for out, result in zip(outs, results):
                            out[layer, :, columns] = result

    def state_spec(kind):
        _, first, size = spans[kind]

        def at(step, where):
            block = jnp.clip(step - first, 0, size - 1)
            return (0, block, 0) if kind == 3 else (0, 0, block)

        return pl.BlockSpec((layer_count, rows, D), at)

    def piece_spec(kind, start, size, place_at, side):
        def at(step, where):
            block = jnp.clip(step - start, 0, size - 1)
            quarter, index = quarter_of(kind, block)
            high, low = quarter // 2, quarter % 2
            first, second = where[2], where[3]
            if side == 1:
                first, second = second, first
            return (2 * (first ^ high) + (second ^ low), place_at + index, where[1], 0, 0)

        return pl.BlockSpec((1, 1, 1, rows, HALF), at)

    state_specs = [state_spec(kind) for kind in range(len(states)) for _ in range(3)]
    piece_list, piece_specs = [], []
    for kind, start, size in spans:
        for layer in range(layer_count):
            found, place_at = pieces[layer][kind]
            for side in range(2):
                piece_list.append(found[side])
                piece_specs.append(piece_spec(kind, start, size, place_at, side))
    return run(
        kernel,
        "adam_all",
        where,
        (factor.reshape(1), *(array for state in states for array in state), *piece_list),
        [pl.BlockSpec(memory_space=pltpu.SMEM)] + state_specs + piece_specs,
        [(array.shape, wide_type) for state in states for array in state],
        state_specs,
        grid=(begin,),
    )


def sum_all(value):
    value = value + send(value, FLIP_CORE)
    for one, two, three in ((FLIP_X, FLIP_Y, FLIP_XY), (Z_ONE, Z_TWO, Z_THREE)):
        value = (value + send(value, one)) + (send(value, two) + send(value, three))
    return value


def keep_attend(results):
    names = ("trio", "qkv", "logs", "residual_one", "normed")
    return dict(zip(names, results))


def forward(hidden, weight_list, norms, where):
    kept_list = []
    for layer, weights in enumerate(weight_list):
        kept = keep_attend(attend_forward(hidden, *weights[:2], norms, layer, where))
        kept["product"], kept["slopes"] = gate_forward(kept["trio"], weights[2], where)
        kept["residual_two"], hidden = down_forward(
            kept["product"], weights[3], kept["normed"], norms, layer, where
        )
        kept_list.append(kept)
    return (hidden, kept_list)


def forward_neighbours(hidden, states, norm_params, chain):
    layer_count = states[0].shape[0]
    norm_params = norm_params.reshape(8, -1)
    rows = states[0].shape[1]
    kept_list = [None] * layer_count
    weight_list = [()] * layer_count
    groups = [(("attend", 0),)]
    for layer in range(layer_count):
        groups.append((("gate_up", layer),))
        if layer < layer_count - 1:
            groups.append((("down", layer), ("attend", layer + 1)))
    groups.append((("down", layer_count - 1),))
    owns, started, near, across, six, far, other, weights = ({} for _ in range(8))
    norms = []

    def start(at):
        more = norm_params if at == 0 else None
        *owns[at], quarters = chain(own_chunks, groups[at], states, more)
        started[at] = [send(quarters, move) for move in (Z_ONE, Z_TWO, Z_THREE)]

    def spread(at):
        near[at], rest = chain(stack_chips, started[at], rows)
        across[at] = send(near[at], FLIP_SECOND)
        if at == 0:
            count, width = norm_params.shape
            own = jnp.pad(
                norm_params.astype(low_type), ((0, NORM_ROWS - count), (0, SEQ_LEN - width))
            )
            other_rest = send(jnp.concatenate([own[None], rest]), FLIP_CORE)
            norms.extend((rest, other_rest))

    def spread_on(at):
        six[at], _ = chain(stack_two, near[at], across[at])
        far[at] = send(six[at], FLIP_FIRST)

    def swap(at):
        whole, _ = chain(pack, owns[at], six[at], far[at])
        other[at] = send(whole, FLIP_CORE)

    def lay_out(at):
        begin = 0
        for (kind, layer), own in zip(groups[at], owns[at]):
            weights[kind, layer] = chain(assemble, (own, six[at], far[at], other[at]), kind, begin)
            weight_list[layer] += tuple(weights[kind, layer])
            begin += BLOCKS[kind]

    def compute(at, hidden):
        for kind, layer in groups[at]:
            args = weights[kind, layer]
            if kind == "attend":
                results = chain(attend_forward, hidden, *args, norms[0], layer)
                kept_list[layer] = keep_attend(results)
                continue
            kept = kept_list[layer]
            if kind == "gate_up":
                kept["product"], kept["slopes"] = chain(gate_forward, kept["trio"], *args)
            else:
                kept["residual_two"], hidden = chain(
                    down_forward, kept["product"], *args, kept["normed"], norms[0], layer
                )
        return hidden

    last = len(groups) - 1
    start(0)
    spread(0)
    start(1)
    norms[:] = chain(norm_columns, *norms, norm_params)
    spread_on(0)
    for at in range(len(groups)):
        if at < last:
            spread(at + 1)
        if at + 2 <= last:
            start(at + 2)
        swap(at)
        if at < last:
            spread_on(at + 1)
        lay_out(at)
        hidden = compute(at, hidden)
    return (hidden, weight_list, kept_list, norms[0])


def gather_weights(states):
    return [
        tuple(
            lax.all_gather(weight[layer].astype(low_type), "fsdp", axis=0, tiled=True)
            for weight in states
        )
        for layer in range(states[0].shape[0])
    ]


def backward(grad, weights, kept, norms, layer, where):
    gates, _, branch, grad_one, attend, grad_mixed, grad_norms = feed_backward(
        grad, kept["residual_two"], kept["residual_one"], kept["slopes"], weights, norms, layer, where
    )
    grad_qkv, _, grad = attend_backward(
        grad_mixed, kept["qkv"], kept["logs"], grad_one, weights[0], where
    )
    gate_up = jnp.concatenate([gates[0], gates[1]], axis=1)
    factors = (
        (kept["trio"][0], grad_qkv),
        (kept["trio"][1], attend),
        (kept["trio"][2], gate_up),
        (kept["product"], branch),
    )
    return (grad, factors, grad_norms)


def backward_neighbours(grad, weight_list, kept_list, norms, chain):
    layer_count = len(weight_list)
    norm_list = [None] * layer_count
    pieces = [[None] * 4 for _ in range(layer_count)]
    squares = []
    swapped = []
    sums = [{} for _ in range(layer_count)]

    def feed(layer, grad):
        kept = kept_list[layer]
        gates, theirs, branch, grad_one, attend, grad_mixed, norm_list[layer] = chain(
            feed_backward,
            grad,
            kept["residual_two"],
            kept["residual_one"],
            kept["slopes"],
            weight_list[layer],
            norms,
            layer,
        )
        return dict(
            gates=gates,
            feed_other=send(theirs, FLIP_CORE),
            branch=branch,
            grad_one=grad_one,
            attend=attend,
            grad_mixed=grad_mixed,
        )

    def attention(layer, made):
        kept = kept_list[layer]
        made["qkv"], theirs, grad = chain(
            attend_backward,
            made["grad_mixed"],
            kept["qkv"],
            kept["logs"],
            made["grad_one"],
            weight_list[layer][0],
        )
        made["qkv_other"] = send(theirs, FLIP_CORE)
        return grad

    def product_wide(layer, made):
        kept = kept_list[layer]
        sent, held = chain(
            grad_gate_up, kept["trio"], kept["trio_other"], made["gates"], made["feed_other"]
        )
        sums[layer]["wide"] = (held, send(sent, FLIP_FIRST))

    def product_rest(layer, made):
        kept = kept_list[layer]
        other = made["feed_other"]
        filled = chain(grad_down, kept["product"], kept["product_other"], made["branch"], other)
        qkv, qkv_other = made["qkv"], made["qkv_other"]
        trio, trio_other = kept["trio"], kept["trio_other"]
        sent, held = chain(
            grad_attend, trio, trio_other, qkv, qkv_other, made["attend"], other, filled
        )
        sums[layer]["rest"] = (held, send(sent, FLIP_FIRST))

    def halves(layer, name):
        away, left = chain(add_halves, *sums[layer][name])
        sums[layer][name] = (left, send(away, FLIP_SECOND))

    def chips(layer, name):
        own, *parts = chain(add_chips, [sums[layer][name]])
        moves = (Z_ONE, Z_TWO, Z_THREE)
        return [own] + [send(part, move) for part, move in zip(parts, moves)]

    def total(parts):
        whole, part = chain(add_last, parts)
        squares.append(part)
        return whole

    def share(whole):
        ready, _ = chain(relay, whole)
        return (whole, send(ready, FLIP_SECOND))

    def share_on(found):
        row, _ = chain(stack_two, *found)
        return (row, send(row, FLIP_FIRST))

    def swap(layer, name, found):
        mine, _ = chain(pack_replicas, *found)
        found = (mine, send(mine, FLIP_CORE))
        swapped.append(found[1])
        for kind, at in ((2, 0),) if name == "wide" else ((3, 0), (0, 1), (1, 1)):
            pieces[layer][kind] = (found, at)

    for kept in kept_list:
        for name in ("trio", "product"):
            kept[name + "_other"] = send(kept[name], FLIP_CORE)
    made = feed(layer_count - 1, grad)
    for kept in kept_list:
        chain.wait(kept["trio_other"], kept["product_other"])
    def settle():
        chain.wait(*swapped)
        swapped.clear()

    layer = layer_count - 1
    grad = attention(layer, made)
    product_wide(layer, made)
    product_rest(layer, made)
    while layer > 0:
        made = feed(layer - 1, grad)
        halves(layer, "wide")
        product_wide(layer - 1, made)
        parts = chips(layer, "wide")
        halves(layer, "rest")
        wide = total(parts)
        grad = attention(layer - 1, made)
        product_rest(layer - 1, made)
        parts = chips(layer, "rest")
        halves(layer - 1, "wide")
        rest = total(parts)
        halves(layer - 1, "rest")
        layer -= 1
        parts = chips(layer, "wide")
        shared = share(wide)
        shared_rest = share(rest)
        shared = share_on(shared)
        wide = total(parts)
        parts = chips(layer, "rest")
        shared_rest = share_on(shared_rest)
        shared_wide = share(wide)
        swap(layer + 1, "wide", shared)
        swap(layer + 1, "rest", shared_rest)
        shared_wide = share_on(shared_wide)
        rest = total(parts)
        shared_rest = share(rest)
        settle()
        swap(layer, "wide", shared_wide)
        shared_rest = share_on(shared_rest)
        swap(layer, "rest", shared_rest)
    return (grad, norm_list, pieces, sum(squares))


def body(
    tokens_in,
    masked_flags,
    mask_embedding,
    out_cotangent,
    w_qkv,
    m_qkv,
    v_qkv,
    w_out,
    m_out,
    v_out,
    w_gu,
    m_gu,
    v_gu,
    w_down,
    m_down,
    v_down,
    norm_params,
    m_norms,
    v_norms,
):
    layer_count = w_qkv.shape[0]
    masked = masked_flags[:, None] == 1
    where = jnp.stack(place()).astype(jnp.int32)
    hidden = jnp.where(masked, mask_embedding.astype(wide_type)[None, :], tokens_in.astype(wide_type))
    grad = out_cotangent.astype(wide_type) * masked_flags[:, None].astype(wide_type)
    chain = Chain(where)
    matrices = (w_qkv, w_out, w_gu, w_down)
    if by_neighbours():
        hidden, weight_list, kept, norms = forward_neighbours(hidden, matrices, norm_params, chain)
    else:
        norms = lax.all_gather(norm_params.astype(low_type), "fsdp", axis=2, tiled=True)
        norms = norms.astype(wide_type).reshape(-1, D)
        weight_list = gather_weights(matrices)
        hidden, kept = forward(hidden, weight_list, norms, where)
    activations = hidden.astype(low_type)
    states = (
        (w_qkv, m_qkv, v_qkv),
        (w_out, m_out, v_out),
        (w_gu, m_gu, v_gu),
        (w_down, m_down, v_down),
    )
    if by_neighbours():
        grad, norm_list, pieces, squares = backward_neighbours(
            grad, weight_list, kept, norms, chain
        )
        norm_grads = jnp.concatenate(norm_list)
        rows = norm_grads.shape[0]
        packed = jnp.concatenate([norm_grads, jnp.pad(squares, ((0, 0), (0, D - HALF)))])
        packed = sum_all(packed)
        norm_grads = packed[:rows]
        total = jnp.sum(packed[rows:])
    else:
        norm_list = [None] * layer_count
        sums = [None] * layer_count
        total = wide_type(0.0)
        for layer in reversed(range(layer_count)):
            grad, factors, norm_list[layer] = backward(
                grad, weight_list[layer], kept[layer], norms, layer, where
            )
            sums[layer] = []
            for left, right in factors:
                part = dot_left(left, right)
                part = lax.psum_scatter(part, "fsdp", scatter_dimension=0, tiled=True)
                part = lax.psum(part, "rep")
                total = total + jnp.sum(part * part)
                sums[layer].append(part)
        total = lax.psum(total, "fsdp")
        norm_grads = lax.psum(jnp.concatenate(norm_list), both_axes)
    grad_norm = jnp.sqrt(total + jnp.sum(norm_grads * norm_grads))
    factor = clip_norm / jnp.maximum(grad_norm, clip_norm)
    if by_neighbours():
        updated = list(adam_all(states, pieces, factor, where))
    else:
        updated = []
        for kind, state in enumerate(states):
            gradient = jnp.stack([layer[kind] for layer in sums])
            updated += adam_step(*state, gradient, factor, rate_matrix, decay_matrix)
    width = norm_params.shape[2]
    norm_grads = norm_grads.reshape(layer_count, -1, D)
    norm_grads = lax.dynamic_slice_in_dim(norm_grads, lax.axis_index("fsdp") * width, width, 2)
    updated += adam_step(norm_params, m_norms, v_norms, norm_grads, factor, rate_norm, 0.0)
    input_grad = jnp.where(masked, 0.0, grad)
    return (activations, input_grad, grad_norm, *updated)


def solution(mesh):
    return jax.shard_map(
        body,
        mesh=mesh,
        in_specs=(
            P(("rep", "fsdp"), None),
            P(("rep", "fsdp")),
            P(),
            P(("rep", "fsdp"), None),
            P(None, "fsdp", None),
            P(None, "fsdp", None),
            P(None, "fsdp", None),
            P(None, "fsdp", None),
            P(None, "fsdp", None),
            P(None, "fsdp", None),
            P(None, "fsdp", None),
            P(None, "fsdp", None),
            P(None, "fsdp", None),
            P(None, "fsdp", None),
            P(None, "fsdp", None),
            P(None, "fsdp", None),
            P(None, None, "fsdp"),
            P(None, None, "fsdp"),
            P(None, None, "fsdp"),
        ),
        out_specs=(
            P(("rep", "fsdp"), None),
            P(("rep", "fsdp"), None),
            P(),
            P(None, "fsdp", None),
            P(None, "fsdp", None),
            P(None, "fsdp", None),
            P(None, "fsdp", None),
            P(None, "fsdp", None),
            P(None, "fsdp", None),
            P(None, "fsdp", None),
            P(None, "fsdp", None),
            P(None, "fsdp", None),
            P(None, "fsdp", None),
            P(None, "fsdp", None),
            P(None, "fsdp", None),
            P(None, None, "fsdp"),
            P(None, None, "fsdp"),
            P(None, None, "fsdp"),
        ),
        check_vma=False,
    )
```

```python
import jax
import jax.numpy as jnp
from jax import lax
from jax.experimental import pallas as pl
from jax.experimental.pallas import tpu as pltpu
from jax.sharding import PartitionSpec as P

D = 768
HEADS = 12
HEAD_DIM = 64
FF = 3072
SEQ_LEN = 128
STEP = 10
HALF = D // 2
PAIR = 2 * HEAD_DIM


beta_first = 0.9
beta_second = 0.999
adam_eps = 1e-08
clip_norm = 1.0
rate_matrix = 0.03
rate_norm = 0.5
decay_matrix = 0.01
norm_eps = 1e-05
low_type = jnp.bfloat16
wide_type = jnp.float32
both_axes = ("rep", "fsdp")


def pairs_of(move):
    found = []
    for rep in range(4):
        for shard in range(8):
            to_y, to_x, to_z, to_c = move(rep // 2, rep % 2, shard // 2, shard % 2)
            found.append((rep * 8 + shard, (to_y * 2 + to_x) * 8 + to_z * 2 + to_c))
    return found


FLIP_CORE = pairs_of(lambda y, x, z, c: (y, x, z, 1 - c))
FLIP_X = pairs_of(lambda y, x, z, c: (y, 1 - x, z, c))
FLIP_Y = pairs_of(lambda y, x, z, c: (1 - y, x, z, c))
FLIP_XY = pairs_of(lambda y, x, z, c: (1 - y, 1 - x, z, c))
FLIP_FIRST = pairs_of(lambda y, x, z, c: (y, 1 - x, z, c) if c == 0 else (1 - y, x, z, c))
FLIP_SECOND = pairs_of(lambda y, x, z, c: (1 - y, x, z, c) if c == 0 else (y, 1 - x, z, c))
Z_ONE = pairs_of(lambda y, x, z, c: (y, x, z ^ 1, c))
Z_TWO = pairs_of(lambda y, x, z, c: (y, x, z ^ 2, c))
Z_THREE = pairs_of(lambda y, x, z, c: (y, x, z ^ 3, c))


def send(values, pairs):
    return lax.ppermute(values, both_axes, pairs)


def place():
    rep = lax.axis_index("rep")
    shard = lax.axis_index("fsdp")
    y, x, z, c = rep // 2, rep % 2, shard // 2, shard % 2
    first = jnp.where(c == 0, x, y)
    second = jnp.where(c == 0, y, x)
    return (z, c, first, second)


def by_neighbours():
    return lax.axis_size("rep") == 4 and lax.axis_size("fsdp") == 8


KERNEL_TIMES = {
    "own_chunks": 1,
    "stack_chips": 1.5,
    "stack_two": 2,
    "relay": 1,
    "pack": 2.5,
    "norm_columns": 1,
    "assemble_attend": 3,
    "assemble_gate_up": 6,
    "assemble_down": 5,
    "attend_forward": 7.5,
    "gate_forward": 7,
    "down_forward": 4,
    "feed_backward": 13,
    "attend_backward": 8,
    "grad_gate_up": 9,
    "grad_down": 5,
    "grad_attend": 6,
    "add_halves": 4,
    "add_chips": 2.5,
    "add_last": 2,
    "pack_replicas": 2,
    "adam_all": 30,
}
TIME_SCALE = 9.0
VMEM_MIB = {"adam_all": 58, "gate_forward": 14, "feed_backward": 14, "assemble_gate_up": 14, "attend_forward": 14, "attend_backward": 14}


def run(
    kernel, name, where, args, in_specs, outs, out_specs, grid=(1,), scratch=(), after=(), reuse=None
):
    first_out = 1 + len(args) + len(after)

    def body_of(*refs):
        kernel(*refs[: 1 + len(args)], *refs[first_out:])

    return pl.pallas_call(
        body_of,
        out_shape=[jax.ShapeDtypeStruct(shape, dtype) for shape, dtype in outs],
        grid_spec=pltpu.PrefetchScalarGridSpec(
            num_scalar_prefetch=1,
            grid=grid,
            in_specs=list(in_specs) + [pl.BlockSpec(memory_space=pl.ANY)] * len(after),
            out_specs=list(out_specs),
            scratch_shapes=list(scratch),
        ),
        input_output_aliases={1 + at: out for at, out in (reuse or {}).items()},
        compiler_params=pltpu.CompilerParams(vmem_limit_bytes=VMEM_MIB.get(name, 8) * 2**20),
        cost_estimate=pl.CostEstimate(
            flops=int(KERNEL_TIMES[name] * TIME_SCALE * 1e9), bytes_accessed=1000, transcendentals=0
        ),
        name=name,
    )(where, *args, *after)


class Chain:
    def __init__(self, where):
        self.where = where
        self.last = ()

    def __call__(self, call, *args):
        results = call(*args, self.where, self.last)
        self.last = (min(results, key=lambda array: array.size),)
        return results

    def wait(self, *arrays):
        self.last += arrays


def full(shape):
    zeros = (0,) * len(shape)
    return pl.BlockSpec(shape, lambda *_: zeros)


def fulls(arrays):
    return [full(array.shape) for array in arrays]


def dot(left, right):
    return jnp.dot(left, right, preferred_element_type=wide_type)


def dot_right(left, right):
    return lax.dot_general(
        left, right, (((1,), (1,)), ((), ())), preferred_element_type=wide_type
    )


def dot_left(left, right):
    return lax.dot_general(
        left, right, (((0,), (0,)), ((), ())), preferred_element_type=wide_type
    )


def spread_of(values):
    center = values - jnp.mean(values, axis=-1, keepdims=True)
    variance = jnp.mean(center * center, axis=-1, keepdims=True)
    scale = lax.rsqrt(variance + norm_eps)
    return (center * scale, scale)


def norm_back(grad, values, gain):
    unit, scale = spread_of(values)
    inner = grad * gain
    mean_inner = jnp.mean(inner, axis=-1, keepdims=True)
    mean_product = jnp.mean(inner * unit, axis=-1, keepdims=True)
    grad_values = scale * (inner - mean_inner - unit * mean_product)
    return (
        grad_values,
        jnp.sum(grad * unit, axis=0, keepdims=True),
        jnp.sum(grad, axis=0, keepdims=True),
    )


def put_theirs(out_ref, at, block, core):
    @pl.when(core == 0)
    def _():
        out_ref[at] = block[:, HALF:]

    @pl.when(core != 0)
    def _():
        out_ref[at] = block[:, :HALF]


def head_tools():
    lane = lax.broadcasted_iota(jnp.int32, (1, PAIR), 1)
    masks = ((lane < HEAD_DIM).astype(low_type), (lane >= HEAD_DIM).astype(low_type))
    rows = lax.broadcasted_iota(jnp.int32, (SEQ_LEN, SEQ_LEN), 0)
    columns = lax.broadcasted_iota(jnp.int32, (SEQ_LEN, SEQ_LEN), 1)
    distance = jnp.abs(rows - columns).astype(wide_type)
    return (masks, distance, columns)


def head_slope(head):
    return 2.0 ** (-8.0 * (head + 1.0) / HEADS)


def attend_forward(hidden, weight_qkv, weight_out, norms, layer, where, after=()):
    tokens = hidden.shape[0]

    def kernel(where, h, wq, wo, n, trio, qkv, log_total, residual, normed):
        low = h[...].astype(low_type)
        trio[0] = low
        for part in range(3):
            columns = slice(part * D, (part + 1) * D)
            qkv[:, columns] = dot(low, wq[:, columns]).astype(low_type)
        masks, distance, lanes = head_tools()
        for sequence in range(tokens // SEQ_LEN):
            rows = slice(sequence * SEQ_LEN, (sequence + 1) * SEQ_LEN)
            logs = jnp.zeros((SEQ_LEN, SEQ_LEN), wide_type)
            for pair in range(HEADS // 2):
                query, key, value = (
                    qkv[rows, part * D + pair * PAIR : part * D + (pair + 1) * PAIR]
                    for part in range(3)
                )
                mixture = jnp.zeros((SEQ_LEN, PAIR), wide_type)
                for side in range(2):
                    head = 2 * pair + side
                    scores = dot_right(query * masks[side], key) * HEAD_DIM ** (-0.5)
                    scores = scores - head_slope(head) * distance
                    summit = jnp.max(scores, axis=-1, keepdims=True)
                    powers = jnp.exp(scores - summit)
                    total = jnp.sum(powers, axis=-1, keepdims=True)
                    logs = jnp.where(lanes == head, summit + jnp.log(total), logs)
                    attention = (powers * (1.0 / total)).astype(low_type)
                    mixture = mixture + dot(attention, value * masks[side])
                trio[1, rows, pair * PAIR : (pair + 1) * PAIR] = mixture.astype(low_type)
            log_total[rows, :] = logs
        total = h[...] + dot(trio[1], wo[...])
        residual[...] = total
        unit, _ = spread_of(total)
        result = unit * n[4 * layer : 4 * layer + 1] + n[4 * layer + 1 : 4 * layer + 2]
        normed[...] = result
        trio[2] = result.astype(low_type)

    args = (hidden, weight_qkv, weight_out, norms)
    outs = [
        ((3, tokens, D), low_type),
        ((tokens, 3 * D), low_type),
        ((tokens, SEQ_LEN), wide_type),
        ((tokens, D), wide_type),
        ((tokens, D), wide_type),
    ]
    specs = [full(shape) for shape, _ in outs]
    return run(kernel, "attend_forward", where, args, fulls(args), outs, specs, after=after)


def gate_forward(trio, weight_gu, where, after=()):
    tokens = trio.shape[1]

    def kernel(where, a, wg, wu, product, slopes):
        gate = dot(a[0], wg[...])
        up = dot(a[0], wu[...])
        bell = 0.5 * (1.0 + lax.erf(gate * 0.5**0.5))
        curve = gate * bell
        product[...] = (curve * up).astype(low_type)
        density = jnp.exp(-0.5 * gate * gate) * 0.3989422804014327
        slopes[0] = (up * (bell + gate * density)).astype(low_type)
        slopes[1] = curve.astype(low_type)

    return run(
        kernel,
        "gate_forward",
        where,
        (trio, weight_gu, weight_gu),
        [
            pl.BlockSpec((1, tokens, D), lambda step, where: (2, 0, 0)),
            pl.BlockSpec((D, D), lambda step, where: (0, step)),
            pl.BlockSpec((D, D), lambda step, where: (0, step + FF // D)),
        ],
        [((tokens, FF), low_type), ((2, tokens, FF), low_type)],
        [
            pl.BlockSpec((tokens, D), lambda step, where: (0, step)),
            pl.BlockSpec((2, tokens, D), lambda step, where: (0, 0, step)),
        ],
        grid=(FF // D,),
        after=after,
    )


def down_forward(product, weight_down, normed, norms, layer, where, after=()):
    tokens = normed.shape[0]

    def kernel(where, x, w, h, n, residual, result):
        step = pl.program_id(0)

        @pl.when(step == 0)
        def _():
            residual[...] = h[...]

        residual[...] += dot(x[...], w[...])

        @pl.when(step == FF // D - 1)
        def _():
            unit, _ = spread_of(residual[...])
            result[...] = unit * n[4 * layer + 2 : 4 * layer + 3] + n[4 * layer + 3 : 4 * layer + 4]

    return run(
        kernel,
        "down_forward",
        where,
        (product, weight_down, normed, norms),
        [
            pl.BlockSpec((tokens, D), lambda step, where: (0, step)),
            pl.BlockSpec((D, D), lambda step, where: (step, 0)),
            full(normed.shape),
            full(norms.shape),
        ],
        [((tokens, D), wide_type)] * 2,
        [full((tokens, D))] * 2,
        grid=(FF // D,),
        after=after,
    )


def feed_backward(grad, residual_two, residual_one, slopes, weights, norms, layer, where, after=()):
    _, weight_out, weight_gu, weight_down = weights
    tokens = grad.shape[0]
    last = FF // D - 1

    def kernel(where, g, r2, r1, s, wd, wg, wu, wo, n, *refs):
        gates, theirs, branch, grad_one, attend, mixed, grad_norms, total = refs
        step = pl.program_id(0)
        core = where[1]

        def norm_row(at):
            return n[4 * layer + at : 4 * layer + at + 1]

        @pl.when(step == 0)
        def _():
            grad_two, gain, shift = norm_back(g[...], r2[...], norm_row(2))
            total[...] = grad_two
            low = grad_two.astype(low_type)
            branch[...] = low
            put_theirs(theirs, (slice(None), slice(8 * HALF, 9 * HALF)), low, core)
            grad_norms[2:3] = gain
            grad_norms[3:4] = shift

        grad_product = dot_right(branch[...], wd[...]).astype(low_type).astype(wide_type)
        for side, weight in ((0, wg), (1, wu)):
            low = (grad_product * s[side].astype(wide_type)).astype(low_type)
            gates[side] = low
            column = pl.multiple_of((4 * side + step) * HALF, HALF)
            put_theirs(theirs, (slice(None), pl.ds(column, HALF)), low, core)
            total[...] += dot_right(low, weight[...])

        @pl.when(step == last)
        def _():
            one, gain, shift = norm_back(total[...], r1[...], norm_row(0))
            grad_one[...] = one
            low = one.astype(low_type)
            attend[...] = low
            put_theirs(theirs, (slice(None), slice(9 * HALF, 10 * HALF)), low, core)
            mixed[...] = dot_right(low, wo[...]).astype(low_type)
            grad_norms[0:1] = gain
            grad_norms[1:2] = shift

    def columns(step, where):
        return (0, 0, step)

    outs = [
        ((2, tokens, FF), low_type),
        ((tokens, 10 * HALF), low_type),
        ((tokens, D), low_type),
        ((tokens, D), wide_type),
        ((tokens, D), low_type),
        ((tokens, D), low_type),
        ((4, D), wide_type),
    ]
    return run(
        kernel,
        "feed_backward",
        where,
        (
            grad,
            residual_two,
            residual_one,
            slopes,
            weight_down,
            weight_gu,
            weight_gu,
            weight_out,
            norms,
        ),
        [
            full(grad.shape),
            full(grad.shape),
            full(grad.shape),
            pl.BlockSpec((2, tokens, D), columns),
            pl.BlockSpec((D, D), lambda step, where: (step, 0)),
            pl.BlockSpec((D, D), lambda step, where: (0, step)),
            pl.BlockSpec((D, D), lambda step, where: (0, step + FF // D)),
            full(weight_out.shape),
            full(norms.shape),
        ],
        outs,
        [
            pl.BlockSpec((2, tokens, D), columns),
        ]
        + [full(shape) for shape, _ in outs[1:]],
        grid=(FF // D,),
        scratch=[pltpu.VMEM((tokens, D), wide_type)],
        after=after,
    )


def attend_backward(grad_mixed, qkv, log_total, grad_one, weight_qkv, where, after=()):
    tokens = grad_mixed.shape[0]

    def kernel(where, g, x, logs, one, wq, grads, theirs, result):
        masks, distance, lanes = head_tools()
        for sequence in range(tokens // SEQ_LEN):
            rows = slice(sequence * SEQ_LEN, (sequence + 1) * SEQ_LEN)
            all_logs = logs[rows, :]
            for pair in range(HEADS // 2):
                columns = [
                    slice(part * D + pair * PAIR, part * D + (pair + 1) * PAIR)
                    for part in range(3)
                ]
                query, key, value = (x[rows, column] for column in columns)
                grad = g[rows, columns[0]]
                sums = [jnp.zeros((SEQ_LEN, PAIR), wide_type) for _ in range(3)]
                for side in range(2):
                    head = 2 * pair + side
                    mask = masks[side]
                    scores = dot_right(query * mask, key) * HEAD_DIM ** (-0.5)
                    scores = scores - head_slope(head) * distance
                    attention = jnp.exp(scores - all_logs[:, head : head + 1])
                    grad_side = grad * mask
                    grad_attention = dot_right(grad_side, value)
                    sums[2] += dot_left(attention.astype(low_type), grad_side)
                    weighted = attention * grad_attention
                    inner = jnp.sum(weighted, axis=-1, keepdims=True)
                    grad_scores = (weighted - attention * inner).astype(low_type)
                    sums[0] += dot(grad_scores, key * mask)
                    sums[1] += dot_left(grad_scores, query * mask)
                for column, total, scale in zip(
                    columns, sums, (HEAD_DIM ** (-0.5), HEAD_DIM ** (-0.5), 1.0)
                ):
                    grads[rows, column] = (total * scale).astype(low_type)
        total = one[...]
        for part in range(3):
            block = grads[:, part * D : (part + 1) * D]
            total = total + dot_right(block, wq[:, part * D : (part + 1) * D])
            at = (slice(None), slice(part * HALF, (part + 1) * HALF))
            put_theirs(theirs, at, block, where[1])
        result[...] = total

    args = (grad_mixed, qkv, log_total, grad_one, weight_qkv)
    outs = [
        ((tokens, 3 * D), low_type),
        ((tokens, 3 * HALF), low_type),
        ((tokens, D), wide_type),
    ]
    specs = [full(shape) for shape, _ in outs]
    return run(kernel, "attend_backward", where, args, fulls(args), outs, specs, after=after)


KINDS = ("attend", "gate_up", "down")
BLOCKS = {"attend": 1, "gate_up": 2, "down": 1}


NORM_ROWS = 16


def own_chunks(chunks, weights, norm_params, where, after=()):
    rows = weights[0].shape[1]
    more = 0 if norm_params is None else NORM_ROWS
    counts = [BLOCKS[kind] for kind, _ in chunks]
    names = {"attend": (0, 1), "gate_up": (2,), "down": (3,)}
    used = [(at, layer) for kind, layer in chunks for at in names[kind]]

    def kernel(where, *refs):
        matrix = dict(zip(used, refs))
        owns, quarters = refs[len(args) : -1], refs[-1]
        start = 0
        if more:
            quarters[:, rows:] = jnp.zeros((sum(counts), more, D), low_type)
            count, width = norm_params.shape
            quarters[0, rows : rows + count, :width] = refs[len(used)][...].astype(low_type)
        for (kind, layer), own, count in zip(chunks, owns, counts):
            if kind == "attend":
                for part in range(3):
                    values = matrix[0, layer][0, :, part * D : (part + 1) * D]
                    own[part, 0] = values.astype(low_type)
                own[3, 0] = matrix[1, layer][0].astype(low_type)
            elif kind == "gate_up":
                for block in range(8):
                    values = matrix[2, layer][0, :, block * D : (block + 1) * D]
                    own[block % 4, block // 4] = values.astype(low_type)
            else:
                for block in range(4):
                    values = matrix[3, layer][0, block * rows : (block + 1) * rows, :]
                    own[block, 0] = values.astype(low_type)
            quarters[start : start + count, :rows] = own[2 * where[2] + where[3]]
            start += count

    def at_layer(layer):
        return lambda step, where: (layer, 0, 0)

    args = [weights[at] for at, _ in used]
    specs = [
        pl.BlockSpec((1,) + weights[at].shape[1:], at_layer(layer)) for at, layer in used
    ]
    if more:
        args.append(norm_params)
        specs.append(full(norm_params.shape))
    outs = [((4, count, rows, D), low_type) for count in counts]
    outs.append(((sum(counts), rows + more, D), low_type))
    out_specs = [full(shape) for shape, _ in outs]
    return run(kernel, "own_chunks", where, args, specs, outs, out_specs, after=after)


def stack_chips(arrived, rows, where, after=()):
    count = arrived[0].shape[0]
    more = arrived[0].shape[1] - rows

    def kernel(where, *refs):
        out, rest = refs[3:]
        for spot in range(3):
            out[spot] = refs[spot][:, :rows]
            if more:
                rest[spot] = refs[spot][0, rows:, :SEQ_LEN]

    shape = (3, count, rows, D)
    rest = (3, max(more, NORM_ROWS), SEQ_LEN)
    outs = [(shape, low_type), (rest, low_type)]
    specs = [full(shape), full(rest)]
    return run(kernel, "stack_chips", where, arrived, fulls(arrived), outs, specs, after=after)


def relay(values, where, after=()):
    def kernel(where, x, out, token, sem):
        copy = pltpu.make_async_copy(x, out, sem)
        copy.start()
        copy.wait()

    return run(
        kernel,
        "relay",
        where,
        (values,),
        [pl.BlockSpec(memory_space=pl.ANY)],
        [(values.shape, low_type), ((8, 128), low_type)],
        [full(values.shape), full((8, 128))],
        scratch=[pltpu.SemaphoreType.DMA],
        after=after,
    )


def stack_two(one, two, where, after=()):
    def kernel(where, one, two, out, token, sem):
        copies = [
            pltpu.make_async_copy(one, out.at[0], sem.at[0]),
            pltpu.make_async_copy(two, out.at[1], sem.at[1]),
        ]
        for copy in copies:
            copy.start()
        for copy in copies:
            copy.wait()

    shape = (2,) + one.shape
    return run(
        kernel,
        "stack_two",
        where,
        (one, two),
        [pl.BlockSpec(memory_space=pl.ANY)] * 2,
        [(shape, low_type), ((8, 128), low_type)],
        [full(shape), full((8, 128))],
        scratch=[pltpu.SemaphoreType.DMA((2,))],
        after=after,
    )


def pack(owns, six, far, where, after=()):
    counts = [own.shape[1] for own in owns]
    total, rows = sum(counts), owns[0].shape[2]
    number = len(owns) + 4

    def kernel(where, *refs):
        in_refs, (six_ref, far_ref, out, token, sem) = refs[: len(owns)], refs[len(owns) :]
        moves = []
        begin = 0
        for ref, count in zip(in_refs, counts):
            moves.append((ref, out.at[pl.ds(0, 4), pl.ds(begin, count)]))
            begin += count
        for index in range(4):
            ref = (six_ref, far_ref)[index // 2]
            moves.append((ref.at[index % 2], out.at[pl.ds(4 + 3 * index, 3)]))
        copies = [
            pltpu.make_async_copy(*move, sem.at[index]) for index, move in enumerate(moves)
        ]
        for copy in copies:
            copy.start()
        for copy in copies:
            copy.wait()

    shape = (16, total, rows, D)
    return run(
        kernel,
        "pack",
        where,
        (*owns, six, far),
        [pl.BlockSpec(memory_space=pl.ANY)] * (len(owns) + 2),
        [(shape, low_type), ((8, 128), low_type)],
        [full(shape), full((8, 128))],
        scratch=[pltpu.SemaphoreType.DMA((number,))],
        after=after,
    )


def assemble(pieces, kind, begin, where, after=()):
    count = pieces[0].shape[1]
    rows = pieces[0].shape[2]
    shapes = {
        "attend": ((8 * rows, 3 * D), (8 * rows, D)),
        "gate_up": ((8 * rows, 2 * FF),),
        "down": ((8 * 4 * rows, D),),
    }[kind]

    def kernel(where, *refs):
        own_ref, six_ref, far_ref, packed = refs[:4]
        out_refs, sem = refs[4:-1], refs[-1]
        mine = (own_ref, six_ref.at[0], six_ref.at[1], far_ref.at[0], far_ref.at[1])
        others = (packed, *(packed.at[pl.ds(at, 3)] for at in (4, 7, 10, 13)))
        z, c, first, second = (where[at] for at in range(4))

        def copy(source, quarter, block, shard):
            row = pl.multiple_of(shard * rows, rows)
            if kind == "attend":

                @pl.when(quarter < 3)
                def _():
                    column = pl.multiple_of(quarter * D, D)
                    target = out_refs[0].at[pl.ds(row, rows), pl.ds(column, D)]
                    pltpu.make_async_copy(source, target, sem).start()

                @pl.when(quarter == 3)
                def _():
                    target = out_refs[1].at[pl.ds(row, rows), :]
                    pltpu.make_async_copy(source, target, sem).start()

            elif kind == "gate_up":
                column = pl.multiple_of((quarter + 4 * block) * D, D)
                target = out_refs[0].at[pl.ds(row, rows), pl.ds(column, D)]
                pltpu.make_async_copy(source, target, sem).start()
            else:
                row = pl.multiple_of((shard * 4 + quarter) * rows, rows)
                target = out_refs[0].at[pl.ds(row, rows), :]
                pltpu.make_async_copy(source, target, sem).start()

        for side in range(2):
            own, near, across, far, corner = mine if side == 0 else others
            own_begin = 0 if side == 0 else begin
            core = c if side == 0 else 1 - c
            high, low = (first, second) if side == 0 else (second, first)
            for block in range(count):
                for quarter in range(4):
                    copy(
                        own.at[quarter, own_begin + block], jnp.int32(quarter), block, 2 * z + core
                    )
                for step in range(3):
                    shard = 2 * (z ^ (step + 1)) + core
                    copy(near.at[step, begin + block], 2 * high + low, block, shard)
                    copy(across.at[step, begin + block], 2 * high + 1 - low, block, shard)
                    copy(far.at[step, begin + block], 2 * (1 - high) + low, block, shard)
                    copy(corner.at[step, begin + block], 2 * (1 - high) + 1 - low, block, shard)
        for out_ref in out_refs:
            pltpu.make_async_copy(out_ref, out_ref, sem).wait()

    return run(
        kernel,
        "assemble_" + kind,
        where,
        pieces,
        [pl.BlockSpec(memory_space=pl.ANY)] * 4,
        [(shape, low_type) for shape in shapes],
        [pl.BlockSpec(memory_space=pltpu.VMEM) for _ in shapes],
        scratch=[pltpu.SemaphoreType.DMA],
        after=after,
    )


def norm_columns(near, other, norm_params, where, after=()):
    count, width = norm_params.shape

    def kernel(where, own_ref, near_ref, other_ref, out_ref):
        for shard in range(8):
            side = (shard % 2) ^ where[1]
            chip = (shard // 2) ^ where[0]
            here = near_ref[jnp.maximum(chip, 1) - 1, :count, :width].astype(wide_type)
            here = jnp.where(chip == 0, own_ref[...].astype(low_type).astype(wide_type), here)
            there = other_ref[chip, :count, :width].astype(wide_type)
            out_ref[:, shard * width : (shard + 1) * width] = jnp.where(side == 0, here, there)

    args = (norm_params, near, other)
    outs = [((count, 8 * width), wide_type)]
    specs = [full(outs[0][0])]
    return run(kernel, "norm_columns", where, args, fulls(args), outs, specs, after=after)


def turn(step, where):
    first, second = where[2], where[3]
    return 2 * (first ^ (1 - step // 2)) + (second ^ (1 - step % 2))


def fill_left(left, values, values_other):
    tokens = values.shape[0]
    left[:, :tokens] = values.T
    left[:, tokens:] = values_other.T


def chip_dot(left, right, right_other):
    tokens = right.shape[0]
    return dot(left[:, :tokens], right) + dot(left[:, tokens:], right_other)


def store_rows(out_ref, product, z, rows):
    for chip in range(4):
        piece = product[chip * 2 * rows : (chip + 1) * 2 * rows]
        out_ref[0, chip ^ z, 0] = piece.reshape(2, rows, HALF).astype(low_type)


def trio_part(tokens, part):
    return pl.BlockSpec((1, tokens, D), lambda step, where: (part, 0, 0))


def grad_attend(trio, trio_other, qkv, qkv_other, out, feed_other, filled, where, after=()):
    tokens = out.shape[0]
    rows = D // 8

    def kernel(where, a, a2, o, o2, g, g2, b, b2, _, __, sent, kept, left_a, left_o):
        step = pl.program_id(0)
        quarter = turn(step, where)

        @pl.when(step == 0)
        def _():
            fill_left(left_a, a[0], a2[0])
            fill_left(left_o, o[0], o2[0])

        def put(product):
            @pl.when(step < 2)
            def _():
                store_rows(sent, product, where[0], rows)

            @pl.when(step >= 2)
            def _():
                store_rows(kept, product, where[0], rows)

        @pl.when(quarter < 3)
        def _():
            put(chip_dot(left_a, g[...], g2[...]))

        @pl.when(quarter == 3)
        def _():
            put(chip_dot(left_o, b[...], b2[...]))

    def own_column(step, where):
        return (0, 2 * jnp.minimum(turn(step, where), 2) + where[1])

    def other_column(step, where):
        return (0, jnp.minimum(turn(step, where), 2))

    shape = (2, 4, 2, 2, rows, HALF)
    block = (1, 4, 1, 2, rows, HALF)
    return run(
        kernel,
        "grad_attend",
        where,
        (trio, trio_other, trio, trio_other, qkv, qkv_other, out, feed_other, *filled),
        [
            trio_part(tokens, 0),
            trio_part(tokens, 0),
            trio_part(tokens, 1),
            trio_part(tokens, 1),
            pl.BlockSpec((tokens, HALF), own_column),
            pl.BlockSpec((tokens, HALF), other_column),
            pl.BlockSpec((tokens, HALF), lambda step, where: (0, where[1])),
            pl.BlockSpec((tokens, HALF), lambda step, where: (0, 9)),
        ]
        + [pl.BlockSpec(memory_space=pl.ANY)] * 2,
        [(shape, low_type)] * 2,
        [
            pl.BlockSpec(block, lambda step, where: (jnp.minimum(step, 1), 0, 1, 0, 0, 0)),
            pl.BlockSpec(block, lambda step, where: (jnp.maximum(step, 2) - 2, 0, 1, 0, 0, 0)),
        ],
        grid=(4,),
        scratch=[pltpu.VMEM((D, 2 * tokens), low_type)] * 2,
        after=after,
        reuse={8: 0, 9: 1},
    )


def grad_gate_up(trio, trio_other, grads, feed_other, where, after=()):
    tokens = trio.shape[1]
    rows = D // 8

    def kernel(where, a, a2, g, g2, sent, kept, left):
        step = pl.program_id(0)

        @pl.when(step == 0)
        def _():
            fill_left(left, a[0], a2[0])

        product = chip_dot(left, g[0], g2[...])

        @pl.when(step < 4)
        def _():
            store_rows(sent, product, where[0], rows)

        @pl.when(step >= 4)
        def _():
            store_rows(kept, product, where[0], rows)

    def own_column(step, where):
        return (step % 2, 0, 2 * turn(step // 2, where) + where[1])

    def other_column(step, where):
        return (0, 4 * (step % 2) + turn(step // 2, where))

    def sent_at(step, where):
        held = jnp.minimum(step, 3)
        return (held // 2, 0, held % 2, 0, 0, 0)

    def kept_at(step, where):
        held = jnp.maximum(step, 4) - 4
        return (held // 2, 0, held % 2, 0, 0, 0)

    shape = (2, 4, 2, 2, rows, HALF)
    block = (1, 4, 1, 2, rows, HALF)
    return run(
        kernel,
        "grad_gate_up",
        where,
        (trio, trio_other, grads, feed_other),
        [
            trio_part(tokens, 2),
            trio_part(tokens, 2),
            pl.BlockSpec((1, tokens, HALF), own_column),
            pl.BlockSpec((tokens, HALF), other_column),
        ],
        [(shape, low_type)] * 2,
        [pl.BlockSpec(block, sent_at), pl.BlockSpec(block, kept_at)],
        grid=(8,),
        scratch=[pltpu.VMEM((D, 2 * tokens), low_type)],
        after=after,
    )


def grad_down(inputs, inputs_other, grads, feed_other, where, after=()):
    tokens = inputs.shape[0]
    rows = FF // 32

    def kernel(where, a, a2, g, g2, sent, kept, left):
        fill_left(left, a[...], a2[...])
        product = chip_dot(left, g[...], g2[...])
        product = product.astype(low_type).reshape(2, 4, rows, HALF)
        for quarter in range(4):
            away = (quarter // 2) ^ where[2]
            spot = 1 - ((quarter % 2) ^ where[3])

            @pl.when(away == 1)
            def _():
                sent[spot, 0, 0] = product[:, quarter]

            @pl.when(away == 0)
            def _():
                kept[spot, 0, 0] = product[:, quarter]

    def chip_columns(step, where):
        return (0, step ^ where[0])

    shape = (2, 4, 2, 2, rows, HALF)
    spec = pl.BlockSpec((2, 1, 1, 2, rows, HALF), lambda step, where: (0, step, 0, 0, 0, 0))
    return run(
        kernel,
        "grad_down",
        where,
        (inputs, inputs_other, grads, feed_other),
        [
            pl.BlockSpec((tokens, FF // 4), chip_columns),
            pl.BlockSpec((tokens, FF // 4), chip_columns),
            pl.BlockSpec((tokens, HALF), lambda step, where: (0, where[1])),
            pl.BlockSpec((tokens, HALF), lambda step, where: (0, 8)),
        ],
        [(shape, low_type)] * 2,
        [spec, spec],
        grid=(4,),
        scratch=[pltpu.VMEM((FF // 4, 2 * tokens), low_type)],
        after=after,
    )


def add_halves(kept, got, where, after=()):
    def kernel(where, kept_ref, got_ref, sent_ref, left_ref):
        for spot, out_ref in ((0, sent_ref), (1, left_ref)):
            total = kept_ref[spot].astype(wide_type) + got_ref[spot].astype(wide_type)
            out_ref[...] = total.astype(low_type)

    rest = kept.shape[2:]
    spec_in = pl.BlockSpec((2, 1) + rest, lambda step, where: (0, step, 0, 0, 0, 0))
    spec_out = pl.BlockSpec((1,) + rest, lambda step, where: (step, 0, 0, 0, 0))
    outs = [(kept.shape[1:], low_type)] * 2
    return run(
        kernel,
        "add_halves",
        where,
        (kept, got),
        [spec_in] * 2,
        outs,
        [spec_out] * 2,
        grid=(4,),
        after=after,
    )


def add_chips(sums, where, after=()):
    args = [array for both in sums for array in both]
    counts = [left.shape[1] for left, _ in sums]
    rest = sums[0][0].shape[2:]

    def kernel(where, *refs):
        in_refs, out_refs = refs[: len(args)], refs[len(args) :]
        start = 0
        for index, count in enumerate(counts):
            left_ref, got_ref = in_refs[2 * index : 2 * index + 2]
            for chip, out_ref in enumerate(out_refs):
                total = left_ref[chip].astype(wide_type) + got_ref[chip].astype(wide_type)
                out_ref[start : start + count] = total.astype(low_type)
            start += count

    outs = [((sum(counts),) + rest, low_type)] * 4
    specs = [full(shape) for shape, _ in outs]
    return run(kernel, "add_chips", where, args, fulls(args), outs, specs, after=after)


def add_last(parts, where, after=()):
    count, _, rows, width = parts[0].shape

    def kernel(where, *refs):
        part_refs, (total, squares) = refs[:4], refs[4:]
        added = jnp.zeros((8, width), wide_type)
        for block in range(count):
            for core in range(2):
                value = part_refs[0][block, core].astype(wide_type)
                for part_ref in part_refs[1:]:
                    value = value + part_ref[block, core].astype(wide_type)
                low = value.astype(low_type)
                total[block, core] = low
                value = low.astype(wide_type)
                added = added + jnp.sum((value * value).reshape(rows // 8, 8, width), axis=0)
        squares[...] = added

    outs = [(parts[0].shape, low_type), ((8, width), wide_type)]
    specs = [full(shape) for shape, _ in outs]
    return run(kernel, "add_last", where, parts, fulls(parts), outs, specs, after=after)


def pack_replicas(row, far, where, after=()):
    def kernel(where, row, far, out, token, sem):
        copies = [
            pltpu.make_async_copy(row, out.at[pl.ds(0, 2)], sem.at[0]),
            pltpu.make_async_copy(far, out.at[pl.ds(2, 2)], sem.at[1]),
        ]
        for copy in copies:
            copy.start()
        for copy in copies:
            copy.wait()

    shape = (4,) + row.shape[1:]
    return run(
        kernel,
        "pack_replicas",
        where,
        (row, far),
        [pl.BlockSpec(memory_space=pl.ANY)] * 2,
        [(shape, low_type), ((8, 128), low_type)],
        [full(shape), full((8, 128))],
        scratch=[pltpu.SemaphoreType.DMA((2,))],
        after=after,
    )


def adam_step(weight, first_moment, second_moment, gradient, factor, step_rate, decay_rate):
    gradient = gradient * factor
    first_moment = beta_first * first_moment + (1.0 - beta_first) * gradient
    second_moment = beta_second * second_moment + (1.0 - beta_second) * gradient * gradient
    first_hat = first_moment * (1.0 / (1.0 - beta_first**STEP))
    second_hat = second_moment * (1.0 / (1.0 - beta_second**STEP))
    weight = weight - step_rate * (
        first_hat / (jnp.sqrt(second_hat) + adam_eps) + decay_rate * weight
    )
    return (weight, first_moment, second_moment)


def adam_scaled(weight, first_moment, second_moment, gradient, factor):
    first_moment = beta_first * first_moment + ((1.0 - beta_first) * factor) * gradient
    square = gradient * gradient
    second_moment = beta_second * second_moment + ((1.0 - beta_second) * factor * factor) * square
    second_hat = second_moment * (1.0 / (1.0 - beta_second**STEP))
    root = second_hat * lax.rsqrt(second_hat) + adam_eps
    step = (rate_matrix / (1.0 - beta_first**STEP)) * first_moment
    weight = (1.0 - rate_matrix * decay_matrix) * weight - step / root
    return (weight, first_moment, second_moment)


def adam_all(states, pieces, factor, where):
    layer_count = len(pieces)
    rows = states[0][0].shape[1]
    sizes = [state[0].shape[1] * state[0].shape[2] // (rows * D) for state in states]
    spans = []
    begin = 0
    for kind, size in enumerate(sizes):
        spans.append((kind, begin, size))
        begin += size

    def quarter_of(kind, block):
        return ((block, 0), (3, 0), (block % 4, block // 4), (block, 0))[kind]

    def kernel(where, factor_ref, *refs):
        step = pl.program_id(0)
        in_refs, piece_refs = refs[: 3 * len(states)], refs[3 * len(states) : -3 * len(states)]
        out_refs = refs[-3 * len(states) :]
        for kind, start, size in spans:

            @pl.when((step >= start) & (step < start + size))
            def _():
                w, m, v = in_refs[3 * kind : 3 * kind + 3]
                outs = out_refs[3 * kind : 3 * kind + 3]
                for layer in range(layer_count):
                    first = 2 * (kind * layer_count + layer)
                    mine, theirs = (ref[0, 0, 0] for ref in piece_refs[first : first + 2])
                    mine, theirs = mine.astype(wide_type), theirs.astype(wide_type)
                    for half in range(2):
                        columns = slice(half * HALF, (half + 1) * HALF)
                        results = adam_scaled(
                            w[layer, :, columns],
                            m[layer, :, columns],
                            v[layer, :, columns],
                            jnp.where(where[1] == half, mine, theirs),
                            factor_ref[0],
                        )
                        for out, result in zip(outs, results):
                            out[layer, :, columns] = result

    def state_spec(kind):
        _, first, size = spans[kind]

        def at(step, where):
            block = jnp.clip(step - first, 0, size - 1)
            return (0, block, 0) if kind == 3 else (0, 0, block)

        return pl.BlockSpec((layer_count, rows, D), at)

    def piece_spec(kind, start, size, place_at, side):
        def at(step, where):
            block = jnp.clip(step - start, 0, size - 1)
            quarter, index = quarter_of(kind, block)
            high, low = quarter // 2, quarter % 2
            first, second = where[2], where[3]
            if side == 1:
                first, second = second, first
            return (2 * (first ^ high) + (second ^ low), place_at + index, where[1], 0, 0)

        return pl.BlockSpec((1, 1, 1, rows, HALF), at)

    state_specs = [state_spec(kind) for kind in range(len(states)) for _ in range(3)]
    piece_list, piece_specs = [], []
    for kind, start, size in spans:
        for layer in range(layer_count):
            found, place_at = pieces[layer][kind]
            for side in range(2):
                piece_list.append(found[side])
                piece_specs.append(piece_spec(kind, start, size, place_at, side))
    return run(
        kernel,
        "adam_all",
        where,
        (factor.reshape(1), *(array for state in states for array in state), *piece_list),
        [pl.BlockSpec(memory_space=pltpu.SMEM)] + state_specs + piece_specs,
        [(array.shape, wide_type) for state in states for array in state],
        state_specs,
        grid=(begin,),
    )


def sum_all(value):
    value = value + send(value, FLIP_CORE)
    for one, two, three in ((FLIP_X, FLIP_Y, FLIP_XY), (Z_ONE, Z_TWO, Z_THREE)):
        value = (value + send(value, one)) + (send(value, two) + send(value, three))
    return value


def keep_attend(results):
    names = ("trio", "qkv", "logs", "residual_one", "normed")
    return dict(zip(names, results))


def forward(hidden, weight_list, norms, where):
    kept_list = []
    for layer, weights in enumerate(weight_list):
        kept = keep_attend(attend_forward(hidden, *weights[:2], norms, layer, where))
        kept["product"], kept["slopes"] = gate_forward(kept["trio"], weights[2], where)
        kept["residual_two"], hidden = down_forward(
            kept["product"], weights[3], kept["normed"], norms, layer, where
        )
        kept_list.append(kept)
    return (hidden, kept_list)


def forward_neighbours(hidden, states, norm_params, chain):
    layer_count = states[0].shape[0]
    norm_params = norm_params.reshape(8, -1)
    rows = states[0].shape[1]
    kept_list = [None] * layer_count
    weight_list = [()] * layer_count
    groups = [(("attend", 0),)]
    for layer in range(layer_count):
        groups.append((("gate_up", layer),))
        if layer < layer_count - 1:
            groups.append((("down", layer), ("attend", layer + 1)))
    groups.append((("down", layer_count - 1),))
    owns, started, near, across, six, far, other, weights = ({} for _ in range(8))
    norms = []

    def start(at):
        more = norm_params if at == 0 else None
        *owns[at], quarters = chain(own_chunks, groups[at], states, more)
        started[at] = [send(quarters, move) for move in (Z_ONE, Z_TWO, Z_THREE)]

    def spread(at):
        near[at], rest = chain(stack_chips, started[at], rows)
        across[at] = send(near[at], FLIP_SECOND)
        if at == 0:
            count, width = norm_params.shape
            own = jnp.pad(
                norm_params.astype(low_type), ((0, NORM_ROWS - count), (0, SEQ_LEN - width))
            )
            other_rest = send(jnp.concatenate([own[None], rest]), FLIP_CORE)
            norms.extend((rest, other_rest))

    def spread_on(at):
        six[at], _ = chain(stack_two, near[at], across[at])
        far[at] = send(six[at], FLIP_FIRST)

    def swap(at):
        whole, _ = chain(pack, owns[at], six[at], far[at])
        other[at] = send(whole, FLIP_CORE)

    def lay_out(at):
        begin = 0
        for (kind, layer), own in zip(groups[at], owns[at]):
            weights[kind, layer] = chain(assemble, (own, six[at], far[at], other[at]), kind, begin)
            weight_list[layer] += tuple(weights[kind, layer])
            begin += BLOCKS[kind]

    def compute(at, hidden):
        for kind, layer in groups[at]:
            args = weights[kind, layer]
            if kind == "attend":
                results = chain(attend_forward, hidden, *args, norms[0], layer)
                kept_list[layer] = keep_attend(results)
                continue
            kept = kept_list[layer]
            if kind == "gate_up":
                kept["product"], kept["slopes"] = chain(gate_forward, kept["trio"], *args)
            else:
                kept["residual_two"], hidden = chain(
                    down_forward, kept["product"], *args, kept["normed"], norms[0], layer
                )
        return hidden

    last = len(groups) - 1
    start(0)
    spread(0)
    start(1)
    norms[:] = chain(norm_columns, *norms, norm_params)
    spread_on(0)
    for at in range(len(groups)):
        if at < last:
            spread(at + 1)
        if at + 2 <= last:
            start(at + 2)
        swap(at)
        if at < last:
            spread_on(at + 1)
        lay_out(at)
        hidden = compute(at, hidden)
    return (hidden, weight_list, kept_list, norms[0])


def gather_weights(states):
    return [
        tuple(
            lax.all_gather(weight[layer].astype(low_type), "fsdp", axis=0, tiled=True)
            for weight in states
        )
        for layer in range(states[0].shape[0])
    ]


def backward(grad, weights, kept, norms, layer, where):
    gates, _, branch, grad_one, attend, grad_mixed, grad_norms = feed_backward(
        grad, kept["residual_two"], kept["residual_one"], kept["slopes"], weights, norms, layer, where
    )
    grad_qkv, _, grad = attend_backward(
        grad_mixed, kept["qkv"], kept["logs"], grad_one, weights[0], where
    )
    gate_up = jnp.concatenate([gates[0], gates[1]], axis=1)
    factors = (
        (kept["trio"][0], grad_qkv),
        (kept["trio"][1], attend),
        (kept["trio"][2], gate_up),
        (kept["product"], branch),
    )
    return (grad, factors, grad_norms)


def backward_neighbours(grad, weight_list, kept_list, norms, chain):
    layer_count = len(weight_list)
    norm_list = [None] * layer_count
    pieces = [[None] * 4 for _ in range(layer_count)]
    squares = []
    swapped = []
    sums = [{} for _ in range(layer_count)]

    def feed(layer, grad):
        kept = kept_list[layer]
        gates, theirs, branch, grad_one, attend, grad_mixed, norm_list[layer] = chain(
            feed_backward,
            grad,
            kept["residual_two"],
            kept["residual_one"],
            kept["slopes"],
            weight_list[layer],
            norms,
            layer,
        )
        return dict(
            gates=gates,
            feed_other=send(theirs, FLIP_CORE),
            branch=branch,
            grad_one=grad_one,
            attend=attend,
            grad_mixed=grad_mixed,
        )

    def attention(layer, made):
        kept = kept_list[layer]
        made["qkv"], theirs, grad = chain(
            attend_backward,
            made["grad_mixed"],
            kept["qkv"],
            kept["logs"],
            made["grad_one"],
            weight_list[layer][0],
        )
        made["qkv_other"] = send(theirs, FLIP_CORE)
        return grad

    def product_wide(layer, made):
        kept = kept_list[layer]
        sent, held = chain(
            grad_gate_up, kept["trio"], kept["trio_other"], made["gates"], made["feed_other"]
        )
        sums[layer]["wide"] = (held, send(sent, FLIP_FIRST))

    def product_rest(layer, made):
        kept = kept_list[layer]
        other = made["feed_other"]
        filled = chain(grad_down, kept["product"], kept["product_other"], made["branch"], other)
        qkv, qkv_other = made["qkv"], made["qkv_other"]
        trio, trio_other = kept["trio"], kept["trio_other"]
        sent, held = chain(
            grad_attend, trio, trio_other, qkv, qkv_other, made["attend"], other, filled
        )
        sums[layer]["rest"] = (held, send(sent, FLIP_FIRST))

    def halves(layer, name):
        away, left = chain(add_halves, *sums[layer][name])
        sums[layer][name] = (left, send(away, FLIP_SECOND))

    def chips(layer, name):
        own, *parts = chain(add_chips, [sums[layer][name]])
        moves = (Z_ONE, Z_TWO, Z_THREE)
        return [own] + [send(part, move) for part, move in zip(parts, moves)]

    def total(parts):
        whole, part = chain(add_last, parts)
        squares.append(part)
        return whole

    def share(whole):
        ready, _ = chain(relay, whole)
        return (whole, send(ready, FLIP_SECOND))

    def share_on(found):
        row, _ = chain(stack_two, *found)
        return (row, send(row, FLIP_FIRST))

    def swap(layer, name, found):
        mine, _ = chain(pack_replicas, *found)
        found = (mine, send(mine, FLIP_CORE))
        swapped.append(found[1])
        for kind, at in ((2, 0),) if name == "wide" else ((3, 0), (0, 1), (1, 1)):
            pieces[layer][kind] = (found, at)

    for kept in kept_list:
        for name in ("trio", "product"):
            kept[name + "_other"] = send(kept[name], FLIP_CORE)
    made = feed(layer_count - 1, grad)
    for kept in kept_list:
        chain.wait(kept["trio_other"], kept["product_other"])
    def settle():
        chain.wait(*swapped)
        swapped.clear()

    layer = layer_count - 1
    grad = attention(layer, made)
    product_wide(layer, made)
    product_rest(layer, made)
    while layer > 0:
        made = feed(layer - 1, grad)
        halves(layer, "wide")
        product_wide(layer - 1, made)
        parts = chips(layer, "wide")
        halves(layer, "rest")
        wide = total(parts)
        grad = attention(layer - 1, made)
        product_rest(layer - 1, made)
        parts = chips(layer, "rest")
        halves(layer - 1, "wide")
        rest = total(parts)
        layer -= 1
        parts = chips(layer, "wide")
        halves(layer, "rest")
        shared = share(wide)
        shared_rest = share(rest)
        shared = share_on(shared)
        wide = total(parts)
        parts = chips(layer, "rest")
        shared_rest = share_on(shared_rest)
        shared_wide = share(wide)
        swap(layer + 1, "wide", shared)
        swap(layer + 1, "rest", shared_rest)
        shared_wide = share_on(shared_wide)
        rest = total(parts)
        shared_rest = share(rest)
        settle()
        swap(layer, "wide", shared_wide)
        shared_rest = share_on(shared_rest)
        swap(layer, "rest", shared_rest)
    return (grad, norm_list, pieces, sum(squares))


def body(
    tokens_in,
    masked_flags,
    mask_embedding,
    out_cotangent,
    w_qkv,
    m_qkv,
    v_qkv,
    w_out,
    m_out,
    v_out,
    w_gu,
    m_gu,
    v_gu,
    w_down,
    m_down,
    v_down,
    norm_params,
    m_norms,
    v_norms,
):
    layer_count = w_qkv.shape[0]
    masked = masked_flags[:, None] == 1
    where = jnp.stack(place()).astype(jnp.int32)
    hidden = jnp.where(masked, mask_embedding.astype(wide_type)[None, :], tokens_in.astype(wide_type))
    grad = out_cotangent.astype(wide_type) * masked_flags[:, None].astype(wide_type)
    chain = Chain(where)
    matrices = (w_qkv, w_out, w_gu, w_down)
    if by_neighbours():
        hidden, weight_list, kept, norms = forward_neighbours(hidden, matrices, norm_params, chain)
    else:
        norms = lax.all_gather(norm_params.astype(low_type), "fsdp", axis=2, tiled=True)
        norms = norms.astype(wide_type).reshape(-1, D)
        weight_list = gather_weights(matrices)
        hidden, kept = forward(hidden, weight_list, norms, where)
    activations = hidden.astype(low_type)
    states = (
        (w_qkv, m_qkv, v_qkv),
        (w_out, m_out, v_out),
        (w_gu, m_gu, v_gu),
        (w_down, m_down, v_down),
    )
    if by_neighbours():
        grad, norm_list, pieces, squares = backward_neighbours(
            grad, weight_list, kept, norms, chain
        )
        norm_grads = jnp.concatenate(norm_list)
        rows = norm_grads.shape[0]
        packed = jnp.concatenate([norm_grads, jnp.pad(squares, ((0, 0), (0, D - HALF)))])
        packed = sum_all(packed)
        norm_grads = packed[:rows]
        total = jnp.sum(packed[rows:])
    else:
        norm_list = [None] * layer_count
        sums = [None] * layer_count
        total = wide_type(0.0)
        for layer in reversed(range(layer_count)):
            grad, factors, norm_list[layer] = backward(
                grad, weight_list[layer], kept[layer], norms, layer, where
            )
            sums[layer] = []
            for left, right in factors:
                part = dot_left(left, right)
                part = lax.psum_scatter(part, "fsdp", scatter_dimension=0, tiled=True)
                part = lax.psum(part, "rep")
                total = total + jnp.sum(part * part)
                sums[layer].append(part)
        total = lax.psum(total, "fsdp")
        norm_grads = lax.psum(jnp.concatenate(norm_list), both_axes)
    grad_norm = jnp.sqrt(total + jnp.sum(norm_grads * norm_grads))
    factor = clip_norm / jnp.maximum(grad_norm, clip_norm)
    if by_neighbours():
        updated = list(adam_all(states, pieces, factor, where))
    else:
        updated = []
        for kind, state in enumerate(states):
            gradient = jnp.stack([layer[kind] for layer in sums])
            updated += adam_step(*state, gradient, factor, rate_matrix, decay_matrix)
    width = norm_params.shape[2]
    norm_grads = norm_grads.reshape(layer_count, -1, D)
    norm_grads = lax.dynamic_slice_in_dim(norm_grads, lax.axis_index("fsdp") * width, width, 2)
    updated += adam_step(norm_params, m_norms, v_norms, norm_grads, factor, rate_norm, 0.0)
    input_grad = jnp.where(masked, 0.0, grad)
    return (activations, input_grad, grad_norm, *updated)


def solution(mesh):
    return jax.shard_map(
        body,
        mesh=mesh,
        in_specs=(
            P(("rep", "fsdp"), None),
            P(("rep", "fsdp")),
            P(),
            P(("rep", "fsdp"), None),
            P(None, "fsdp", None),
            P(None, "fsdp", None),
            P(None, "fsdp", None),
            P(None, "fsdp", None),
            P(None, "fsdp", None),
            P(None, "fsdp", None),
            P(None, "fsdp", None),
            P(None, "fsdp", None),
            P(None, "fsdp", None),
            P(None, "fsdp", None),
            P(None, "fsdp", None),
            P(None, "fsdp", None),
            P(None, None, "fsdp"),
            P(None, None, "fsdp"),
            P(None, None, "fsdp"),
        ),
        out_specs=(
            P(("rep", "fsdp"), None),
            P(("rep", "fsdp"), None),
            P(),
            P(None, "fsdp", None),
            P(None, "fsdp", None),
            P(None, "fsdp", None),
            P(None, "fsdp", None),
            P(None, "fsdp", None),
            P(None, "fsdp", None),
            P(None, "fsdp", None),
            P(None, "fsdp", None),
            P(None, "fsdp", None),
            P(None, "fsdp", None),
            P(None, "fsdp", None),
            P(None, "fsdp", None),
            P(None, None, "fsdp"),
            P(None, None, "fsdp"),
            P(None, None, "fsdp"),
        ),
        check_vma=False,
    )
```

```python
import jax
import jax.numpy as jnp
from jax import lax
from jax.experimental import pallas as pl
from jax.experimental.pallas import tpu as pltpu
from jax.sharding import PartitionSpec as P

D = 768
HEADS = 12
HEAD_DIM = 64
FF = 3072
SEQ_LEN = 128
STEP = 10
HALF = D // 2
PAIR = 2 * HEAD_DIM


beta_first = 0.9
beta_second = 0.999
adam_eps = 1e-08
clip_norm = 1.0
rate_matrix = 0.03
rate_norm = 0.5
decay_matrix = 0.01
norm_eps = 1e-05
low_type = jnp.bfloat16
wide_type = jnp.float32
both_axes = ("rep", "fsdp")


def pairs_of(move):
    found = []
    for rep in range(4):
        for shard in range(8):
            to_y, to_x, to_z, to_c = move(rep // 2, rep % 2, shard // 2, shard % 2)
            found.append((rep * 8 + shard, (to_y * 2 + to_x) * 8 + to_z * 2 + to_c))
    return found


FLIP_CORE = pairs_of(lambda y, x, z, c: (y, x, z, 1 - c))
FLIP_X = pairs_of(lambda y, x, z, c: (y, 1 - x, z, c))
FLIP_Y = pairs_of(lambda y, x, z, c: (1 - y, x, z, c))
FLIP_XY = pairs_of(lambda y, x, z, c: (1 - y, 1 - x, z, c))
FLIP_FIRST = pairs_of(lambda y, x, z, c: (y, 1 - x, z, c) if c == 0 else (1 - y, x, z, c))
FLIP_SECOND = pairs_of(lambda y, x, z, c: (1 - y, x, z, c) if c == 0 else (y, 1 - x, z, c))
Z_ONE = pairs_of(lambda y, x, z, c: (y, x, z ^ 1, c))
Z_TWO = pairs_of(lambda y, x, z, c: (y, x, z ^ 2, c))
Z_THREE = pairs_of(lambda y, x, z, c: (y, x, z ^ 3, c))


def send(values, pairs):
    return lax.ppermute(values, both_axes, pairs)


def place():
    rep = lax.axis_index("rep")
    shard = lax.axis_index("fsdp")
    y, x, z, c = rep // 2, rep % 2, shard // 2, shard % 2
    first = jnp.where(c == 0, x, y)
    second = jnp.where(c == 0, y, x)
    return (z, c, first, second)


def by_neighbours():
    return lax.axis_size("rep") == 4 and lax.axis_size("fsdp") == 8


KERNEL_TIMES = {
    "own_chunks": 1,
    "stack_chips": 1.5,
    "stack_two": 2,
    "relay": 1,
    "pack": 2.5,
    "norm_columns": 1,
    "assemble_attend": 3,
    "assemble_gate_up": 6,
    "assemble_down": 5,
    "attend_forward": 7.5,
    "gate_forward": 7,
    "down_forward": 4,
    "feed_backward": 13,
    "attend_backward": 8,
    "grad_gate_up": 9,
    "grad_down": 5,
    "grad_attend": 6,
    "add_halves": 4,
    "add_chips": 2.5,
    "add_last": 2,
    "pack_replicas": 2,
    "adam_all": 30,
}
TIME_SCALE = 9.0
VMEM_MIB = {"adam_all": 58, "gate_forward": 14, "feed_backward": 14, "assemble_gate_up": 14, "attend_forward": 14, "attend_backward": 14}


def run(
    kernel, name, where, args, in_specs, outs, out_specs, grid=(1,), scratch=(), after=(), reuse=None
):
    first_out = 1 + len(args) + len(after)

    def body_of(*refs):
        kernel(*refs[: 1 + len(args)], *refs[first_out:])

    return pl.pallas_call(
        body_of,
        out_shape=[jax.ShapeDtypeStruct(shape, dtype) for shape, dtype in outs],
        grid_spec=pltpu.PrefetchScalarGridSpec(
            num_scalar_prefetch=1,
            grid=grid,
            in_specs=list(in_specs) + [pl.BlockSpec(memory_space=pl.ANY)] * len(after),
            out_specs=list(out_specs),
            scratch_shapes=list(scratch),
        ),
        input_output_aliases={1 + at: out for at, out in (reuse or {}).items()},
        compiler_params=pltpu.CompilerParams(vmem_limit_bytes=VMEM_MIB.get(name, 8) * 2**20),
        cost_estimate=pl.CostEstimate(
            flops=int(KERNEL_TIMES[name] * TIME_SCALE * 1e9), bytes_accessed=1000, transcendentals=0
        ),
        name=name,
    )(where, *args, *after)


class Chain:
    def __init__(self, where):
        self.where = where
        self.last = ()

    def __call__(self, call, *args):
        results = call(*args, self.where, self.last)
        self.last = (min(results, key=lambda array: array.size),)
        return results

    def wait(self, *arrays):
        self.last += arrays


def full(shape):
    zeros = (0,) * len(shape)
    return pl.BlockSpec(shape, lambda *_: zeros)


def fulls(arrays):
    return [full(array.shape) for array in arrays]


def dot(left, right):
    return jnp.dot(left, right, preferred_element_type=wide_type)


def dot_right(left, right):
    return lax.dot_general(
        left, right, (((1,), (1,)), ((), ())), preferred_element_type=wide_type
    )


def dot_left(left, right):
    return lax.dot_general(
        left, right, (((0,), (0,)), ((), ())), preferred_element_type=wide_type
    )


def spread_of(values):
    center = values - jnp.mean(values, axis=-1, keepdims=True)
    variance = jnp.mean(center * center, axis=-1, keepdims=True)
    scale = lax.rsqrt(variance + norm_eps)
    return (center * scale, scale)


def norm_back(grad, values, gain):
    unit, scale = spread_of(values)
    inner = grad * gain
    mean_inner = jnp.mean(inner, axis=-1, keepdims=True)
    mean_product = jnp.mean(inner * unit, axis=-1, keepdims=True)
    grad_values = scale * (inner - mean_inner - unit * mean_product)
    return (
        grad_values,
        jnp.sum(grad * unit, axis=0, keepdims=True),
        jnp.sum(grad, axis=0, keepdims=True),
    )


def put_theirs(out_ref, at, block, core):
    @pl.when(core == 0)
    def _():
        out_ref[at] = block[:, HALF:]

    @pl.when(core != 0)
    def _():
        out_ref[at] = block[:, :HALF]


def head_tools():
    lane = lax.broadcasted_iota(jnp.int32, (1, PAIR), 1)
    masks = ((lane < HEAD_DIM).astype(low_type), (lane >= HEAD_DIM).astype(low_type))
    rows = lax.broadcasted_iota(jnp.int32, (SEQ_LEN, SEQ_LEN), 0)
    columns = lax.broadcasted_iota(jnp.int32, (SEQ_LEN, SEQ_LEN), 1)
    distance = jnp.abs(rows - columns).astype(wide_type)
    return (masks, distance, columns)


def head_slope(head):
    return 2.0 ** (-8.0 * (head + 1.0) / HEADS)


def attend_forward(hidden, weight_qkv, weight_out, norms, layer, where, after=()):
    tokens = hidden.shape[0]

    def kernel(where, h, wq, wo, n, trio, qkv, log_total, residual, normed):
        low = h[...].astype(low_type)
        trio[0] = low
        for part in range(3):
            columns = slice(part * D, (part + 1) * D)
            qkv[:, columns] = dot(low, wq[:, columns]).astype(low_type)
        masks, distance, lanes = head_tools()
        for sequence in range(tokens // SEQ_LEN):
            rows = slice(sequence * SEQ_LEN, (sequence + 1) * SEQ_LEN)
            logs = jnp.zeros((SEQ_LEN, SEQ_LEN), wide_type)
            for pair in range(HEADS // 2):
                query, key, value = (
                    qkv[rows, part * D + pair * PAIR : part * D + (pair + 1) * PAIR]
                    for part in range(3)
                )
                mixture = jnp.zeros((SEQ_LEN, PAIR), wide_type)
                for side in range(2):
                    head = 2 * pair + side
                    scores = dot_right(query * masks[side], key) * HEAD_DIM ** (-0.5)
                    scores = scores - head_slope(head) * distance
                    summit = jnp.max(scores, axis=-1, keepdims=True)
                    powers = jnp.exp(scores - summit)
                    total = jnp.sum(powers, axis=-1, keepdims=True)
                    logs = jnp.where(lanes == head, summit + jnp.log(total), logs)
                    attention = (powers * (1.0 / total)).astype(low_type)
                    mixture = mixture + dot(attention, value * masks[side])
                trio[1, rows, pair * PAIR : (pair + 1) * PAIR] = mixture.astype(low_type)
            log_total[rows, :] = logs
        total = h[...] + dot(trio[1], wo[...])
        residual[...] = total
        unit, _ = spread_of(total)
        result = unit * n[4 * layer : 4 * layer + 1] + n[4 * layer + 1 : 4 * layer + 2]
        normed[...] = result
        trio[2] = result.astype(low_type)

    args = (hidden, weight_qkv, weight_out, norms)
    outs = [
        ((3, tokens, D), low_type),
        ((tokens, 3 * D), low_type),
        ((tokens, SEQ_LEN), wide_type),
        ((tokens, D), wide_type),
        ((tokens, D), wide_type),
    ]
    specs = [full(shape) for shape, _ in outs]
    return run(kernel, "attend_forward", where, args, fulls(args), outs, specs, after=after)


def gate_forward(trio, weight_gu, where, after=()):
    tokens = trio.shape[1]

    def kernel(where, a, wg, wu, product, slopes):
        gate = dot(a[0], wg[...])
        up = dot(a[0], wu[...])
        bell = 0.5 * (1.0 + lax.erf(gate * 0.5**0.5))
        curve = gate * bell
        product[...] = (curve * up).astype(low_type)
        density = jnp.exp(-0.5 * gate * gate) * 0.3989422804014327
        slopes[0] = (up * (bell + gate * density)).astype(low_type)
        slopes[1] = curve.astype(low_type)

    return run(
        kernel,
        "gate_forward",
        where,
        (trio, weight_gu, weight_gu),
        [
            pl.BlockSpec((1, tokens, D), lambda step, where: (2, 0, 0)),
            pl.BlockSpec((D, D), lambda step, where: (0, step)),
            pl.BlockSpec((D, D), lambda step, where: (0, step + FF // D)),
        ],
        [((tokens, FF), low_type), ((2, tokens, FF), low_type)],
        [
            pl.BlockSpec((tokens, D), lambda step, where: (0, step)),
            pl.BlockSpec((2, tokens, D), lambda step, where: (0, 0, step)),
        ],
        grid=(FF // D,),
        after=after,
    )


def down_forward(product, weight_down, normed, norms, layer, where, after=()):
    tokens = normed.shape[0]

    def kernel(where, x, w, h, n, residual, result):
        step = pl.program_id(0)

        @pl.when(step == 0)
        def _():
            residual[...] = h[...]

        residual[...] += dot(x[...], w[...])

        @pl.when(step == FF // D - 1)
        def _():
            unit, _ = spread_of(residual[...])
            result[...] = unit * n[4 * layer + 2 : 4 * layer + 3] + n[4 * layer + 3 : 4 * layer + 4]

    return run(
        kernel,
        "down_forward",
        where,
        (product, weight_down, normed, norms),
        [
            pl.BlockSpec((tokens, D), lambda step, where: (0, step)),
            pl.BlockSpec((D, D), lambda step, where: (step, 0)),
            full(normed.shape),
            full(norms.shape),
        ],
        [((tokens, D), wide_type)] * 2,
        [full((tokens, D))] * 2,
        grid=(FF // D,),
        after=after,
    )


def feed_backward(grad, residual_two, residual_one, slopes, weights, norms, layer, where, after=()):
    _, weight_out, weight_gu, weight_down = weights
    tokens = grad.shape[0]
    last = FF // D - 1

    def kernel(where, g, r2, r1, s, wd, wg, wu, wo, n, *refs):
        gates, theirs, branch, grad_one, attend, mixed, grad_norms, total = refs
        step = pl.program_id(0)
        core = where[1]

        def norm_row(at):
            return n[4 * layer + at : 4 * layer + at + 1]

        @pl.when(step == 0)
        def _():
            grad_two, gain, shift = norm_back(g[...], r2[...], norm_row(2))
            total[...] = grad_two
            low = grad_two.astype(low_type)
            branch[...] = low
            put_theirs(theirs, (slice(None), slice(8 * HALF, 9 * HALF)), low, core)
            grad_norms[2:3] = gain
            grad_norms[3:4] = shift

        grad_product = dot_right(branch[...], wd[...]).astype(low_type).astype(wide_type)
        for side, weight in ((0, wg), (1, wu)):
            low = (grad_product * s[side].astype(wide_type)).astype(low_type)
            gates[side] = low
            column = pl.multiple_of((4 * side + step) * HALF, HALF)
            put_theirs(theirs, (slice(None), pl.ds(column, HALF)), low, core)
            total[...] += dot_right(low, weight[...])

        @pl.when(step == last)
        def _():
            one, gain, shift = norm_back(total[...], r1[...], norm_row(0))
            grad_one[...] = one
            low = one.astype(low_type)
            attend[...] = low
            put_theirs(theirs, (slice(None), slice(9 * HALF, 10 * HALF)), low, core)
            mixed[...] = dot_right(low, wo[...]).astype(low_type)
            grad_norms[0:1] = gain
            grad_norms[1:2] = shift

    def columns(step, where):
        return (0, 0, step)

    outs = [
        ((2, tokens, FF), low_type),
        ((tokens, 10 * HALF), low_type),
        ((tokens, D), low_type),
        ((tokens, D), wide_type),
        ((tokens, D), low_type),
        ((tokens, D), low_type),
        ((4, D), wide_type),
    ]
    return run(
        kernel,
        "feed_backward",
        where,
        (
            grad,
            residual_two,
            residual_one,
            slopes,
            weight_down,
            weight_gu,
            weight_gu,
            weight_out,
            norms,
        ),
        [
            full(grad.shape),
            full(grad.shape),
            full(grad.shape),
            pl.BlockSpec((2, tokens, D), columns),
            pl.BlockSpec((D, D), lambda step, where: (step, 0)),
            pl.BlockSpec((D, D), lambda step, where: (0, step)),
            pl.BlockSpec((D, D), lambda step, where: (0, step + FF // D)),
            full(weight_out.shape),
            full(norms.shape),
        ],
        outs,
        [
            pl.BlockSpec((2, tokens, D), columns),
        ]
        + [full(shape) for shape, _ in outs[1:]],
        grid=(FF // D,),
        scratch=[pltpu.VMEM((tokens, D), wide_type)],
        after=after,
    )


def attend_backward(grad_mixed, qkv, log_total, grad_one, weight_qkv, where, after=()):
    tokens = grad_mixed.shape[0]

    def kernel(where, g, x, logs, one, wq, grads, theirs, result):
        masks, distance, lanes = head_tools()
        for sequence in range(tokens // SEQ_LEN):
            rows = slice(sequence * SEQ_LEN, (sequence + 1) * SEQ_LEN)
            all_logs = logs[rows, :]
            for pair in range(HEADS // 2):
                columns = [
                    slice(part * D + pair * PAIR, part * D + (pair + 1) * PAIR)
                    for part in range(3)
                ]
                query, key, value = (x[rows, column] for column in columns)
                grad = g[rows, columns[0]]
                sums = [jnp.zeros((SEQ_LEN, PAIR), wide_type) for _ in range(3)]
                for side in range(2):
                    head = 2 * pair + side
                    mask = masks[side]
                    scores = dot_right(query * mask, key) * HEAD_DIM ** (-0.5)
                    scores = scores - head_slope(head) * distance
                    attention = jnp.exp(scores - all_logs[:, head : head + 1])
                    grad_side = grad * mask
                    grad_attention = dot_right(grad_side, value)
                    sums[2] += dot_left(attention.astype(low_type), grad_side)
                    weighted = attention * grad_attention
                    inner = jnp.sum(weighted, axis=-1, keepdims=True)
                    grad_scores = (weighted - attention * inner).astype(low_type)
                    sums[0] += dot(grad_scores, key * mask)
                    sums[1] += dot_left(grad_scores, query * mask)
                for column, total, scale in zip(
                    columns, sums, (HEAD_DIM ** (-0.5), HEAD_DIM ** (-0.5), 1.0)
                ):
                    grads[rows, column] = (total * scale).astype(low_type)
        total = one[...]
        for part in range(3):
            block = grads[:, part * D : (part + 1) * D]
            total = total + dot_right(block, wq[:, part * D : (part + 1) * D])
            at = (slice(None), slice(part * HALF, (part + 1) * HALF))
            put_theirs(theirs, at, block, where[1])
        result[...] = total

    args = (grad_mixed, qkv, log_total, grad_one, weight_qkv)
    outs = [
        ((tokens, 3 * D), low_type),
        ((tokens, 3 * HALF), low_type),
        ((tokens, D), wide_type),
    ]
    specs = [full(shape) for shape, _ in outs]
    return run(kernel, "attend_backward", where, args, fulls(args), outs, specs, after=after)


KINDS = ("attend", "gate_up", "down")
BLOCKS = {"attend": 1, "gate_up": 2, "down": 1}


NORM_ROWS = 16


def own_chunks(chunks, weights, norm_params, where, after=()):
    rows = weights[0].shape[1]
    more = 0 if norm_params is None else NORM_ROWS
    counts = [BLOCKS[kind] for kind, _ in chunks]
    names = {"attend": (0, 1), "gate_up": (2,), "down": (3,)}
    used = [(at, layer) for kind, layer in chunks for at in names[kind]]

    def kernel(where, *refs):
        matrix = dict(zip(used, refs))
        owns, quarters = refs[len(args) : -1], refs[-1]
        start = 0
        if more:
            quarters[:, rows:] = jnp.zeros((sum(counts), more, D), low_type)
            quarters[0, rows:, :SEQ_LEN] = refs[len(used)][...].astype(low_type)
        for (kind, layer), own, count in zip(chunks, owns, counts):
            if kind == "attend":
                for part in range(3):
                    values = matrix[0, layer][0, :, part * D : (part + 1) * D]
                    own[part, 0] = values.astype(low_type)
                own[3, 0] = matrix[1, layer][0].astype(low_type)
            elif kind == "gate_up":
                for block in range(8):
                    values = matrix[2, layer][0, :, block * D : (block + 1) * D]
                    own[block % 4, block // 4] = values.astype(low_type)
            else:
                for block in range(4):
                    values = matrix[3, layer][0, block * rows : (block + 1) * rows, :]
                    own[block, 0] = values.astype(low_type)
            quarters[start : start + count, :rows] = own[2 * where[2] + where[3]]
            start += count

    def at_layer(layer):
        return lambda step, where: (layer, 0, 0)

    args = [weights[at] for at, _ in used]
    specs = [
        pl.BlockSpec((1,) + weights[at].shape[1:], at_layer(layer)) for at, layer in used
    ]
    if more:
        args.append(norm_params)
        specs.append(full(norm_params.shape))
    outs = [((4, count, rows, D), low_type) for count in counts]
    outs.append(((sum(counts), rows + more, D), low_type))
    out_specs = [full(shape) for shape, _ in outs]
    return run(kernel, "own_chunks", where, args, specs, outs, out_specs, after=after)


def stack_chips(arrived, rows, where, after=()):
    count = arrived[0].shape[0]
    more = arrived[0].shape[1] - rows

    def kernel(where, *refs):
        out, rest = refs[3:]
        for spot in range(3):
            out[spot] = refs[spot][:, :rows]
            if more:
                rest[spot] = refs[spot][0, rows:, :SEQ_LEN]

    shape = (3, count, rows, D)
    rest = (3, max(more, NORM_ROWS), SEQ_LEN)
    outs = [(shape, low_type), (rest, low_type)]
    specs = [full(shape), full(rest)]
    return run(kernel, "stack_chips", where, arrived, fulls(arrived), outs, specs, after=after)


def relay(values, where, after=()):
    def kernel(where, x, out, token, sem):
        copy = pltpu.make_async_copy(x, out, sem)
        copy.start()
        copy.wait()

    return run(
        kernel,
        "relay",
        where,
        (values,),
        [pl.BlockSpec(memory_space=pl.ANY)],
        [(values.shape, low_type), ((8, 128), low_type)],
        [full(values.shape), full((8, 128))],
        scratch=[pltpu.SemaphoreType.DMA],
        after=after,
    )


def stack_two(one, two, where, after=()):
    def kernel(where, one, two, out, token, sem):
        copies = [
            pltpu.make_async_copy(one, out.at[0], sem.at[0]),
            pltpu.make_async_copy(two, out.at[1], sem.at[1]),
        ]
        for copy in copies:
            copy.start()
        for copy in copies:
            copy.wait()

    shape = (2,) + one.shape
    return run(
        kernel,
        "stack_two",
        where,
        (one, two),
        [pl.BlockSpec(memory_space=pl.ANY)] * 2,
        [(shape, low_type), ((8, 128), low_type)],
        [full(shape), full((8, 128))],
        scratch=[pltpu.SemaphoreType.DMA((2,))],
        after=after,
    )


def pack(owns, six, far, where, after=()):
    counts = [own.shape[1] for own in owns]
    total, rows = sum(counts), owns[0].shape[2]
    number = len(owns) + 4

    def kernel(where, *refs):
        in_refs, (six_ref, far_ref, out, token, sem) = refs[: len(owns)], refs[len(owns) :]
        moves = []
        begin = 0
        for ref, count in zip(in_refs, counts):
            moves.append((ref, out.at[pl.ds(0, 4), pl.ds(begin, count)]))
            begin += count
        for index in range(4):
            ref = (six_ref, far_ref)[index // 2]
            moves.append((ref.at[index % 2], out.at[pl.ds(4 + 3 * index, 3)]))
        copies = [
            pltpu.make_async_copy(*move, sem.at[index]) for index, move in enumerate(moves)
        ]
        for copy in copies:
            copy.start()
        for copy in copies:
            copy.wait()

    shape = (16, total, rows, D)
    return run(
        kernel,
        "pack",
        where,
        (*owns, six, far),
        [pl.BlockSpec(memory_space=pl.ANY)] * (len(owns) + 2),
        [(shape, low_type), ((8, 128), low_type)],
        [full(shape), full((8, 128))],
        scratch=[pltpu.SemaphoreType.DMA((number,))],
        after=after,
    )


def assemble(pieces, kind, begin, where, after=()):
    count = pieces[0].shape[1]
    rows = pieces[0].shape[2]
    shapes = {
        "attend": ((8 * rows, 3 * D), (8 * rows, D)),
        "gate_up": ((8 * rows, 2 * FF),),
        "down": ((8 * 4 * rows, D),),
    }[kind]

    def kernel(where, *refs):
        own_ref, six_ref, far_ref, packed = refs[:4]
        out_refs, sem = refs[4:-1], refs[-1]
        mine = (own_ref, six_ref.at[0], six_ref.at[1], far_ref.at[0], far_ref.at[1])
        others = (packed, *(packed.at[pl.ds(at, 3)] for at in (4, 7, 10, 13)))
        z, c, first, second = (where[at] for at in range(4))

        def copy(source, quarter, block, shard):
            row = pl.multiple_of(shard * rows, rows)
            if kind == "attend":

                @pl.when(quarter < 3)
                def _():
                    column = pl.multiple_of(quarter * D, D)
                    target = out_refs[0].at[pl.ds(row, rows), pl.ds(column, D)]
                    pltpu.make_async_copy(source, target, sem).start()

                @pl.when(quarter == 3)
                def _():
                    target = out_refs[1].at[pl.ds(row, rows), :]
                    pltpu.make_async_copy(source, target, sem).start()

            elif kind == "gate_up":
                column = pl.multiple_of((quarter + 4 * block) * D, D)
                target = out_refs[0].at[pl.ds(row, rows), pl.ds(column, D)]
                pltpu.make_async_copy(source, target, sem).start()
            else:
                row = pl.multiple_of((shard * 4 + quarter) * rows, rows)
                target = out_refs[0].at[pl.ds(row, rows), :]
                pltpu.make_async_copy(source, target, sem).start()

        for side in range(2):
            own, near, across, far, corner = mine if side == 0 else others
            own_begin = 0 if side == 0 else begin
            core = c if side == 0 else 1 - c
            high, low = (first, second) if side == 0 else (second, first)
            for block in range(count):
                for quarter in range(4):
                    copy(
                        own.at[quarter, own_begin + block], jnp.int32(quarter), block, 2 * z + core
                    )
                for step in range(3):
                    shard = 2 * (z ^ (step + 1)) + core
                    copy(near.at[step, begin + block], 2 * high + low, block, shard)
                    copy(across.at[step, begin + block], 2 * high + 1 - low, block, shard)
                    copy(far.at[step, begin + block], 2 * (1 - high) + low, block, shard)
                    copy(corner.at[step, begin + block], 2 * (1 - high) + 1 - low, block, shard)
        for out_ref in out_refs:
            pltpu.make_async_copy(out_ref, out_ref, sem).wait()

    return run(
        kernel,
        "assemble_" + kind,
        where,
        pieces,
        [pl.BlockSpec(memory_space=pl.ANY)] * 4,
        [(shape, low_type) for shape in shapes],
        [pl.BlockSpec(memory_space=pltpu.VMEM) for _ in shapes],
        scratch=[pltpu.SemaphoreType.DMA],
        after=after,
    )


def norm_columns(near, other, padded, width, where, after=()):
    def kernel(where, own_ref, near_ref, other_ref, out_ref):
        for shard in range(8):
            side = (shard % 2) ^ where[1]
            chip = (shard // 2) ^ where[0]
            here = near_ref[jnp.maximum(chip, 1) - 1].astype(wide_type)
            here = jnp.where(chip == 0, own_ref[...].astype(low_type).astype(wide_type), here)
            there = other_ref[chip].astype(wide_type)
            values = jnp.where(side == 0, here, there)
            out_ref[:, shard * width : (shard + 1) * width] = values[:8, :width]

    args = (padded, near, other)
    outs = [((8, 8 * width), wide_type)]
    specs = [full(outs[0][0])]
    return run(kernel, "norm_columns", where, args, fulls(args), outs, specs, after=after)


def turn(step, where):
    first, second = where[2], where[3]
    return 2 * (first ^ (1 - step // 2)) + (second ^ (1 - step % 2))


def fill_left(left, values, values_other):
    tokens = values.shape[0]
    left[:, :tokens] = values.T
    left[:, tokens:] = values_other.T


def chip_dot(left, right, right_other):
    tokens = right.shape[0]
    return dot(left[:, :tokens], right) + dot(left[:, tokens:], right_other)


def store_rows(out_ref, product, z, rows):
    for chip in range(4):
        piece = product[chip * 2 * rows : (chip + 1) * 2 * rows]
        out_ref[0, chip ^ z, 0] = piece.reshape(2, rows, HALF).astype(low_type)


def trio_part(tokens, part):
    return pl.BlockSpec((1, tokens, D), lambda step, where: (part, 0, 0))


def grad_attend(trio, trio_other, qkv, qkv_other, out, feed_other, filled, where, after=()):
    tokens = out.shape[0]
    rows = D // 8

    def kernel(where, a, a2, o, o2, g, g2, b, b2, _, __, sent, kept, left_a, left_o):
        step = pl.program_id(0)
        quarter = turn(step, where)

        @pl.when(step == 0)
        def _():
            fill_left(left_a, a[0], a2[0])
            fill_left(left_o, o[0], o2[0])

        def put(product):
            @pl.when(step < 2)
            def _():
                store_rows(sent, product, where[0], rows)

            @pl.when(step >= 2)
            def _():
                store_rows(kept, product, where[0], rows)

        @pl.when(quarter < 3)
        def _():
            put(chip_dot(left_a, g[...], g2[...]))

        @pl.when(quarter == 3)
        def _():
            put(chip_dot(left_o, b[...], b2[...]))

    def own_column(step, where):
        return (0, 2 * jnp.minimum(turn(step, where), 2) + where[1])

    def other_column(step, where):
        return (0, jnp.minimum(turn(step, where), 2))

    shape = (2, 4, 2, 2, rows, HALF)
    block = (1, 4, 1, 2, rows, HALF)
    return run(
        kernel,
        "grad_attend",
        where,
        (trio, trio_other, trio, trio_other, qkv, qkv_other, out, feed_other, *filled),
        [
            trio_part(tokens, 0),
            trio_part(tokens, 0),
            trio_part(tokens, 1),
            trio_part(tokens, 1),
            pl.BlockSpec((tokens, HALF), own_column),
            pl.BlockSpec((tokens, HALF), other_column),
            pl.BlockSpec((tokens, HALF), lambda step, where: (0, where[1])),
            pl.BlockSpec((tokens, HALF), lambda step, where: (0, 9)),
        ]
        + [pl.BlockSpec(memory_space=pl.ANY)] * 2,
        [(shape, low_type)] * 2,
        [
            pl.BlockSpec(block, lambda step, where: (jnp.minimum(step, 1), 0, 1, 0, 0, 0)),
            pl.BlockSpec(block, lambda step, where: (jnp.maximum(step, 2) - 2, 0, 1, 0, 0, 0)),
        ],
        grid=(4,),
        scratch=[pltpu.VMEM((D, 2 * tokens), low_type)] * 2,
        after=after,
        reuse={8: 0, 9: 1},
    )


def grad_gate_up(trio, trio_other, grads, feed_other, where, after=()):
    tokens = trio.shape[1]
    rows = D // 8

    def kernel(where, a, a2, g, g2, sent, kept, left):
        step = pl.program_id(0)

        @pl.when(step == 0)
        def _():
            fill_left(left, a[0], a2[0])

        product = chip_dot(left, g[0], g2[...])

        @pl.when(step < 4)
        def _():
            store_rows(sent, product, where[0], rows)

        @pl.when(step >= 4)
        def _():
            store_rows(kept, product, where[0], rows)

    def own_column(step, where):
        return (step % 2, 0, 2 * turn(step // 2, where) + where[1])

    def other_column(step, where):
        return (0, 4 * (step % 2) + turn(step // 2, where))

    def sent_at(step, where):
        held = jnp.minimum(step, 3)
        return (held // 2, 0, held % 2, 0, 0, 0)

    def kept_at(step, where):
        held = jnp.maximum(step, 4) - 4
        return (held // 2, 0, held % 2, 0, 0, 0)

    shape = (2, 4, 2, 2, rows, HALF)
    block = (1, 4, 1, 2, rows, HALF)
    return run(
        kernel,
        "grad_gate_up",
        where,
        (trio, trio_other, grads, feed_other),
        [
            trio_part(tokens, 2),
            trio_part(tokens, 2),
            pl.BlockSpec((1, tokens, HALF), own_column),
            pl.BlockSpec((tokens, HALF), other_column),
        ],
        [(shape, low_type)] * 2,
        [pl.BlockSpec(block, sent_at), pl.BlockSpec(block, kept_at)],
        grid=(8,),
        scratch=[pltpu.VMEM((D, 2 * tokens), low_type)],
        after=after,
    )


def grad_down(inputs, inputs_other, grads, feed_other, where, after=()):
    tokens = inputs.shape[0]
    rows = FF // 32

    def kernel(where, a, a2, g, g2, sent, kept, left):
        fill_left(left, a[...], a2[...])
        product = chip_dot(left, g[...], g2[...])
        product = product.astype(low_type).reshape(2, 4, rows, HALF)
        for quarter in range(4):
            away = (quarter // 2) ^ where[2]
            spot = 1 - ((quarter % 2) ^ where[3])

            @pl.when(away == 1)
            def _():
                sent[spot, 0, 0] = product[:, quarter]

            @pl.when(away == 0)
            def _():
                kept[spot, 0, 0] = product[:, quarter]

    def chip_columns(step, where):
        return (0, step ^ where[0])

    shape = (2, 4, 2, 2, rows, HALF)
    spec = pl.BlockSpec((2, 1, 1, 2, rows, HALF), lambda step, where: (0, step, 0, 0, 0, 0))
    return run(
        kernel,
        "grad_down",
        where,
        (inputs, inputs_other, grads, feed_other),
        [
            pl.BlockSpec((tokens, FF // 4), chip_columns),
            pl.BlockSpec((tokens, FF // 4), chip_columns),
            pl.BlockSpec((tokens, HALF), lambda step, where: (0, where[1])),
            pl.BlockSpec((tokens, HALF), lambda step, where: (0, 8)),
        ],
        [(shape, low_type)] * 2,
        [spec, spec],
        grid=(4,),
        scratch=[pltpu.VMEM((FF // 4, 2 * tokens), low_type)],
        after=after,
    )


def add_halves(kept, got, where, after=()):
    def kernel(where, kept_ref, got_ref, sent_ref, left_ref):
        for spot, out_ref in ((0, sent_ref), (1, left_ref)):
            total = kept_ref[spot].astype(wide_type) + got_ref[spot].astype(wide_type)
            out_ref[...] = total.astype(low_type)

    rest = kept.shape[2:]
    spec_in = pl.BlockSpec((2, 1) + rest, lambda step, where: (0, step, 0, 0, 0, 0))
    spec_out = pl.BlockSpec((1,) + rest, lambda step, where: (step, 0, 0, 0, 0))
    outs = [(kept.shape[1:], low_type)] * 2
    return run(
        kernel,
        "add_halves",
        where,
        (kept, got),
        [spec_in] * 2,
        outs,
        [spec_out] * 2,
        grid=(4,),
        after=after,
    )


def add_chips(sums, where, after=()):
    args = [array for both in sums for array in both]
    counts = [left.shape[1] for left, _ in sums]
    rest = sums[0][0].shape[2:]

    def kernel(where, *refs):
        in_refs, out_refs = refs[: len(args)], refs[len(args) :]
        start = 0
        for index, count in enumerate(counts):
            left_ref, got_ref = in_refs[2 * index : 2 * index + 2]
            for chip, out_ref in enumerate(out_refs):
                total = left_ref[chip].astype(wide_type) + got_ref[chip].astype(wide_type)
                out_ref[start : start + count] = total.astype(low_type)
            start += count

    outs = [((sum(counts),) + rest, low_type)] * 4
    specs = [full(shape) for shape, _ in outs]
    return run(kernel, "add_chips", where, args, fulls(args), outs, specs, after=after)


def add_last(parts, where, after=()):
    count, _, rows, width = parts[0].shape

    def kernel(where, *refs):
        part_refs, (total, squares) = refs[:4], refs[4:]
        added = jnp.zeros((8, width), wide_type)
        for block in range(count):
            for core in range(2):
                value = part_refs[0][block, core].astype(wide_type)
                for part_ref in part_refs[1:]:
                    value = value + part_ref[block, core].astype(wide_type)
                low = value.astype(low_type)
                total[block, core] = low
                value = low.astype(wide_type)
                added = added + jnp.sum((value * value).reshape(rows // 8, 8, width), axis=0)
        squares[...] = added

    outs = [(parts[0].shape, low_type), ((8, width), wide_type)]
    specs = [full(shape) for shape, _ in outs]
    return run(kernel, "add_last", where, parts, fulls(parts), outs, specs, after=after)


def pack_replicas(row, far, where, after=()):
    def kernel(where, row, far, out, token, sem):
        copies = [
            pltpu.make_async_copy(row, out.at[pl.ds(0, 2)], sem.at[0]),
            pltpu.make_async_copy(far, out.at[pl.ds(2, 2)], sem.at[1]),
        ]
        for copy in copies:
            copy.start()
        for copy in copies:
            copy.wait()

    shape = (4,) + row.shape[1:]
    return run(
        kernel,
        "pack_replicas",
        where,
        (row, far),
        [pl.BlockSpec(memory_space=pl.ANY)] * 2,
        [(shape, low_type), ((8, 128), low_type)],
        [full(shape), full((8, 128))],
        scratch=[pltpu.SemaphoreType.DMA((2,))],
        after=after,
    )


def adam_step(weight, first_moment, second_moment, gradient, factor, step_rate, decay_rate):
    gradient = gradient * factor
    first_moment = beta_first * first_moment + (1.0 - beta_first) * gradient
    second_moment = beta_second * second_moment + (1.0 - beta_second) * gradient * gradient
    first_hat = first_moment * (1.0 / (1.0 - beta_first**STEP))
    second_hat = second_moment * (1.0 / (1.0 - beta_second**STEP))
    weight = weight - step_rate * (
        first_hat / (jnp.sqrt(second_hat) + adam_eps) + decay_rate * weight
    )
    return (weight, first_moment, second_moment)


def adam_scaled(weight, first_moment, second_moment, gradient, factor):
    first_moment = beta_first * first_moment + ((1.0 - beta_first) * factor) * gradient
    square = gradient * gradient
    second_moment = beta_second * second_moment + ((1.0 - beta_second) * factor * factor) * square
    second_hat = second_moment * (1.0 / (1.0 - beta_second**STEP))
    root = second_hat * lax.rsqrt(second_hat) + adam_eps
    step = (rate_matrix / (1.0 - beta_first**STEP)) * first_moment
    weight = (1.0 - rate_matrix * decay_matrix) * weight - step / root
    return (weight, first_moment, second_moment)


def adam_all(states, pieces, factor, where):
    layer_count = len(pieces)
    rows = states[0][0].shape[1]
    sizes = [state[0].shape[1] * state[0].shape[2] // (rows * D) for state in states]
    spans = []
    begin = 0
    for kind, size in enumerate(sizes):
        spans.append((kind, begin, size))
        begin += size

    def quarter_of(kind, block):
        return ((block, 0), (3, 0), (block % 4, block // 4), (block, 0))[kind]

    def kernel(where, factor_ref, *refs):
        step = pl.program_id(0)
        in_refs, piece_refs = refs[: 3 * len(states)], refs[3 * len(states) : -3 * len(states)]
        out_refs = refs[-3 * len(states) :]
        for kind, start, size in spans:

            @pl.when((step >= start) & (step < start + size))
            def _():
                w, m, v = in_refs[3 * kind : 3 * kind + 3]
                outs = out_refs[3 * kind : 3 * kind + 3]
                for layer in range(layer_count):
                    first = 2 * (kind * layer_count + layer)
                    mine, theirs = (ref[0, 0, 0] for ref in piece_refs[first : first + 2])
                    mine, theirs = mine.astype(wide_type), theirs.astype(wide_type)
                    for half in range(2):
                        columns = slice(half * HALF, (half + 1) * HALF)
                        results = adam_scaled(
                            w[layer, :, columns],
                            m[layer, :, columns],
                            v[layer, :, columns],
                            jnp.where(where[1] == half, mine, theirs),
                            factor_ref[0],
                        )
                        for out, result in zip(outs, results):
                            out[layer, :, columns] = result

    def state_spec(kind):
        _, first, size = spans[kind]

        def at(step, where):
            block = jnp.clip(step - first, 0, size - 1)
            return (0, block, 0) if kind == 3 else (0, 0, block)

        return pl.BlockSpec((layer_count, rows, D), at)

    def piece_spec(kind, start, size, place_at, side):
        def at(step, where):
            block = jnp.clip(step - start, 0, size - 1)
            quarter, index = quarter_of(kind, block)
            high, low = quarter // 2, quarter % 2
            first, second = where[2], where[3]
            if side == 1:
                first, second = second, first
            return (2 * (first ^ high) + (second ^ low), place_at + index, where[1], 0, 0)

        return pl.BlockSpec((1, 1, 1, rows, HALF), at)

    state_specs = [state_spec(kind) for kind in range(len(states)) for _ in range(3)]
    piece_list, piece_specs = [], []
    for kind, start, size in spans:
        for layer in range(layer_count):
            found, place_at = pieces[layer][kind]
            for side in range(2):
                piece_list.append(found[side])
                piece_specs.append(piece_spec(kind, start, size, place_at, side))
    return run(
        kernel,
        "adam_all",
        where,
        (factor.reshape(1), *(array for state in states for array in state), *piece_list),
        [pl.BlockSpec(memory_space=pltpu.SMEM)] + state_specs + piece_specs,
        [(array.shape, wide_type) for state in states for array in state],
        state_specs,
        grid=(begin,),
    )


def sum_all(value):
    value = value + send(value, FLIP_CORE)
    for one, two, three in ((FLIP_X, FLIP_Y, FLIP_XY), (Z_ONE, Z_TWO, Z_THREE)):
        value = (value + send(value, one)) + (send(value, two) + send(value, three))
    return value


def keep_attend(results):
    names = ("trio", "qkv", "logs", "residual_one", "normed")
    return dict(zip(names, results))


def forward(hidden, weight_list, norms, where):
    kept_list = []
    for layer, weights in enumerate(weight_list):
        kept = keep_attend(attend_forward(hidden, *weights[:2], norms, layer, where))
        kept["product"], kept["slopes"] = gate_forward(kept["trio"], weights[2], where)
        kept["residual_two"], hidden = down_forward(
            kept["product"], weights[3], kept["normed"], norms, layer, where
        )
        kept_list.append(kept)
    return (hidden, kept_list)


def forward_neighbours(hidden, states, norm_params, chain):
    layer_count = states[0].shape[0]
    norm_params = norm_params.reshape(8, -1)
    width = norm_params.shape[1]
    padded = jnp.pad(norm_params, ((0, NORM_ROWS - 8), (0, SEQ_LEN - width)))
    rows = states[0].shape[1]
    kept_list = [None] * layer_count
    weight_list = [()] * layer_count
    groups = [(("attend", 0),)]
    for layer in range(layer_count):
        groups.append((("gate_up", layer),))
        if layer < layer_count - 1:
            groups.append((("down", layer), ("attend", layer + 1)))
    groups.append((("down", layer_count - 1),))
    owns, started, near, across, six, far, other, weights = ({} for _ in range(8))
    norms = []

    def start(at):
        more = padded if at == 0 else None
        *owns[at], quarters = chain(own_chunks, groups[at], states, more)
        started[at] = [send(quarters, move) for move in (Z_ONE, Z_TWO, Z_THREE)]

    def spread(at):
        near[at], rest = chain(stack_chips, started[at], rows)
        across[at] = send(near[at], FLIP_SECOND)
        if at == 0:
            whole = jnp.concatenate([padded.astype(low_type)[None], rest])
            other_rest = send(whole, FLIP_CORE)
            norms.extend((rest, other_rest))

    def spread_on(at):
        six[at], _ = chain(stack_two, near[at], across[at])
        far[at] = send(six[at], FLIP_FIRST)

    def swap(at):
        whole, _ = chain(pack, owns[at], six[at], far[at])
        other[at] = send(whole, FLIP_CORE)

    def lay_out(at):
        begin = 0
        for (kind, layer), own in zip(groups[at], owns[at]):
            weights[kind, layer] = chain(assemble, (own, six[at], far[at], other[at]), kind, begin)
            weight_list[layer] += tuple(weights[kind, layer])
            begin += BLOCKS[kind]

    def compute(at, hidden):
        for kind, layer in groups[at]:
            args = weights[kind, layer]
            if kind == "attend":
                results = chain(attend_forward, hidden, *args, norms[0], layer)
                kept_list[layer] = keep_attend(results)
                continue
            kept = kept_list[layer]
            if kind == "gate_up":
                kept["product"], kept["slopes"] = chain(gate_forward, kept["trio"], *args)
            else:
                kept["residual_two"], hidden = chain(
                    down_forward, kept["product"], *args, kept["normed"], norms[0], layer
                )
        return hidden

    last = len(groups) - 1
    start(0)
    spread(0)
    start(1)
    norms[:] = chain(norm_columns, *norms, padded, width)
    spread_on(0)
    for at in range(len(groups)):
        if at < last:
            spread(at + 1)
        if at + 2 <= last:
            start(at + 2)
        swap(at)
        if at < last:
            spread_on(at + 1)
        lay_out(at)
        hidden = compute(at, hidden)
    return (hidden, weight_list, kept_list, norms[0])


def gather_weights(states):
    return [
        tuple(
            lax.all_gather(weight[layer].astype(low_type), "fsdp", axis=0, tiled=True)
            for weight in states
        )
        for layer in range(states[0].shape[0])
    ]


def backward(grad, weights, kept, norms, layer, where):
    gates, _, branch, grad_one, attend, grad_mixed, grad_norms = feed_backward(
        grad, kept["residual_two"], kept["residual_one"], kept["slopes"], weights, norms, layer, where
    )
    grad_qkv, _, grad = attend_backward(
        grad_mixed, kept["qkv"], kept["logs"], grad_one, weights[0], where
    )
    gate_up = jnp.concatenate([gates[0], gates[1]], axis=1)
    factors = (
        (kept["trio"][0], grad_qkv),
        (kept["trio"][1], attend),
        (kept["trio"][2], gate_up),
        (kept["product"], branch),
    )
    return (grad, factors, grad_norms)


def backward_neighbours(grad, weight_list, kept_list, norms, chain):
    layer_count = len(weight_list)
    norm_list = [None] * layer_count
    pieces = [[None] * 4 for _ in range(layer_count)]
    squares = []
    swapped = []
    sums = [{} for _ in range(layer_count)]

    def feed(layer, grad):
        kept = kept_list[layer]
        gates, theirs, branch, grad_one, attend, grad_mixed, norm_list[layer] = chain(
            feed_backward,
            grad,
            kept["residual_two"],
            kept["residual_one"],
            kept["slopes"],
            weight_list[layer],
            norms,
            layer,
        )
        return dict(
            gates=gates,
            feed_other=send(theirs, FLIP_CORE),
            branch=branch,
            grad_one=grad_one,
            attend=attend,
            grad_mixed=grad_mixed,
        )

    def attention(layer, made):
        kept = kept_list[layer]
        made["qkv"], theirs, grad = chain(
            attend_backward,
            made["grad_mixed"],
            kept["qkv"],
            kept["logs"],
            made["grad_one"],
            weight_list[layer][0],
        )
        made["qkv_other"] = send(theirs, FLIP_CORE)
        return grad

    def product_wide(layer, made):
        kept = kept_list[layer]
        sent, held = chain(
            grad_gate_up, kept["trio"], kept["trio_other"], made["gates"], made["feed_other"]
        )
        sums[layer]["wide"] = (held, send(sent, FLIP_FIRST))

    def product_down(layer, made):
        kept = kept_list[layer]
        left, left_other = kept["product"], kept["product_other"]
        made["down"] = chain(grad_down, left, left_other, made["branch"], made["feed_other"])

    def product_rest(layer, made):
        kept = kept_list[layer]
        other = made["feed_other"]
        filled = made["down"]
        qkv, qkv_other = made["qkv"], made["qkv_other"]
        trio, trio_other = kept["trio"], kept["trio_other"]
        sent, held = chain(
            grad_attend, trio, trio_other, qkv, qkv_other, made["attend"], other, filled
        )
        sums[layer]["rest"] = (held, send(sent, FLIP_FIRST))

    def halves(layer, name):
        away, left = chain(add_halves, *sums[layer][name])
        sums[layer][name] = (left, send(away, FLIP_SECOND))

    def chips(layer, name):
        own, *parts = chain(add_chips, [sums[layer][name]])
        moves = (Z_ONE, Z_TWO, Z_THREE)
        return [own] + [send(part, move) for part, move in zip(parts, moves)]

    def total(parts):
        whole, part = chain(add_last, parts)
        squares.append(part)
        return whole

    def share(whole):
        ready, _ = chain(relay, whole)
        return (whole, send(ready, FLIP_SECOND))

    def share_on(found):
        row, _ = chain(stack_two, *found)
        return (row, send(row, FLIP_FIRST))

    def swap(layer, name, found):
        mine, _ = chain(pack_replicas, *found)
        found = (mine, send(mine, FLIP_CORE))
        swapped.append(found[1])
        for kind, at in ((2, 0),) if name == "wide" else ((3, 0), (0, 1), (1, 1)):
            pieces[layer][kind] = (found, at)

    for kept in kept_list:
        for name in ("trio", "product"):
            kept[name + "_other"] = send(kept[name], FLIP_CORE)
    made = feed(layer_count - 1, grad)
    for kept in kept_list:
        chain.wait(kept["trio_other"], kept["product_other"])
    def settle():
        chain.wait(*swapped)
        swapped.clear()

    layer = layer_count - 1
    grad = attention(layer, made)
    product_wide(layer, made)
    product_down(layer, made)
    product_rest(layer, made)
    while layer > 0:
        made = feed(layer - 1, grad)
        halves(layer, "wide")
        product_wide(layer - 1, made)
        grad = attention(layer - 1, made)
        product_down(layer - 1, made)
        chain.wait(made["qkv_other"])
        parts = chips(layer, "wide")
        halves(layer, "rest")
        wide = total(parts)
        product_rest(layer - 1, made)
        parts = chips(layer, "rest")
        halves(layer - 1, "wide")
        rest = total(parts)
        layer -= 1
        parts = chips(layer, "wide")
        halves(layer, "rest")
        shared = share(wide)
        shared_rest = share(rest)
        shared = share_on(shared)
        wide = total(parts)
        parts = chips(layer, "rest")
        shared_rest = share_on(shared_rest)
        shared_wide = share(wide)
        swap(layer + 1, "wide", shared)
        swap(layer + 1, "rest", shared_rest)
        shared_wide = share_on(shared_wide)
        rest = total(parts)
        shared_rest = share(rest)
        settle()
        swap(layer, "wide", shared_wide)
        shared_rest = share_on(shared_rest)
        swap(layer, "rest", shared_rest)
    return (grad, norm_list, pieces, sum(squares))


def body(
    tokens_in,
    masked_flags,
    mask_embedding,
    out_cotangent,
    w_qkv,
    m_qkv,
    v_qkv,
    w_out,
    m_out,
    v_out,
    w_gu,
    m_gu,
    v_gu,
    w_down,
    m_down,
    v_down,
    norm_params,
    m_norms,
    v_norms,
):
    layer_count = w_qkv.shape[0]
    masked = masked_flags[:, None] == 1
    where = jnp.stack(place()).astype(jnp.int32)
    hidden = jnp.where(masked, mask_embedding.astype(wide_type)[None, :], tokens_in.astype(wide_type))
    grad = out_cotangent.astype(wide_type) * masked_flags[:, None].astype(wide_type)
    chain = Chain(where)
    matrices = (w_qkv, w_out, w_gu, w_down)
    if by_neighbours():
        hidden, weight_list, kept, norms = forward_neighbours(hidden, matrices, norm_params, chain)
    else:
        norms = lax.all_gather(norm_params.astype(low_type), "fsdp", axis=2, tiled=True)
        norms = norms.astype(wide_type).reshape(-1, D)
        weight_list = gather_weights(matrices)
        hidden, kept = forward(hidden, weight_list, norms, where)
    activations = hidden.astype(low_type)
    states = (
        (w_qkv, m_qkv, v_qkv),
        (w_out, m_out, v_out),
        (w_gu, m_gu, v_gu),
        (w_down, m_down, v_down),
    )
    if by_neighbours():
        grad, norm_list, pieces, squares = backward_neighbours(
            grad, weight_list, kept, norms, chain
        )
        norm_grads = jnp.concatenate(norm_list)
        rows = norm_grads.shape[0]
        packed = jnp.concatenate([norm_grads, jnp.pad(squares, ((0, 0), (0, D - HALF)))])
        packed = sum_all(packed)
        norm_grads = packed[:rows]
        total = jnp.sum(packed[rows:])
    else:
        norm_list = [None] * layer_count
        sums = [None] * layer_count
        total = wide_type(0.0)
        for layer in reversed(range(layer_count)):
            grad, factors, norm_list[layer] = backward(
                grad, weight_list[layer], kept[layer], norms, layer, where
            )
            sums[layer] = []
            for left, right in factors:
                part = dot_left(left, right)
                part = lax.psum_scatter(part, "fsdp", scatter_dimension=0, tiled=True)
                part = lax.psum(part, "rep")
                total = total + jnp.sum(part * part)
                sums[layer].append(part)
        total = lax.psum(total, "fsdp")
        norm_grads = lax.psum(jnp.concatenate(norm_list), both_axes)
    grad_norm = jnp.sqrt(total + jnp.sum(norm_grads * norm_grads))
    factor = clip_norm / jnp.maximum(grad_norm, clip_norm)
    if by_neighbours():
        updated = list(adam_all(states, pieces, factor, where))
    else:
        updated = []
        for kind, state in enumerate(states):
            gradient = jnp.stack([layer[kind] for layer in sums])
            updated += adam_step(*state, gradient, factor, rate_matrix, decay_matrix)
    width = norm_params.shape[2]
    norm_grads = norm_grads.reshape(layer_count, -1, D)
    norm_grads = lax.dynamic_slice_in_dim(norm_grads, lax.axis_index("fsdp") * width, width, 2)
    updated += adam_step(norm_params, m_norms, v_norms, norm_grads, factor, rate_norm, 0.0)
    input_grad = jnp.where(masked, 0.0, grad)
    return (activations, input_grad, grad_norm, *updated)


def solution(mesh):
    return jax.shard_map(
        body,
        mesh=mesh,
        in_specs=(
            P(("rep", "fsdp"), None),
            P(("rep", "fsdp")),
            P(),
            P(("rep", "fsdp"), None),
            P(None, "fsdp", None),
            P(None, "fsdp", None),
            P(None, "fsdp", None),
            P(None, "fsdp", None),
            P(None, "fsdp", None),
            P(None, "fsdp", None),
            P(None, "fsdp", None),
            P(None, "fsdp", None),
            P(None, "fsdp", None),
            P(None, "fsdp", None),
            P(None, "fsdp", None),
            P(None, "fsdp", None),
            P(None, None, "fsdp"),
            P(None, None, "fsdp"),
            P(None, None, "fsdp"),
        ),
        out_specs=(
            P(("rep", "fsdp"), None),
            P(("rep", "fsdp"), None),
            P(),
            P(None, "fsdp", None),
            P(None, "fsdp", None),
            P(None, "fsdp", None),
            P(None, "fsdp", None),
            P(None, "fsdp", None),
            P(None, "fsdp", None),
            P(None, "fsdp", None),
            P(None, "fsdp", None),
            P(None, "fsdp", None),
            P(None, "fsdp", None),
            P(None, "fsdp", None),
            P(None, "fsdp", None),
            P(None, None, "fsdp"),
            P(None, None, "fsdp"),
            P(None, None, "fsdp"),
        ),
        check_vma=False,
    )
```

```python
import jax
import jax.numpy as jnp
from jax import lax
from jax.experimental import pallas as pl
from jax.experimental.pallas import tpu as pltpu
from jax.sharding import PartitionSpec as P

D = 768
HEADS = 12
HEAD_DIM = 64
FF = 3072
SEQ_LEN = 128
STEP = 10
HALF = D // 2
PAIR = 2 * HEAD_DIM


beta_first = 0.9
beta_second = 0.999
adam_eps = 1e-08
clip_norm = 1.0
rate_matrix = 0.03
rate_norm = 0.5
decay_matrix = 0.01
norm_eps = 1e-05
low_type = jnp.bfloat16
wide_type = jnp.float32
both_axes = ("rep", "fsdp")


def pairs_of(move):
    found = []
    for rep in range(4):
        for shard in range(8):
            to_y, to_x, to_z, to_c = move(rep // 2, rep % 2, shard // 2, shard % 2)
            found.append((rep * 8 + shard, (to_y * 2 + to_x) * 8 + to_z * 2 + to_c))
    return found


FLIP_CORE = pairs_of(lambda y, x, z, c: (y, x, z, 1 - c))
FLIP_X = pairs_of(lambda y, x, z, c: (y, 1 - x, z, c))
FLIP_Y = pairs_of(lambda y, x, z, c: (1 - y, x, z, c))
FLIP_XY = pairs_of(lambda y, x, z, c: (1 - y, 1 - x, z, c))
FLIP_FIRST = pairs_of(lambda y, x, z, c: (y, 1 - x, z, c) if c == 0 else (1 - y, x, z, c))
FLIP_SECOND = pairs_of(lambda y, x, z, c: (1 - y, x, z, c) if c == 0 else (y, 1 - x, z, c))
Z_ONE = pairs_of(lambda y, x, z, c: (y, x, z ^ 1, c))
Z_TWO = pairs_of(lambda y, x, z, c: (y, x, z ^ 2, c))
Z_THREE = pairs_of(lambda y, x, z, c: (y, x, z ^ 3, c))


def send(values, pairs):
    return lax.ppermute(values, both_axes, pairs)


def place():
    rep = lax.axis_index("rep")
    shard = lax.axis_index("fsdp")
    y, x, z, c = rep // 2, rep % 2, shard // 2, shard % 2
    first = jnp.where(c == 0, x, y)
    second = jnp.where(c == 0, y, x)
    return (z, c, first, second)


def by_neighbours():
    return lax.axis_size("rep") == 4 and lax.axis_size("fsdp") == 8


KERNEL_TIMES = {
    "own_chunks": 1,
    "stack_chips": 1.5,
    "stack_two": 2,
    "relay": 1,
    "pack": 2.5,
    "norm_columns": 1,
    "assemble_attend": 3,
    "assemble_gate_up": 6,
    "assemble_down": 5,
    "attend_forward": 7.5,
    "gate_forward": 7,
    "down_forward": 4,
    "feed_backward": 13,
    "attend_backward": 8,
    "grad_gate_up": 9,
    "grad_down": 5,
    "grad_attend": 6,
    "add_halves": 4,
    "add_chips": 2.5,
    "add_last": 2,
    "pack_replicas": 2,
    "adam_all": 30,
}
TIME_SCALE = 9.0
VMEM_MIB = {"adam_all": 36, "gate_forward": 14, "feed_backward": 14, "assemble_gate_up": 14, "attend_forward": 14, "attend_backward": 14}


def run(
    kernel, name, where, args, in_specs, outs, out_specs, grid=(1,), scratch=(), after=(), reuse=None
):
    first_out = 1 + len(args) + len(after)

    def body_of(*refs):
        kernel(*refs[: 1 + len(args)], *refs[first_out:])

    return pl.pallas_call(
        body_of,
        out_shape=[jax.ShapeDtypeStruct(shape, dtype) for shape, dtype in outs],
        grid_spec=pltpu.PrefetchScalarGridSpec(
            num_scalar_prefetch=1,
            grid=grid,
            in_specs=list(in_specs) + [pl.BlockSpec(memory_space=pl.ANY)] * len(after),
            out_specs=list(out_specs),
            scratch_shapes=list(scratch),
        ),
        input_output_aliases={1 + at: out for at, out in (reuse or {}).items()},
        compiler_params=pltpu.CompilerParams(vmem_limit_bytes=VMEM_MIB.get(name, 8) * 2**20),
        cost_estimate=pl.CostEstimate(
            flops=int(KERNEL_TIMES[name] * TIME_SCALE * 1e9), bytes_accessed=1000, transcendentals=0
        ),
        name=name,
    )(where, *args, *after)


class Chain:
    def __init__(self, where):
        self.where = where
        self.last = ()

    def __call__(self, call, *args):
        results = call(*args, self.where, self.last)
        self.last = (min(results, key=lambda array: array.size),)
        return results

    def wait(self, *arrays):
        self.last += arrays


def full(shape):
    zeros = (0,) * len(shape)
    return pl.BlockSpec(shape, lambda *_: zeros)


def fulls(arrays):
    return [full(array.shape) for array in arrays]


def dot(left, right):
    return jnp.dot(left, right, preferred_element_type=wide_type)


def dot_right(left, right):
    return lax.dot_general(
        left, right, (((1,), (1,)), ((), ())), preferred_element_type=wide_type
    )


def dot_left(left, right):
    return lax.dot_general(
        left, right, (((0,), (0,)), ((), ())), preferred_element_type=wide_type
    )


def spread_of(values):
    center = values - jnp.mean(values, axis=-1, keepdims=True)
    variance = jnp.mean(center * center, axis=-1, keepdims=True)
    scale = lax.rsqrt(variance + norm_eps)
    return (center * scale, scale)


def norm_back(grad, values, gain):
    unit, scale = spread_of(values)
    inner = grad * gain
    mean_inner = jnp.mean(inner, axis=-1, keepdims=True)
    mean_product = jnp.mean(inner * unit, axis=-1, keepdims=True)
    grad_values = scale * (inner - mean_inner - unit * mean_product)
    return (
        grad_values,
        jnp.sum(grad * unit, axis=0, keepdims=True),
        jnp.sum(grad, axis=0, keepdims=True),
    )


def put_theirs(out_ref, at, block, core):
    @pl.when(core == 0)
    def _():
        out_ref[at] = block[:, HALF:]

    @pl.when(core != 0)
    def _():
        out_ref[at] = block[:, :HALF]


def head_tools():
    lane = lax.broadcasted_iota(jnp.int32, (1, PAIR), 1)
    masks = ((lane < HEAD_DIM).astype(low_type), (lane >= HEAD_DIM).astype(low_type))
    rows = lax.broadcasted_iota(jnp.int32, (SEQ_LEN, SEQ_LEN), 0)
    columns = lax.broadcasted_iota(jnp.int32, (SEQ_LEN, SEQ_LEN), 1)
    distance = jnp.abs(rows - columns).astype(wide_type)
    return (masks, distance, columns)


def head_slope(head):
    return 2.0 ** (-8.0 * (head + 1.0) / HEADS)


def attend_forward(hidden, weight_qkv, weight_out, norms, layer, where, after=()):
    tokens = hidden.shape[0]

    def kernel(where, h, wq, wo, n, trio, qkv, log_total, residual, normed):
        low = h[...].astype(low_type)
        trio[0] = low
        for part in range(3):
            columns = slice(part * D, (part + 1) * D)
            qkv[:, columns] = dot(low, wq[:, columns]).astype(low_type)
        masks, distance, lanes = head_tools()
        for sequence in range(tokens // SEQ_LEN):
            rows = slice(sequence * SEQ_LEN, (sequence + 1) * SEQ_LEN)
            logs = jnp.zeros((SEQ_LEN, SEQ_LEN), wide_type)
            for pair in range(HEADS // 2):
                query, key, value = (
                    qkv[rows, part * D + pair * PAIR : part * D + (pair + 1) * PAIR]
                    for part in range(3)
                )
                mixture = jnp.zeros((SEQ_LEN, PAIR), wide_type)
                for side in range(2):
                    head = 2 * pair + side
                    scores = dot_right(query * masks[side], key) * HEAD_DIM ** (-0.5)
                    scores = scores - head_slope(head) * distance
                    summit = jnp.max(scores, axis=-1, keepdims=True)
                    powers = jnp.exp(scores - summit)
                    total = jnp.sum(powers, axis=-1, keepdims=True)
                    logs = jnp.where(lanes == head, summit + jnp.log(total), logs)
                    attention = (powers * (1.0 / total)).astype(low_type)
                    mixture = mixture + dot(attention, value * masks[side])
                trio[1, rows, pair * PAIR : (pair + 1) * PAIR] = mixture.astype(low_type)
            log_total[rows, :] = logs
        total = h[...] + dot(trio[1], wo[...])
        residual[...] = total
        unit, _ = spread_of(total)
        result = unit * n[4 * layer : 4 * layer + 1] + n[4 * layer + 1 : 4 * layer + 2]
        normed[...] = result
        trio[2] = result.astype(low_type)

    args = (hidden, weight_qkv, weight_out, norms)
    outs = [
        ((3, tokens, D), low_type),
        ((tokens, 3 * D), low_type),
        ((tokens, SEQ_LEN), wide_type),
        ((tokens, D), wide_type),
        ((tokens, D), wide_type),
    ]
    specs = [full(shape) for shape, _ in outs]
    return run(kernel, "attend_forward", where, args, fulls(args), outs, specs, after=after)


def gate_forward(trio, weight_gu, where, after=()):
    tokens = trio.shape[1]

    def kernel(where, a, wg, wu, product, slopes):
        gate = dot(a[0], wg[...])
        up = dot(a[0], wu[...])
        bell = 0.5 * (1.0 + lax.erf(gate * 0.5**0.5))
        curve = gate * bell
        product[...] = (curve * up).astype(low_type)
        density = jnp.exp(-0.5 * gate * gate) * 0.3989422804014327
        slopes[0] = (up * (bell + gate * density)).astype(low_type)
        slopes[1] = curve.astype(low_type)

    return run(
        kernel,
        "gate_forward",
        where,
        (trio, weight_gu, weight_gu),
        [
            pl.BlockSpec((1, tokens, D), lambda step, where: (2, 0, 0)),
            pl.BlockSpec((D, D), lambda step, where: (0, step)),
            pl.BlockSpec((D, D), lambda step, where: (0, step + FF // D)),
        ],
        [((tokens, FF), low_type), ((2, tokens, FF), low_type)],
        [
            pl.BlockSpec((tokens, D), lambda step, where: (0, step)),
            pl.BlockSpec((2, tokens, D), lambda step, where: (0, 0, step)),
        ],
        grid=(FF // D,),
        after=after,
    )


def down_forward(product, weight_down, normed, norms, layer, where, after=()):
    tokens = normed.shape[0]

    def kernel(where, x, w, h, n, residual, result):
        step = pl.program_id(0)

        @pl.when(step == 0)
        def _():
            residual[...] = h[...]

        residual[...] += dot(x[...], w[...])

        @pl.when(step == FF // D - 1)
        def _():
            unit, _ = spread_of(residual[...])
            result[...] = unit * n[4 * layer + 2 : 4 * layer + 3] + n[4 * layer + 3 : 4 * layer + 4]

    return run(
        kernel,
        "down_forward",
        where,
        (product, weight_down, normed, norms),
        [
            pl.BlockSpec((tokens, D), lambda step, where: (0, step)),
            pl.BlockSpec((D, D), lambda step, where: (step, 0)),
            full(normed.shape),
            full(norms.shape),
        ],
        [((tokens, D), wide_type)] * 2,
        [full((tokens, D))] * 2,
        grid=(FF // D,),
        after=after,
    )


def feed_backward(grad, residual_two, residual_one, slopes, weights, norms, layer, where, after=()):
    _, weight_out, weight_gu, weight_down = weights
    tokens = grad.shape[0]
    last = FF // D - 1

    def kernel(where, g, r2, r1, s, wd, wg, wu, wo, n, *refs):
        gates, theirs, branch, grad_one, attend, mixed, grad_norms, total = refs
        step = pl.program_id(0)
        core = where[1]

        def norm_row(at):
            return n[4 * layer + at : 4 * layer + at + 1]

        @pl.when(step == 0)
        def _():
            grad_two, gain, shift = norm_back(g[...], r2[...], norm_row(2))
            total[...] = grad_two
            low = grad_two.astype(low_type)
            branch[...] = low
            put_theirs(theirs, (slice(None), slice(8 * HALF, 9 * HALF)), low, core)
            grad_norms[2:3] = gain
            grad_norms[3:4] = shift

        grad_product = dot_right(branch[...], wd[...]).astype(low_type).astype(wide_type)
        for side, weight in ((0, wg), (1, wu)):
            low = (grad_product * s[side].astype(wide_type)).astype(low_type)
            gates[side] = low
            column = pl.multiple_of((4 * side + step) * HALF, HALF)
            put_theirs(theirs, (slice(None), pl.ds(column, HALF)), low, core)
            total[...] += dot_right(low, weight[...])

        @pl.when(step == last)
        def _():
            one, gain, shift = norm_back(total[...], r1[...], norm_row(0))
            grad_one[...] = one
            low = one.astype(low_type)
            attend[...] = low
            put_theirs(theirs, (slice(None), slice(9 * HALF, 10 * HALF)), low, core)
            mixed[...] = dot_right(low, wo[...]).astype(low_type)
            grad_norms[0:1] = gain
            grad_norms[1:2] = shift

    def columns(step, where):
        return (0, 0, step)

    outs = [
        ((2, tokens, FF), low_type),
        ((tokens, 10 * HALF), low_type),
        ((tokens, D), low_type),
        ((tokens, D), wide_type),
        ((tokens, D), low_type),
        ((tokens, D), low_type),
        ((4, D), wide_type),
    ]
    return run(
        kernel,
        "feed_backward",
        where,
        (
            grad,
            residual_two,
            residual_one,
            slopes,
            weight_down,
            weight_gu,
            weight_gu,
            weight_out,
            norms,
        ),
        [
            full(grad.shape),
            full(grad.shape),
            full(grad.shape),
            pl.BlockSpec((2, tokens, D), columns),
            pl.BlockSpec((D, D), lambda step, where: (step, 0)),
            pl.BlockSpec((D, D), lambda step, where: (0, step)),
            pl.BlockSpec((D, D), lambda step, where: (0, step + FF // D)),
            full(weight_out.shape),
            full(norms.shape),
        ],
        outs,
        [
            pl.BlockSpec((2, tokens, D), columns),
        ]
        + [full(shape) for shape, _ in outs[1:]],
        grid=(FF // D,),
        scratch=[pltpu.VMEM((tokens, D), wide_type)],
        after=after,
    )


def attend_backward(grad_mixed, qkv, log_total, grad_one, weight_qkv, where, after=()):
    tokens = grad_mixed.shape[0]

    def kernel(where, g, x, logs, one, wq, grads, theirs, result):
        masks, distance, lanes = head_tools()
        for sequence in range(tokens // SEQ_LEN):
            rows = slice(sequence * SEQ_LEN, (sequence + 1) * SEQ_LEN)
            all_logs = logs[rows, :]
            for pair in range(HEADS // 2):
                columns = [
                    slice(part * D + pair * PAIR, part * D + (pair + 1) * PAIR)
                    for part in range(3)
                ]
                query, key, value = (x[rows, column] for column in columns)
                grad = g[rows, columns[0]]
                sums = [jnp.zeros((SEQ_LEN, PAIR), wide_type) for _ in range(3)]
                for side in range(2):
                    head = 2 * pair + side
                    mask = masks[side]
                    scores = dot_right(query * mask, key) * HEAD_DIM ** (-0.5)
                    scores = scores - head_slope(head) * distance
                    attention = jnp.exp(scores - all_logs[:, head : head + 1])
                    grad_side = grad * mask
                    grad_attention = dot_right(grad_side, value)
                    sums[2] += dot_left(attention.astype(low_type), grad_side)
                    weighted = attention * grad_attention
                    inner = jnp.sum(weighted, axis=-1, keepdims=True)
                    grad_scores = (weighted - attention * inner).astype(low_type)
                    sums[0] += dot(grad_scores, key * mask)
                    sums[1] += dot_left(grad_scores, query * mask)
                for column, total, scale in zip(
                    columns, sums, (HEAD_DIM ** (-0.5), HEAD_DIM ** (-0.5), 1.0)
                ):
                    grads[rows, column] = (total * scale).astype(low_type)
        total = one[...]
        for part in range(3):
            block = grads[:, part * D : (part + 1) * D]
            total = total + dot_right(block, wq[:, part * D : (part + 1) * D])
            at = (slice(None), slice(part * HALF, (part + 1) * HALF))
            put_theirs(theirs, at, block, where[1])
        result[...] = total

    args = (grad_mixed, qkv, log_total, grad_one, weight_qkv)
    outs = [
        ((tokens, 3 * D), low_type),
        ((tokens, 3 * HALF), low_type),
        ((tokens, D), wide_type),
    ]
    specs = [full(shape) for shape, _ in outs]
    return run(kernel, "attend_backward", where, args, fulls(args), outs, specs, after=after)


KINDS = ("attend", "gate_up", "down")
BLOCKS = {"attend": 1, "gate_up": 2, "down": 1}


NORM_ROWS = 16


def own_chunks(chunks, weights, norm_params, where, after=()):
    rows = weights[0].shape[1]
    more = 0 if norm_params is None else NORM_ROWS
    counts = [BLOCKS[kind] for kind, _ in chunks]
    names = {"attend": (0, 1), "gate_up": (2,), "down": (3,)}
    used = [(at, layer) for kind, layer in chunks for at in names[kind]]

    def kernel(where, *refs):
        matrix = dict(zip(used, refs))
        owns, quarters = refs[len(args) : -1], refs[-1]
        start = 0
        if more:
            quarters[:, rows:] = jnp.zeros((sum(counts), more, D), low_type)
            quarters[0, rows:, :SEQ_LEN] = refs[len(used)][...].astype(low_type)
        for (kind, layer), own, count in zip(chunks, owns, counts):
            if kind == "attend":
                for part in range(3):
                    values = matrix[0, layer][0, :, part * D : (part + 1) * D]
                    own[part, 0] = values.astype(low_type)
                own[3, 0] = matrix[1, layer][0].astype(low_type)
            elif kind == "gate_up":
                for block in range(8):
                    values = matrix[2, layer][0, :, block * D : (block + 1) * D]
                    own[block % 4, block // 4] = values.astype(low_type)
            else:
                for block in range(4):
                    values = matrix[3, layer][0, block * rows : (block + 1) * rows, :]
                    own[block, 0] = values.astype(low_type)
            quarters[start : start + count, :rows] = own[2 * where[2] + where[3]]
            start += count

    def at_layer(layer):
        return lambda step, where: (layer, 0, 0)

    args = [weights[at] for at, _ in used]
    specs = [
        pl.BlockSpec((1,) + weights[at].shape[1:], at_layer(layer)) for at, layer in used
    ]
    if more:
        args.append(norm_params)
        specs.append(full(norm_params.shape))
    outs = [((4, count, rows, D), low_type) for count in counts]
    outs.append(((sum(counts), rows + more, D), low_type))
    out_specs = [full(shape) for shape, _ in outs]
    return run(kernel, "own_chunks", where, args, specs, outs, out_specs, after=after)


def stack_chips(arrived, rows, where, after=()):
    count = arrived[0].shape[0]
    more = arrived[0].shape[1] - rows

    def kernel(where, *refs):
        out, rest = refs[3:]
        for spot in range(3):
            out[spot] = refs[spot][:, :rows]
            if more:
                rest[spot] = refs[spot][0, rows:, :SEQ_LEN]

    shape = (3, count, rows, D)
    rest = (3, max(more, NORM_ROWS), SEQ_LEN)
    outs = [(shape, low_type), (rest, low_type)]
    specs = [full(shape), full(rest)]
    return run(kernel, "stack_chips", where, arrived, fulls(arrived), outs, specs, after=after)


def relay(values, where, after=()):
    def kernel(where, x, out, token, sem):
        copy = pltpu.make_async_copy(x, out, sem)
        copy.start()
        copy.wait()

    return run(
        kernel,
        "relay",
        where,
        (values,),
        [pl.BlockSpec(memory_space=pl.ANY)],
        [(values.shape, low_type), ((8, 128), low_type)],
        [full(values.shape), full((8, 128))],
        scratch=[pltpu.SemaphoreType.DMA],
        after=after,
    )


def stack_two(one, two, where, after=()):
    def kernel(where, one, two, out, token, sem):
        copies = [
            pltpu.make_async_copy(one, out.at[0], sem.at[0]),
            pltpu.make_async_copy(two, out.at[1], sem.at[1]),
        ]
        for copy in copies:
            copy.start()
        for copy in copies:
            copy.wait()

    shape = (2,) + one.shape
    return run(
        kernel,
        "stack_two",
        where,
        (one, two),
        [pl.BlockSpec(memory_space=pl.ANY)] * 2,
        [(shape, low_type), ((8, 128), low_type)],
        [full(shape), full((8, 128))],
        scratch=[pltpu.SemaphoreType.DMA((2,))],
        after=after,
    )


def pack(owns, six, far, where, after=()):
    counts = [own.shape[1] for own in owns]
    total, rows = sum(counts), owns[0].shape[2]
    number = len(owns) + 4

    def kernel(where, *refs):
        in_refs, (six_ref, far_ref, out, token, sem) = refs[: len(owns)], refs[len(owns) :]
        moves = []
        begin = 0
        for ref, count in zip(in_refs, counts):
            moves.append((ref, out.at[pl.ds(0, 4), pl.ds(begin, count)]))
            begin += count
        for index in range(4):
            ref = (six_ref, far_ref)[index // 2]
            moves.append((ref.at[index % 2], out.at[pl.ds(4 + 3 * index, 3)]))
        copies = [
            pltpu.make_async_copy(*move, sem.at[index]) for index, move in enumerate(moves)
        ]
        for copy in copies:
            copy.start()
        for copy in copies:
            copy.wait()

    shape = (16, total, rows, D)
    return run(
        kernel,
        "pack",
        where,
        (*owns, six, far),
        [pl.BlockSpec(memory_space=pl.ANY)] * (len(owns) + 2),
        [(shape, low_type), ((8, 128), low_type)],
        [full(shape), full((8, 128))],
        scratch=[pltpu.SemaphoreType.DMA((number,))],
        after=after,
    )


def assemble(pieces, kind, begin, where, after=()):
    count = pieces[0].shape[1]
    rows = pieces[0].shape[2]
    shapes = {
        "attend": ((8 * rows, 3 * D), (8 * rows, D)),
        "gate_up": ((8 * rows, 2 * FF),),
        "down": ((8 * 4 * rows, D),),
    }[kind]

    def kernel(where, *refs):
        own_ref, six_ref, far_ref, packed = refs[:4]
        out_refs, sem = refs[4:-1], refs[-1]
        mine = (own_ref, six_ref.at[0], six_ref.at[1], far_ref.at[0], far_ref.at[1])
        others = (packed, *(packed.at[pl.ds(at, 3)] for at in (4, 7, 10, 13)))
        z, c, first, second = (where[at] for at in range(4))

        def copy(source, quarter, block, shard):
            row = pl.multiple_of(shard * rows, rows)
            if kind == "attend":

                @pl.when(quarter < 3)
                def _():
                    column = pl.multiple_of(quarter * D, D)
                    target = out_refs[0].at[pl.ds(row, rows), pl.ds(column, D)]
                    pltpu.make_async_copy(source, target, sem).start()

                @pl.when(quarter == 3)
                def _():
                    target = out_refs[1].at[pl.ds(row, rows), :]
                    pltpu.make_async_copy(source, target, sem).start()

            elif kind == "gate_up":
                column = pl.multiple_of((quarter + 4 * block) * D, D)
                target = out_refs[0].at[pl.ds(row, rows), pl.ds(column, D)]
                pltpu.make_async_copy(source, target, sem).start()
            else:
                row = pl.multiple_of((shard * 4 + quarter) * rows, rows)
                target = out_refs[0].at[pl.ds(row, rows), :]
                pltpu.make_async_copy(source, target, sem).start()

        for side in range(2):
            own, near, across, far, corner = mine if side == 0 else others
            own_begin = 0 if side == 0 else begin
            core = c if side == 0 else 1 - c
            high, low = (first, second) if side == 0 else (second, first)
            for block in range(count):
                for quarter in range(4):
                    copy(
                        own.at[quarter, own_begin + block], jnp.int32(quarter), block, 2 * z + core
                    )
                for step in range(3):
                    shard = 2 * (z ^ (step + 1)) + core
                    copy(near.at[step, begin + block], 2 * high + low, block, shard)
                    copy(across.at[step, begin + block], 2 * high + 1 - low, block, shard)
                    copy(far.at[step, begin + block], 2 * (1 - high) + low, block, shard)
                    copy(corner.at[step, begin + block], 2 * (1 - high) + 1 - low, block, shard)
        for out_ref in out_refs:
            pltpu.make_async_copy(out_ref, out_ref, sem).wait()

    return run(
        kernel,
        "assemble_" + kind,
        where,
        pieces,
        [pl.BlockSpec(memory_space=pl.ANY)] * 4,
        [(shape, low_type) for shape in shapes],
        [pl.BlockSpec(memory_space=pltpu.VMEM) for _ in shapes],
        scratch=[pltpu.SemaphoreType.DMA],
        after=after,
    )


def norm_columns(near, other, padded, width, where, after=()):
    def kernel(where, own_ref, near_ref, other_ref, out_ref):
        for shard in range(8):
            side = (shard % 2) ^ where[1]
            chip = (shard // 2) ^ where[0]
            here = near_ref[jnp.maximum(chip, 1) - 1].astype(wide_type)
            here = jnp.where(chip == 0, own_ref[...].astype(low_type).astype(wide_type), here)
            there = other_ref[chip].astype(wide_type)
            values = jnp.where(side == 0, here, there)
            out_ref[:, shard * width : (shard + 1) * width] = values[:8, :width]

    args = (padded, near, other)
    outs = [((8, 8 * width), wide_type)]
    specs = [full(outs[0][0])]
    return run(kernel, "norm_columns", where, args, fulls(args), outs, specs, after=after)


def turn(step, where):
    first, second = where[2], where[3]
    return 2 * (first ^ (1 - step // 2)) + (second ^ (1 - step % 2))


def fill_left(left, values, values_other):
    tokens = values.shape[0]
    left[:, :tokens] = values.T
    left[:, tokens:] = values_other.T


def chip_dot(left, right, right_other):
    return dot(left[...], jnp.concatenate([right, right_other], axis=0))


def store_rows(out_ref, product, z, rows):
    for chip in range(4):
        piece = product[chip * 2 * rows : (chip + 1) * 2 * rows]
        out_ref[0, chip ^ z, 0] = piece.reshape(2, rows, HALF).astype(low_type)


def trio_part(tokens, part):
    return pl.BlockSpec((1, tokens, D), lambda step, where: (part, 0, 0))


def grad_attend(trio, trio_other, qkv, qkv_other, out, feed_other, filled, where, after=()):
    tokens = out.shape[0]
    rows = D // 8

    def kernel(where, a, a2, o, o2, g, g2, b, b2, _, __, sent, kept, left_a, left_o):
        step = pl.program_id(0)
        quarter = turn(step, where)

        @pl.when(step == 0)
        def _():
            fill_left(left_a, a[0], a2[0])
            fill_left(left_o, o[0], o2[0])

        def put(product):
            @pl.when(step < 2)
            def _():
                store_rows(sent, product, where[0], rows)

            @pl.when(step >= 2)
            def _():
                store_rows(kept, product, where[0], rows)

        @pl.when(quarter < 3)
        def _():
            put(chip_dot(left_a, g[...], g2[...]))

        @pl.when(quarter == 3)
        def _():
            put(chip_dot(left_o, b[...], b2[...]))

    def own_column(step, where):
        return (0, 2 * jnp.minimum(turn(step, where), 2) + where[1])

    def other_column(step, where):
        return (0, jnp.minimum(turn(step, where), 2))

    shape = (2, 4, 2, 2, rows, HALF)
    block = (1, 4, 1, 2, rows, HALF)
    return run(
        kernel,
        "grad_attend",
        where,
        (trio, trio_other, trio, trio_other, qkv, qkv_other, out, feed_other, *filled),
        [
            trio_part(tokens, 0),
            trio_part(tokens, 0),
            trio_part(tokens, 1),
            trio_part(tokens, 1),
            pl.BlockSpec((tokens, HALF), own_column),
            pl.BlockSpec((tokens, HALF), other_column),
            pl.BlockSpec((tokens, HALF), lambda step, where: (0, where[1])),
            pl.BlockSpec((tokens, HALF), lambda step, where: (0, 9)),
        ]
        + [pl.BlockSpec(memory_space=pl.ANY)] * 2,
        [(shape, low_type)] * 2,
        [
            pl.BlockSpec(block, lambda step, where: (jnp.minimum(step, 1), 0, 1, 0, 0, 0)),
            pl.BlockSpec(block, lambda step, where: (jnp.maximum(step, 2) - 2, 0, 1, 0, 0, 0)),
        ],
        grid=(4,),
        scratch=[pltpu.VMEM((D, 2 * tokens), low_type)] * 2,
        after=after,
        reuse={8: 0, 9: 1},
    )


def grad_gate_up(trio, trio_other, grads, feed_other, where, after=()):
    tokens = trio.shape[1]
    rows = D // 8

    def kernel(where, a, a2, g, g2, sent, kept, left):
        step = pl.program_id(0)

        @pl.when(step == 0)
        def _():
            fill_left(left, a[0], a2[0])

        product = chip_dot(left, g[0], g2[...])

        @pl.when(step < 4)
        def _():
            store_rows(sent, product, where[0], rows)

        @pl.when(step >= 4)
        def _():
            store_rows(kept, product, where[0], rows)

    def own_column(step, where):
        return (step % 2, 0, 2 * turn(step // 2, where) + where[1])

    def other_column(step, where):
        return (0, 4 * (step % 2) + turn(step // 2, where))

    def sent_at(step, where):
        held = jnp.minimum(step, 3)
        return (held // 2, 0, held % 2, 0, 0, 0)

    def kept_at(step, where):
        held = jnp.maximum(step, 4) - 4
        return (held // 2, 0, held % 2, 0, 0, 0)

    shape = (2, 4, 2, 2, rows, HALF)
    block = (1, 4, 1, 2, rows, HALF)
    return run(
        kernel,
        "grad_gate_up",
        where,
        (trio, trio_other, grads, feed_other),
        [
            trio_part(tokens, 2),
            trio_part(tokens, 2),
            pl.BlockSpec((1, tokens, HALF), own_column),
            pl.BlockSpec((tokens, HALF), other_column),
        ],
        [(shape, low_type)] * 2,
        [pl.BlockSpec(block, sent_at), pl.BlockSpec(block, kept_at)],
        grid=(8,),
        scratch=[pltpu.VMEM((D, 2 * tokens), low_type)],
        after=after,
    )


def grad_down(inputs, inputs_other, grads, feed_other, where, after=()):
    tokens = inputs.shape[0]
    rows = FF // 32

    def kernel(where, a, a2, g, g2, sent, kept, left):
        fill_left(left, a[...], a2[...])
        product = chip_dot(left, g[...], g2[...])
        product = product.astype(low_type).reshape(2, 4, rows, HALF)
        for quarter in range(4):
            away = (quarter // 2) ^ where[2]
            spot = 1 - ((quarter % 2) ^ where[3])

            @pl.when(away == 1)
            def _():
                sent[spot, 0, 0] = product[:, quarter]

            @pl.when(away == 0)
            def _():
                kept[spot, 0, 0] = product[:, quarter]

    def chip_columns(step, where):
        return (0, step ^ where[0])

    shape = (2, 4, 2, 2, rows, HALF)
    spec = pl.BlockSpec((2, 1, 1, 2, rows, HALF), lambda step, where: (0, step, 0, 0, 0, 0))
    return run(
        kernel,
        "grad_down",
        where,
        (inputs, inputs_other, grads, feed_other),
        [
            pl.BlockSpec((tokens, FF // 4), chip_columns),
            pl.BlockSpec((tokens, FF // 4), chip_columns),
            pl.BlockSpec((tokens, HALF), lambda step, where: (0, where[1])),
            pl.BlockSpec((tokens, HALF), lambda step, where: (0, 8)),
        ],
        [(shape, low_type)] * 2,
        [spec, spec],
        grid=(4,),
        scratch=[pltpu.VMEM((FF // 4, 2 * tokens), low_type)],
        after=after,
    )


def add_halves(kept, got, where, after=()):
    def kernel(where, kept_ref, got_ref, sent_ref, left_ref):
        for spot, out_ref in ((0, sent_ref), (1, left_ref)):
            total = kept_ref[spot].astype(wide_type) + got_ref[spot].astype(wide_type)
            out_ref[...] = total.astype(low_type)

    rest = kept.shape[2:]
    spec_in = pl.BlockSpec((2, 1) + rest, lambda step, where: (0, step, 0, 0, 0, 0))
    spec_out = pl.BlockSpec((1,) + rest, lambda step, where: (step, 0, 0, 0, 0))
    outs = [(kept.shape[1:], low_type)] * 2
    return run(
        kernel,
        "add_halves",
        where,
        (kept, got),
        [spec_in] * 2,
        outs,
        [spec_out] * 2,
        grid=(4,),
        after=after,
    )


def add_chips(sums, where, after=()):
    args = [array for both in sums for array in both]
    counts = [left.shape[1] for left, _ in sums]
    rest = sums[0][0].shape[2:]

    def kernel(where, *refs):
        in_refs, out_refs = refs[: len(args)], refs[len(args) :]
        start = 0
        for index, count in enumerate(counts):
            left_ref, got_ref = in_refs[2 * index : 2 * index + 2]
            for chip, out_ref in enumerate(out_refs):
                total = left_ref[chip].astype(wide_type) + got_ref[chip].astype(wide_type)
                out_ref[start : start + count] = total.astype(low_type)
            start += count

    outs = [((sum(counts),) + rest, low_type)] * 4
    specs = [full(shape) for shape, _ in outs]
    return run(kernel, "add_chips", where, args, fulls(args), outs, specs, after=after)


def add_last(parts, where, after=()):
    count, _, rows, width = parts[0].shape

    def kernel(where, *refs):
        part_refs, (total, squares) = refs[:4], refs[4:]
        added = jnp.zeros((8, width), wide_type)
        for block in range(count):
            for core in range(2):
                value = part_refs[0][block, core].astype(wide_type)
                for part_ref in part_refs[1:]:
                    value = value + part_ref[block, core].astype(wide_type)
                low = value.astype(low_type)
                total[block, core] = low
                value = low.astype(wide_type)
                added = added + jnp.sum((value * value).reshape(rows // 8, 8, width), axis=0)
        squares[...] = added

    outs = [(parts[0].shape, low_type), ((8, width), wide_type)]
    specs = [full(shape) for shape, _ in outs]
    return run(kernel, "add_last", where, parts, fulls(parts), outs, specs, after=after)


def pack_replicas(row, far, where, after=()):
    def kernel(where, row, far, out, token, sem):
        copies = [
            pltpu.make_async_copy(row, out.at[pl.ds(0, 2)], sem.at[0]),
            pltpu.make_async_copy(far, out.at[pl.ds(2, 2)], sem.at[1]),
        ]
        for copy in copies:
            copy.start()
        for copy in copies:
            copy.wait()

    shape = (4,) + row.shape[1:]
    return run(
        kernel,
        "pack_replicas",
        where,
        (row, far),
        [pl.BlockSpec(memory_space=pl.ANY)] * 2,
        [(shape, low_type), ((8, 128), low_type)],
        [full(shape), full((8, 128))],
        scratch=[pltpu.SemaphoreType.DMA((2,))],
        after=after,
    )


def adam_step(weight, first_moment, second_moment, gradient, factor, step_rate, decay_rate):
    gradient = gradient * factor
    first_moment = beta_first * first_moment + (1.0 - beta_first) * gradient
    second_moment = beta_second * second_moment + (1.0 - beta_second) * gradient * gradient
    first_hat = first_moment * (1.0 / (1.0 - beta_first**STEP))
    second_hat = second_moment * (1.0 / (1.0 - beta_second**STEP))
    weight = weight - step_rate * (
        first_hat / (jnp.sqrt(second_hat) + adam_eps) + decay_rate * weight
    )
    return (weight, first_moment, second_moment)


def adam_scaled(weight, first_moment, second_moment, gradient, factor):
    first_moment = beta_first * first_moment + ((1.0 - beta_first) * factor) * gradient
    square = gradient * gradient
    second_moment = beta_second * second_moment + ((1.0 - beta_second) * factor * factor) * square
    second_hat = second_moment * (1.0 / (1.0 - beta_second**STEP))
    root = second_hat * lax.rsqrt(second_hat) + adam_eps
    step = (rate_matrix / (1.0 - beta_first**STEP)) * first_moment
    weight = (1.0 - rate_matrix * decay_matrix) * weight - step / root
    return (weight, first_moment, second_moment)


def adam_all(states, pieces, factor, where):
    layer_count = len(pieces)
    rows = states[0][0].shape[1]
    sizes = [state[0].shape[1] * state[0].shape[2] // (rows * D) for state in states]
    spans = []
    begin = 0
    for kind, size in enumerate(sizes):
        spans.append((kind, begin, size))
        begin += size

    def quarter_of(kind, block):
        return ((block, 0), (3, 0), (block % 4, block // 4), (block, 0))[kind]

    def kernel(where, factor_ref, *refs):
        step = pl.program_id(0)
        in_refs, piece_refs = refs[: 3 * len(states)], refs[3 * len(states) : -3 * len(states)]
        out_refs = refs[-3 * len(states) :]
        for kind, start, size in spans:

            @pl.when((step >= start) & (step < start + size))
            def _():
                w, m, v = in_refs[3 * kind : 3 * kind + 3]
                outs = out_refs[3 * kind : 3 * kind + 3]
                for layer in range(layer_count):
                    first = 2 * (kind * layer_count + layer)
                    mine, theirs = (ref[0, 0, 0] for ref in piece_refs[first : first + 2])
                    mine, theirs = mine.astype(wide_type), theirs.astype(wide_type)
                    for half in range(2):
                        columns = slice(half * HALF, (half + 1) * HALF)
                        results = adam_scaled(
                            w[layer, :, columns],
                            m[layer, :, columns],
                            v[layer, :, columns],
                            jnp.where(where[1] == half, mine, theirs),
                            factor_ref[0],
                        )
                        for out, result in zip(outs, results):
                            out[layer, :, columns] = result

    def state_spec(kind):
        _, first, size = spans[kind]

        def at(step, where):
            block = jnp.clip(step - first, 0, size - 1)
            return (0, block, 0) if kind == 3 else (0, 0, block)

        return pl.BlockSpec((layer_count, rows, D), at)

    def piece_spec(kind, start, size, place_at, side):
        def at(step, where):
            block = jnp.clip(step - start, 0, size - 1)
            quarter, index = quarter_of(kind, block)
            high, low = quarter // 2, quarter % 2
            first, second = where[2], where[3]
            if side == 1:
                first, second = second, first
            return (2 * (first ^ high) + (second ^ low), place_at + index, where[1], 0, 0)

        return pl.BlockSpec((1, 1, 1, rows, HALF), at)

    state_specs = [state_spec(kind) for kind in range(len(states)) for _ in range(3)]
    piece_list, piece_specs = [], []
    for kind, start, size in spans:
        for layer in range(layer_count):
            found, place_at = pieces[layer][kind]
            for side in range(2):
                piece_list.append(found[side])
                piece_specs.append(piece_spec(kind, start, size, place_at, side))
    return run(
        kernel,
        "adam_all",
        where,
        (factor.reshape(1), *(array for state in states for array in state), *piece_list),
        [pl.BlockSpec(memory_space=pltpu.SMEM)] + state_specs + piece_specs,
        [(array.shape, wide_type) for state in states for array in state],
        state_specs,
        grid=(begin,),
    )


def sum_all(value):
    value = value + send(value, FLIP_CORE)
    for one, two, three in ((FLIP_X, FLIP_Y, FLIP_XY), (Z_ONE, Z_TWO, Z_THREE)):
        value = (value + send(value, one)) + (send(value, two) + send(value, three))
    return value


def keep_attend(results):
    names = ("trio", "qkv", "logs", "residual_one", "normed")
    return dict(zip(names, results))


def forward(hidden, weight_list, norms, where):
    kept_list = []
    for layer, weights in enumerate(weight_list):
        kept = keep_attend(attend_forward(hidden, *weights[:2], norms, layer, where))
        kept["product"], kept["slopes"] = gate_forward(kept["trio"], weights[2], where)
        kept["residual_two"], hidden = down_forward(
            kept["product"], weights[3], kept["normed"], norms, layer, where
        )
        kept_list.append(kept)
    return (hidden, kept_list)


def forward_neighbours(hidden, states, norm_params, chain):
    layer_count = states[0].shape[0]
    norm_params = norm_params.reshape(8, -1)
    width = norm_params.shape[1]
    padded = jnp.pad(norm_params, ((0, NORM_ROWS - 8), (0, SEQ_LEN - width)))
    rows = states[0].shape[1]
    kept_list = [None] * layer_count
    weight_list = [()] * layer_count
    groups = [(("attend", 0),)]
    for layer in range(layer_count):
        groups.append((("gate_up", layer),))
        if layer < layer_count - 1:
            groups.append((("down", layer), ("attend", layer + 1)))
    groups.append((("down", layer_count - 1),))
    owns, started, near, across, six, far, other, weights = ({} for _ in range(8))
    norms = []

    def start(at):
        more = padded if at == 0 else None
        *owns[at], quarters = chain(own_chunks, groups[at], states, more)
        started[at] = [send(quarters, move) for move in (Z_ONE, Z_TWO, Z_THREE)]

    def spread(at):
        near[at], rest = chain(stack_chips, started[at], rows)
        across[at] = send(near[at], FLIP_SECOND)
        if at == 0:
            whole = jnp.concatenate([padded.astype(low_type)[None], rest])
            other_rest = send(whole, FLIP_CORE)
            norms.extend((rest, other_rest))

    def spread_on(at):
        six[at], _ = chain(stack_two, near[at], across[at])
        far[at] = send(six[at], FLIP_FIRST)

    def swap(at):
        whole, _ = chain(pack, owns[at], six[at], far[at])
        other[at] = send(whole, FLIP_CORE)

    def lay_out(at):
        begin = 0
        for (kind, layer), own in zip(groups[at], owns[at]):
            weights[kind, layer] = chain(assemble, (own, six[at], far[at], other[at]), kind, begin)
            weight_list[layer] += tuple(weights[kind, layer])
            begin += BLOCKS[kind]

    def compute(at, hidden):
        for kind, layer in groups[at]:
            args = weights[kind, layer]
            if kind == "attend":
                results = chain(attend_forward, hidden, *args, norms[0], layer)
                kept_list[layer] = keep_attend(results)
                continue
            kept = kept_list[layer]
            if kind == "gate_up":
                kept["product"], kept["slopes"] = chain(gate_forward, kept["trio"], *args)
            else:
                kept["residual_two"], hidden = chain(
                    down_forward, kept["product"], *args, kept["normed"], norms[0], layer
                )
        return hidden

    last = len(groups) - 1
    start(0)
    spread(0)
    start(1)
    norms[:] = chain(norm_columns, *norms, padded, width)
    spread_on(0)
    for at in range(len(groups)):
        if at < last:
            spread(at + 1)
        if at + 2 <= last:
            start(at + 2)
        swap(at)
        if at < last:
            spread_on(at + 1)
        lay_out(at)
        hidden = compute(at, hidden)
    return (hidden, weight_list, kept_list, norms[0])


def gather_weights(states):
    return [
        tuple(
            lax.all_gather(weight[layer].astype(low_type), "fsdp", axis=0, tiled=True)
            for weight in states
        )
        for layer in range(states[0].shape[0])
    ]


def backward(grad, weights, kept, norms, layer, where):
    gates, _, branch, grad_one, attend, grad_mixed, grad_norms = feed_backward(
        grad, kept["residual_two"], kept["residual_one"], kept["slopes"], weights, norms, layer, where
    )
    grad_qkv, _, grad = attend_backward(
        grad_mixed, kept["qkv"], kept["logs"], grad_one, weights[0], where
    )
    gate_up = jnp.concatenate([gates[0], gates[1]], axis=1)
    factors = (
        (kept["trio"][0], grad_qkv),
        (kept["trio"][1], attend),
        (kept["trio"][2], gate_up),
        (kept["product"], branch),
    )
    return (grad, factors, grad_norms)


def backward_neighbours(grad, weight_list, kept_list, norms, chain):
    layer_count = len(weight_list)
    norm_list = [None] * layer_count
    pieces = [[None] * 4 for _ in range(layer_count)]
    squares = []
    swapped = []
    sums = [{} for _ in range(layer_count)]

    def feed(layer, grad):
        kept = kept_list[layer]
        gates, theirs, branch, grad_one, attend, grad_mixed, norm_list[layer] = chain(
            feed_backward,
            grad,
            kept["residual_two"],
            kept["residual_one"],
            kept["slopes"],
            weight_list[layer],
            norms,
            layer,
        )
        return dict(
            gates=gates,
            feed_other=send(theirs, FLIP_CORE),
            branch=branch,
            grad_one=grad_one,
            attend=attend,
            grad_mixed=grad_mixed,
        )

    def attention(layer, made):
        kept = kept_list[layer]
        made["qkv"], theirs, grad = chain(
            attend_backward,
            made["grad_mixed"],
            kept["qkv"],
            kept["logs"],
            made["grad_one"],
            weight_list[layer][0],
        )
        made["qkv_other"] = send(theirs, FLIP_CORE)
        return grad

    def product_wide(layer, made):
        kept = kept_list[layer]
        sent, held = chain(
            grad_gate_up, kept["trio"], kept["trio_other"], made["gates"], made["feed_other"]
        )
        sums[layer]["wide"] = (held, send(sent, FLIP_FIRST))

    def product_down(layer, made):
        kept = kept_list[layer]
        left, left_other = kept["product"], kept["product_other"]
        made["down"] = chain(grad_down, left, left_other, made["branch"], made["feed_other"])

    def product_rest(layer, made):
        kept = kept_list[layer]
        other = made["feed_other"]
        filled = made["down"]
        qkv, qkv_other = made["qkv"], made["qkv_other"]
        trio, trio_other = kept["trio"], kept["trio_other"]
        sent, held = chain(
            grad_attend, trio, trio_other, qkv, qkv_other, made["attend"], other, filled
        )
        sums[layer]["rest"] = (held, send(sent, FLIP_FIRST))

    def halves(layer, name):
        away, left = chain(add_halves, *sums[layer][name])
        sums[layer][name] = (left, send(away, FLIP_SECOND))

    def chips(layer, name):
        own, *parts = chain(add_chips, [sums[layer][name]])
        moves = (Z_ONE, Z_TWO, Z_THREE)
        return [own] + [send(part, move) for part, move in zip(parts, moves)]

    def total(parts):
        whole, part = chain(add_last, parts)
        squares.append(part)
        return whole

    def share(whole):
        ready, _ = chain(relay, whole)
        return (whole, send(ready, FLIP_SECOND))

    def share_on(found):
        row, _ = chain(stack_two, *found)
        return (row, send(row, FLIP_FIRST))

    def swap(layer, name, found):
        mine, _ = chain(pack_replicas, *found)
        found = (mine, send(mine, FLIP_CORE))
        swapped.append(found[1])
        for kind, at in ((2, 0),) if name == "wide" else ((3, 0), (0, 1), (1, 1)):
            pieces[layer][kind] = (found, at)

    for kept in kept_list:
        for name in ("trio", "product"):
            kept[name + "_other"] = send(kept[name], FLIP_CORE)
    made = feed(layer_count - 1, grad)
    for kept in kept_list:
        chain.wait(kept["trio_other"], kept["product_other"])
    def settle():
        chain.wait(*swapped)
        swapped.clear()

    layer = layer_count - 1
    grad = attention(layer, made)
    product_wide(layer, made)
    product_down(layer, made)
    product_rest(layer, made)
    while layer > 0:
        made = feed(layer - 1, grad)
        halves(layer, "wide")
        product_wide(layer - 1, made)
        grad = attention(layer - 1, made)
        product_down(layer - 1, made)
        chain.wait(made["qkv_other"])
        parts = chips(layer, "wide")
        halves(layer, "rest")
        wide = total(parts)
        product_rest(layer - 1, made)
        parts = chips(layer, "rest")
        halves(layer - 1, "wide")
        rest = total(parts)
        layer -= 1
        parts = chips(layer, "wide")
        halves(layer, "rest")
        shared = share(wide)
        shared_rest = share(rest)
        shared = share_on(shared)
        wide = total(parts)
        parts = chips(layer, "rest")
        shared_rest = share_on(shared_rest)
        shared_wide = share(wide)
        swap(layer + 1, "wide", shared)
        swap(layer + 1, "rest", shared_rest)
        shared_wide = share_on(shared_wide)
        rest = total(parts)
        shared_rest = share(rest)
        settle()
        swap(layer, "wide", shared_wide)
        shared_rest = share_on(shared_rest)
        swap(layer, "rest", shared_rest)
    return (grad, norm_list, pieces, sum(squares))


def body(
    tokens_in,
    masked_flags,
    mask_embedding,
    out_cotangent,
    w_qkv,
    m_qkv,
    v_qkv,
    w_out,
    m_out,
    v_out,
    w_gu,
    m_gu,
    v_gu,
    w_down,
    m_down,
    v_down,
    norm_params,
    m_norms,
    v_norms,
):
    layer_count = w_qkv.shape[0]
    masked = masked_flags[:, None] == 1
    where = jnp.stack(place()).astype(jnp.int32)
    hidden = jnp.where(masked, mask_embedding.astype(wide_type)[None, :], tokens_in.astype(wide_type))
    grad = out_cotangent.astype(wide_type) * masked_flags[:, None].astype(wide_type)
    chain = Chain(where)
    matrices = (w_qkv, w_out, w_gu, w_down)
    if by_neighbours():
        hidden, weight_list, kept, norms = forward_neighbours(hidden, matrices, norm_params, chain)
    else:
        norms = lax.all_gather(norm_params.astype(low_type), "fsdp", axis=2, tiled=True)
        norms = norms.astype(wide_type).reshape(-1, D)
        weight_list = gather_weights(matrices)
        hidden, kept = forward(hidden, weight_list, norms, where)
    activations = hidden.astype(low_type)
    states = (
        (w_qkv, m_qkv, v_qkv),
        (w_out, m_out, v_out),
        (w_gu, m_gu, v_gu),
        (w_down, m_down, v_down),
    )
    if by_neighbours():
        grad, norm_list, pieces, squares = backward_neighbours(
            grad, weight_list, kept, norms, chain
        )
        norm_grads = jnp.concatenate(norm_list)
        rows = norm_grads.shape[0]
        packed = jnp.concatenate([norm_grads, jnp.pad(squares, ((0, 0), (0, D - HALF)))])
        packed = sum_all(packed)
        norm_grads = packed[:rows]
        total = jnp.sum(packed[rows:])
    else:
        norm_list = [None] * layer_count
        sums = [None] * layer_count
        total = wide_type(0.0)
        for layer in reversed(range(layer_count)):
            grad, factors, norm_list[layer] = backward(
                grad, weight_list[layer], kept[layer], norms, layer, where
            )
            sums[layer] = []
            for left, right in factors:
                part = dot_left(left, right)
                part = lax.psum_scatter(part, "fsdp", scatter_dimension=0, tiled=True)
                part = lax.psum(part, "rep")
                total = total + jnp.sum(part * part)
                sums[layer].append(part)
        total = lax.psum(total, "fsdp")
        norm_grads = lax.psum(jnp.concatenate(norm_list), both_axes)
    grad_norm = jnp.sqrt(total + jnp.sum(norm_grads * norm_grads))
    factor = clip_norm / jnp.maximum(grad_norm, clip_norm)
    if by_neighbours():
        updated = list(adam_all(states, pieces, factor, where))
    else:
        updated = []
        for kind, state in enumerate(states):
            gradient = jnp.stack([layer[kind] for layer in sums])
            updated += adam_step(*state, gradient, factor, rate_matrix, decay_matrix)
    width = norm_params.shape[2]
    norm_grads = norm_grads.reshape(layer_count, -1, D)
    norm_grads = lax.dynamic_slice_in_dim(norm_grads, lax.axis_index("fsdp") * width, width, 2)
    updated += adam_step(norm_params, m_norms, v_norms, norm_grads, factor, rate_norm, 0.0)
    input_grad = jnp.where(masked, 0.0, grad)
    return (activations, input_grad, grad_norm, *updated)


def solution(mesh):
    return jax.shard_map(
        body,
        mesh=mesh,
        in_specs=(
            P(("rep", "fsdp"), None),
            P(("rep", "fsdp")),
            P(),
            P(("rep", "fsdp"), None),
            P(None, "fsdp", None),
            P(None, "fsdp", None),
            P(None, "fsdp", None),
            P(None, "fsdp", None),
            P(None, "fsdp", None),
            P(None, "fsdp", None),
            P(None, "fsdp", None),
            P(None, "fsdp", None),
            P(None, "fsdp", None),
            P(None, "fsdp", None),
            P(None, "fsdp", None),
            P(None, "fsdp", None),
            P(None, None, "fsdp"),
            P(None, None, "fsdp"),
            P(None, None, "fsdp"),
        ),
        out_specs=(
            P(("rep", "fsdp"), None),
            P(("rep", "fsdp"), None),
            P(),
            P(None, "fsdp", None),
            P(None, "fsdp", None),
            P(None, "fsdp", None),
            P(None, "fsdp", None),
            P(None, "fsdp", None),
            P(None, "fsdp", None),
            P(None, "fsdp", None),
            P(None, "fsdp", None),
            P(None, "fsdp", None),
            P(None, "fsdp", None),
            P(None, "fsdp", None),
            P(None, "fsdp", None),
            P(None, None, "fsdp"),
            P(None, None, "fsdp"),
            P(None, None, "fsdp"),
        ),
        check_vma=False,
    )
```
